32 devices in a mesh: rep: 4 (over z), fsdp: 4 (over x, core), sp: 2 (over y).
Axes of the slice: x: 2, y: 2, z: 4, core: 2. Of those that a mesh axis runs over, the one named last changes fastest.
Arguments:
- latent_in: bfloat16 [16, 1024, 1152], P(('rep', 'fsdp'), 'sp'), may hold values from -6 to 6
- condition: bfloat16 [16, 1152], P(('rep', 'fsdp')), may hold values from -6 to 6
- valid_slots: int32 [16], P(('rep', 'fsdp')), may hold values 0 or 1
- ada_weight: bfloat16 [1152, 6912], P(('fsdp', 'sp')), may hold values from -0.1875 to 0.1875
- ada_bias: bfloat16 [6912], P(('fsdp', 'sp')), may hold values from -3 to 3
- qkv_weight: bfloat16 [1152, 3456], P(('fsdp', 'sp')), may hold values from -0.1875 to 0.1875
- qv_bias: bfloat16 [2304], P(('fsdp', 'sp')), may hold values from -3 to 3
- out_weight: bfloat16 [1152, 1152], P(('fsdp', 'sp')), may hold values from -2 to 2
- out_bias: bfloat16 [1152], P(('fsdp', 'sp')), may hold values from -3 to 3
- up_weight: bfloat16 [1152, 4608], P(('fsdp', 'sp')), may hold values from -0.1875 to 0.1875
- up_bias: bfloat16 [4608], P(('fsdp', 'sp')), may hold values from -3 to 3
- down_weight: bfloat16 [4608, 1152], P(('fsdp', 'sp')), may hold values from -0.09375 to 0.09375
- down_bias: bfloat16 [1152], P(('fsdp', 'sp')), may hold values from -3 to 3
- cotangent: bfloat16 [16, 1024, 1152], P(('rep', 'fsdp'), 'sp'), may hold values from -6 to 6
Outputs:
- block_out: bfloat16 [16, 1024, 1152], P(('rep', 'fsdp'), 'sp')
- latent_grad: float32 [16, 1024, 1152], P(('rep', 'fsdp'), 'sp')
- cond_grad: float32 [16, 1152], P(('rep', 'fsdp'))
- ada_wgrad: float32 [1152, 6912], P(('fsdp', 'sp'))
- ada_bgrad: float32 [6912], P(('fsdp', 'sp'))
- qkv_wgrad: float32 [1152, 3456], P(('fsdp', 'sp'))
- qv_bgrad: float32 [2304], P(('fsdp', 'sp'))
- out_wgrad: float32 [1152, 1152], P(('fsdp', 'sp'))
- out_bgrad: float32 [1152], P(('fsdp', 'sp'))
- up_wgrad: float32 [1152, 4608], P(('fsdp', 'sp'))
- up_bgrad: float32 [4608], P(('fsdp', 'sp'))
- down_wgrad: float32 [4608, 1152], P(('fsdp', 'sp'))
- down_bgrad: float32 [1152], P(('fsdp', 'sp'))
The draws below stay inside these ranges and needn't reach their ends.
All inputs are finite; a program needn't handle non-finite values. No bound on the sum of `valid_slots` on one device may be relied on, other than what follows from the above.
Results may differ from the reference program's by a relative error of at most 0.013.
The reference program's roundings to bfloat16 on the way count: a program that leaves them out, or rounds other values in their place, can miss the bound.
Values may be sent and summed in bfloat16 or wider, within the bound.
No kernel may reach another device: no remote copies, remote signals or barrier semaphores. Data moves between devices by JAX's collectives and lax.ppermute only.
A program may use at most 256 MiB of HBM per device.

```python
import jax
import jax.numpy as jnp
from jax import lax

D = 1152
HEADS = 16
HEAD = 72
FF = 4608
SEQ = 1024
LATENTS = 16


def set_ends(drawn, stream_key, least, top_value):
    place = [jax.random.randint(jax.random.fold_in(stream_key, axis), (), 0, length) for axis, length in enumerate(drawn.shape)]
    main_axis = drawn.shape.index(max(drawn.shape))
    neighbour = place[:main_axis] + [(place[main_axis] + 1) % drawn.shape[main_axis]] + place[main_axis + 1:]
    return drawn.at[tuple(place)].set(least).at[tuple(neighbour)].set(top_value)


def steps_of(rng, extent, shards, low, high):
    def one(axis_at, parts):
        draws = jax.random.uniform(jax.random.fold_in(jax.random.fold_in(rng, 6), axis_at), (parts,), jnp.float32, low / len(shards), high / len(shards))
        return jnp.repeat(jnp.exp(draws), extent[axis_at] // parts).reshape((-1,) + (1,) * (len(extent) - axis_at - 1))

    loudness = one(*shards[0])
    for cut in shards[1:]:
        loudness = loudness * one(*cut)
    return loudness


def normal_values(own_key, dims, deviation, reach, cuts=(), dtype=jnp.bfloat16):
    loudness = steps_of(own_key, dims, cuts, -0.22, 0.18) if cuts else 1.0
    entries = jax.random.normal(own_key, dims, jnp.float32) * deviation * loudness
    return jnp.minimum(jnp.maximum(entries, -reach), reach).astype(dtype)


def setup_inputs(seed: int = 0) -> dict:
    seeds = jax.random.split(jax.random.key(seed), 15)
    return {
        "latent_in": normal_values(seeds[0], (LATENTS, SEQ, D), 1.0, 6.0, ((0, 16), (1, 2))),
        "condition": normal_values(seeds[1], (LATENTS, D), 1.0, 6.0, ((0, 16),)),
        "valid_slots": set_ends((jax.random.randint(seeds[2], (LATENTS,), 0, 32) < 29).astype(jnp.int32), jax.random.fold_in(seeds[2], 1), 0, 1),
        "ada_weight": normal_values(seeds[3], (D, 6 * D), D ** -0.5, 0.1875, ((0, 8),)),
        "ada_bias": normal_values(seeds[4], (6 * D,), 0.5, 3.0, ((0, 8),)),
        "qkv_weight": normal_values(seeds[5], (D, 3 * D), D ** -0.5, 0.1875, ((0, 8),)),
        "qv_bias": normal_values(seeds[6], (2 * D,), 0.5, 3.0, ((0, 8),)),
        "out_weight": normal_values(seeds[7], (D, D), (max(D // 128, 4)) ** -0.5, 2.0, ((0, 8),)),
        "out_bias": normal_values(seeds[8], (D,), 0.5, 3.0, ((0, 8),)),
        "up_weight": normal_values(seeds[9], (D, FF), D ** -0.5, 0.1875, ((0, 8),)),
        "up_bias": normal_values(seeds[10], (FF,), 0.5, 3.0, ((0, 8),)),
        "down_weight": normal_values(seeds[11], (FF, D), FF ** -0.5, 0.09375, ((0, 8),)),
        "down_bias": normal_values(seeds[12], (D,), 0.5, 3.0, ((0, 8),)),
        "cotangent": normal_values(seeds[13], (LATENTS, SEQ, D), 1.0, 6.0, ((0, 16), (1, 2))),
    }


exact_mode = lax.Precision.HIGHEST
epsilon = 1e-06

@jax.custom_vjp
def low(v):
    return lax.optimization_barrier(v.astype(jnp.bfloat16)).astype(jnp.float32)

@jax.custom_vjp
def low_back(v):
    return v

def low_keep(v):
    return (low(v), None)

def low_pass(kept, grad):
    return (grad,)

def back_keep(v):
    return (v, None)

def back_low(kept, grad):
    return (low(grad),)
low.defvjp(low_keep, low_pass)
low_back.defvjp(back_keep, back_low)

def normalize(values):
    average = lax.optimization_barrier(jnp.mean(values, -1, keepdims=True))
    centered = values - average
    variance = lax.optimization_barrier(jnp.mean(centered * centered, -1, keepdims=True))
    return centered * lax.rsqrt(variance + epsilon)

def product(left, right):
    return jnp.dot(left, right, precision=exact_mode)

def attend(triple):
    query, keys, values = triple
    query = query.reshape(SEQ, HEADS, HEAD)
    keys = keys.reshape(SEQ, HEADS, HEAD)
    values = values.reshape(SEQ, HEADS, HEAD)
    scores = jnp.einsum('qhd,khd->hqk', query, keys, precision=exact_mode) * HEAD ** (-0.5)
    scores = low_back(scores)
    weights = low(jax.nn.softmax(scores, axis=-1))
    mixed = jnp.einsum('hqk,khd->qhd', weights, values, precision=exact_mode)
    return mixed.reshape(SEQ, D)

def block(latent, cond_rows, slot_mask, ada_weight, ada_bias, qkv_weight, qv_bias, out_weight, out_bias, up_weight, up_bias, down_weight, down_bias):
    number = latent.shape[0]
    tokens = number * SEQ
    silu_cond = low(jax.nn.silu(cond_rows))
    modulation = product(silu_cond, ada_weight) + ada_bias
    shift_one, scale_one, gate_one, shift_two, scale_two, gate_two = jnp.split(modulation[:, None, :], 6, axis=-1)
    hidden_one = low(normalize(latent) * (1.0 + scale_one) + shift_one)
    bias_full = jnp.concatenate([qv_bias[:D], jnp.zeros((D,), jnp.float32), qv_bias[D:]])
    projected = low(low_back(product(hidden_one.reshape(tokens, D), qkv_weight) + bias_full))
    projected = projected.reshape(number, SEQ, 3 * D)
    attended = lax.map(jax.checkpoint(attend), (projected[..., :D], projected[..., D:2 * D], projected[..., 2 * D:]))
    attended = low(low_back(attended))
    branch_one = low_back(product(attended.reshape(tokens, D), out_weight) + out_bias).reshape(number, SEQ, D)
    middle = latent + gate_one * branch_one
    hidden_two = low(normalize(middle) * (1.0 + scale_two) + shift_two)
    preact = low_back(product(hidden_two.reshape(tokens, D), up_weight) + up_bias)
    activated = low(jax.nn.gelu(preact, approximate=True))
    branch_two = low_back(product(activated, down_weight) + down_bias).reshape(number, SEQ, D)
    return slot_mask[:, None, None] * (middle + gate_two * branch_two)

def reference(latent_in, condition, valid_slots, ada_weight, ada_bias, qkv_weight, qv_bias, out_weight, out_bias, up_weight, up_bias, down_weight, down_bias, cotangent):
    params = tuple((weight.astype(jnp.float32) for weight in (ada_weight, ada_bias, qkv_weight, qv_bias, out_weight, out_bias, up_weight, up_bias, down_weight, down_bias)))
    blocks = LATENTS // 4
    latents = latent_in.astype(jnp.float32).reshape(blocks, 4, SEQ, D)
    conds = condition.astype(jnp.float32).reshape(blocks, 4, D)
    masks = valid_slots.astype(jnp.float32).reshape(blocks, 4)
    upstreams = cotangent.astype(jnp.float32).reshape(blocks, 4, SEQ, D)

    def advance(totals, scan_item):
        latent, cond_rows, slot_mask, upstream = scan_item

        def forward(latent_arg, cond_arg, *weights):
            return block(latent_arg, cond_arg, slot_mask, *weights)
        result, pullback = jax.vjp(forward, latent, cond_rows, *params)
        gradients = pullback(upstream)
        totals = tuple((first + second for first, second in zip(totals, gradients[2:])))
        return (totals, (result.astype(jnp.bfloat16), gradients[0], gradients[1]))
    initial = tuple((jnp.zeros_like(weight) for weight in params))
    totals, stacked = lax.scan(advance, initial, (latents, conds, masks, upstreams))
    outputs, latent_grads, cond_grads = stacked
    return (outputs.reshape(LATENTS, SEQ, D), latent_grads.reshape(LATENTS, SEQ, D), cond_grads.reshape(LATENTS, D), totals[0], totals[1], totals[2], totals[3], totals[4], totals[5], totals[6], totals[7], totals[8], totals[9])
```

```python
import jax
import jax.numpy as jnp
from jax import lax
from jax.sharding import PartitionSpec as P

HEAD = 72
GROUP = ("fsdp", "sp")
SHARDS = 8

exact_mode = lax.Precision.HIGHEST
epsilon = 1e-06


def normalize(values):
    average = jnp.mean(values, -1, keepdims=True)
    centered = values - average
    inverse = lax.rsqrt(jnp.mean(centered * centered, -1, keepdims=True) + epsilon)
    return (centered * inverse, inverse)


def norm_back(upstream, normed, inverse):
    return (
        upstream
        - jnp.mean(upstream, -1, keepdims=True)
        - normed * jnp.mean(upstream * normed, -1, keepdims=True)
    ) * inverse


def matmul(left, right):
    return jnp.dot(left, right, preferred_element_type=jnp.float32)


def matmul_left(left, right):
    return lax.dot_general(
        left, right, (((0,), (0,)), ((), ())), preferred_element_type=jnp.float32
    )


def matmul_right(left, right):
    return lax.dot_general(
        left, right, (((1,), (1,)), ((), ())), preferred_element_type=jnp.float32
    )


def place_of():
    return lax.axis_index("fsdp") * 2 + lax.axis_index("sp")


def pairs_by(rule):
    return [(place, rule(place)) for place in range(SHARDS)]


def swap_rule(place):
    return (place & 4) | ((place & 1) << 1) | ((place >> 1) & 1)


def core_rule(place):
    return place ^ 2


def first_rule(place):
    return place ^ (1 if place & 2 else 4)


def second_rule(place):
    return place ^ (4 if place & 2 else 1)


def permute(values, rule):
    return lax.ppermute(values, GROUP, pairs_by(rule))


def reduce_scatter(partial):
    low = partial.dtype
    place = place_of()
    core = (place >> 1) & 1
    _, rows, columns = partial.shape
    spread = partial.reshape(2, 2, 2, rows, columns)

    def core_half(which):
        return lax.dynamic_index_in_dim(spread, which, 1, keepdims=False)

    received = permute(core_half(1 - core), core_rule)
    kept = (core_half(core).astype(jnp.float32) + received.astype(jnp.float32)).astype(low)
    kept = kept.reshape(4, rows, columns)
    mine = ((place >> 2) << 1) | (place & 1)
    near = jnp.where(core == 0, 2, 1)
    far = 3 - near

    def block(which):
        return lax.dynamic_slice_in_dim(kept, which, 1, 0)

    received = permute(jnp.concatenate([block(mine ^ near), block(mine ^ 3)]), first_rule)
    halved = jnp.concatenate([block(mine), block(mine ^ far)]).astype(jnp.float32)
    halved = halved + received.astype(jnp.float32)
    received = permute(halved[1].astype(low), second_rule)
    return halved[0] + received.astype(jnp.float32)


def head_slice(values, group_index, group_width):
    number, length, model_width = values.shape
    piece = lax.dynamic_slice_in_dim(values, group_index * group_width, group_width, 2)
    return piece.reshape(number, length, 4, HEAD)


def join_groups(stacked):
    groups, number, length, group_width = stacked.shape
    return jnp.moveaxis(stacked, 0, 2).reshape(number, length, groups * group_width)


def attn_forward(query, keys, values, score_scale):
    group_width = 4 * HEAD
    groups = query.shape[2] // group_width

    def per_group(group_index):
        query_part = head_slice(query, group_index, group_width)
        keys_part = head_slice(keys, group_index, group_width)
        values_part = head_slice(values, group_index, group_width)
        scores = (
            jnp.einsum("lqhd,lkhd->lhqk", query_part, keys_part, preferred_element_type=jnp.float32)
            * score_scale
        )
        row_max = jnp.max(scores, -1, keepdims=True)
        weights = jnp.exp(scores - row_max)
        row_total = jnp.sum(weights, -1, keepdims=True)
        probs = (weights / row_total).astype(jnp.bfloat16)
        mixed = jnp.einsum(
            "lhqk,lkhd->lqhd", probs, values_part, preferred_element_type=jnp.float32
        )
        log_total = row_max[..., 0] + jnp.log(row_total[..., 0])
        return (mixed.reshape(mixed.shape[0], mixed.shape[1], group_width), log_total)

    mixed_all, log_totals = lax.map(per_group, jnp.arange(groups))
    return (join_groups(mixed_all), log_totals)


def attn_backward(query, keys, values, upstream, log_totals, score_scale):
    group_width = 4 * HEAD
    groups = query.shape[2] // group_width

    def per_group(group_item):
        group_index, log_total = group_item
        query_part = head_slice(query, group_index, group_width)
        keys_part = head_slice(keys, group_index, group_width)
        values_part = head_slice(values, group_index, group_width)
        upstream_part = head_slice(upstream, group_index, group_width)
        scores = (
            jnp.einsum("lqhd,lkhd->lhqk", query_part, keys_part, preferred_element_type=jnp.float32)
            * score_scale
        )
        probs = jnp.exp(scores - log_total[..., None])
        d_probs = jnp.einsum(
            "lqhd,lkhd->lhqk", upstream_part, values_part, preferred_element_type=jnp.float32
        )
        d_scores = (probs * (d_probs - jnp.sum(probs * d_probs, -1, keepdims=True))).astype(
            jnp.bfloat16
        )
        d_query = (
            jnp.einsum("lhqk,lkhd->lqhd", d_scores, keys_part, preferred_element_type=jnp.float32)
            * score_scale
        )
        d_keys = (
            jnp.einsum("lhqk,lqhd->lkhd", d_scores, query_part, preferred_element_type=jnp.float32)
            * score_scale
        )
        d_values = jnp.einsum(
            "lhqk,lqhd->lkhd",
            probs.astype(jnp.bfloat16),
            upstream_part,
            preferred_element_type=jnp.float32,
        )
        number = d_query.shape[0]
        return (
            d_query.reshape(number, d_query.shape[1], group_width),
            d_keys.reshape(number, d_keys.shape[1], group_width),
            d_values.reshape(number, d_values.shape[1], group_width),
        )

    d_query, d_keys, d_values = lax.map(per_group, (jnp.arange(groups), log_totals))
    return (join_groups(d_query), join_groups(d_keys), join_groups(d_values))


def per_device(
    latent_in,
    condition,
    valid_slots,
    ada_weight,
    ada_bias,
    qkv_weight,
    qv_bias,
    out_weight,
    out_bias,
    up_weight,
    up_bias,
    down_weight,
    down_bias,
    cotangent,
):
    number, length, width = latent_in.shape
    hidden_width = up_weight.shape[1]
    score_scale = float(HEAD) ** (-0.5)
    place = place_of()
    fsdp_index = lax.axis_index("fsdp")
    held = (place >> 2) * 2 + (place & 1)
    rows = width // SHARDS

    small = jnp.concatenate(
        [
            condition[0],
            qv_bias,
            out_bias,
            up_bias,
            down_bias,
            jnp.broadcast_to(valid_slots.astype(jnp.bfloat16), (128,)),
        ]
    )
    small_all = lax.all_gather(small, GROUP, axis=0)
    full_qkv = lax.all_gather(qkv_weight, GROUP, axis=0, tiled=True)
    latent_low = permute(latent_in, swap_rule)
    cotangent_low = permute(cotangent, swap_rule)
    full_out = lax.all_gather(out_weight, GROUP, axis=0, tiled=True)
    full_up = lax.all_gather(up_weight, GROUP, axis=0, tiled=True)
    full_down = lax.all_gather(down_weight, GROUP, axis=0, tiled=True)

    bounds = [0, width]
    for bias in (qv_bias, out_bias, up_bias, down_bias):
        bounds.append(bounds[-1] + bias.shape[0])
    cond_group = small_all[::2, :width].astype(jnp.float32)
    full_qv_bias, full_out_bias, full_up_bias, full_down_bias = (
        small_all[:, low:high].reshape(-1).astype(jnp.float32)
        for low, high in zip(bounds[1:-1], bounds[2:])
    )
    valid_group = small_all[::2, bounds[-1]].astype(jnp.float32)
    slot_mask = lax.dynamic_slice_in_dim(valid_group, held, 1)[:, None, None]

    silu_group = jax.nn.silu(cond_group).astype(jnp.bfloat16)
    silu_mine = lax.dynamic_slice_in_dim(silu_group, place * rows, rows, 1)
    ada_bias_row = lax.dynamic_update_slice_in_dim(
        jnp.zeros((ada_weight.shape[1],), jnp.float32),
        ada_bias.astype(jnp.float32),
        place * ada_bias.shape[0],
        0,
    )
    modulation_all = lax.psum(matmul(silu_mine, ada_weight) + ada_bias_row, GROUP)
    modulation = lax.dynamic_slice_in_dim(modulation_all, held, 1, 0)
    shift_one, scale_one, gate_one, shift_two, scale_two, gate_two = jnp.split(
        modulation, 6, axis=-1
    )

    latent = latent_low[0].astype(jnp.float32)
    normed_one, inverse_one = normalize(latent)
    hidden_one = (normed_one * (1.0 + scale_one) + shift_one).astype(jnp.bfloat16)
    bias_full = jnp.concatenate(
        [full_qv_bias[:width], jnp.zeros((width,), jnp.float32), full_qv_bias[width:]]
    )
    projected = (matmul(hidden_one, full_qkv) + bias_full).astype(jnp.bfloat16)
    query = projected[:, :width]
    pair_own = projected[:, width:]
    pair_other = permute(pair_own, core_rule)
    pair_all = jnp.concatenate([pair_own, pair_other], axis=0)[None]
    keys = pair_all[..., :width]
    values = pair_all[..., width:]
    attended, log_totals = attn_forward(query[None], keys, values, score_scale)
    attended_low = attended[0].astype(jnp.bfloat16)
    branch_one = matmul(attended_low, full_out) + full_out_bias
    middle = latent + gate_one * branch_one

    normed_two, inverse_two = normalize(middle)
    hidden_two = (normed_two * (1.0 + scale_two) + shift_two).astype(jnp.bfloat16)
    preact = matmul(hidden_two, full_up) + full_up_bias
    activated, gelu_pull = jax.vjp(lambda inner: jax.nn.gelu(inner, approximate=True), preact)
    activated_low = activated.astype(jnp.bfloat16)
    branch_two = matmul(activated_low, full_down) + full_down_bias
    mask_row = slot_mask[0]
    block_out = (mask_row * (middle + gate_two * branch_two)).astype(jnp.bfloat16)
    block_out = permute(block_out[None], swap_rule)

    d_out = cotangent_low[0].astype(jnp.float32) * mask_row
    d_gate_two = jnp.sum(d_out * branch_two, axis=0)
    d_branch_two = (gate_two * d_out).astype(jnp.bfloat16)
    down_grad = matmul_left(activated_low, d_branch_two).astype(jnp.bfloat16)
    down_shard = lax.psum_scatter(down_grad, GROUP, scatter_dimension=0, tiled=True)
    down_total = lax.psum(down_shard, "rep").astype(jnp.float32)
    down_bias_grad = jnp.sum(d_branch_two.astype(jnp.float32), axis=0)
    d_activated = matmul_right(d_branch_two, full_down)
    d_preact = gelu_pull(d_activated)[0].astype(jnp.bfloat16)

    up_grad = matmul_left(hidden_two, d_preact).astype(jnp.bfloat16)
    up_shard = reduce_scatter(up_grad.reshape(SHARDS, rows, hidden_width))
    up_total = lax.psum(up_shard.astype(jnp.bfloat16), "rep").astype(jnp.float32)
    up_bias_grad = jnp.sum(d_preact.astype(jnp.float32), axis=0)
    d_hidden_two = matmul_right(d_preact, full_up)
    d_shift_two = jnp.sum(d_hidden_two, axis=0)
    d_scale_two = jnp.sum(d_hidden_two * normed_two, axis=0)
    d_middle = d_out + norm_back(d_hidden_two * (1.0 + scale_two), normed_two, inverse_two)
    d_gate_one = jnp.sum(d_middle * branch_one, axis=0)
    d_branch_one = (gate_one * d_middle).astype(jnp.bfloat16)

    out_grad = matmul_left(attended_low, d_branch_one).astype(jnp.bfloat16)
    out_shard = reduce_scatter(out_grad.reshape(SHARDS, rows, width))
    out_total = lax.psum(out_shard.astype(jnp.bfloat16), "rep").astype(jnp.float32)
    out_bias_grad = jnp.sum(d_branch_one.astype(jnp.float32), axis=0)
    d_attended = matmul_right(d_branch_one, full_out).astype(jnp.bfloat16)
    d_query, d_keys_all, d_values_all = attn_backward(
        query[None], keys, values, d_attended[None], log_totals, score_scale
    )
    d_pair = jnp.concatenate([d_keys_all[0], d_values_all[0]], axis=-1)
    d_pair_other = permute(d_pair[length:].astype(jnp.bfloat16), core_rule)
    d_pair = d_pair[:length] + d_pair_other.astype(jnp.float32)
    d_projected = jnp.concatenate([d_query[0], d_pair], axis=-1).astype(jnp.bfloat16)

    qkv_grad = matmul_left(hidden_one, d_projected).astype(jnp.bfloat16)
    qkv_shard = reduce_scatter(qkv_grad.reshape(SHARDS, rows, 3 * width))
    qkv_total = lax.psum(qkv_shard.astype(jnp.bfloat16), "rep").astype(jnp.float32)
    column_sums = jnp.sum(d_projected.astype(jnp.float32), axis=0)
    d_hidden_one = matmul_right(d_projected, full_qkv)
    d_shift_one = jnp.sum(d_hidden_one, axis=0)
    d_scale_one = jnp.sum(d_hidden_one * normed_one, axis=0)
    latent_grad = d_middle + norm_back(d_hidden_one * (1.0 + scale_one), normed_one, inverse_one)
    latent_grad = permute(latent_grad.astype(jnp.bfloat16)[None], swap_rule).astype(jnp.float32)

    bias_grads = (
        jnp.concatenate([column_sums[:width], column_sums[2 * width :]]),
        out_bias_grad,
        up_bias_grad,
        down_bias_grad,
    )
    sums = [d_shift_one, d_scale_one, d_gate_one, d_shift_two, d_scale_two, d_gate_two]
    ada_width = 6 * width
    sums_all = lax.all_gather(jnp.concatenate(sums + list(bias_grads)), GROUP, axis=0)
    d_group = sums_all[:, :ada_width].reshape(2, 2, 2, ada_width).sum(1).reshape(4, ada_width)
    bias_mine = []
    start = ada_width
    for grad in bias_grads:
        total = jnp.sum(sums_all[:, start : start + grad.shape[0]], axis=0)
        piece = grad.shape[0] // SHARDS
        bias_mine.append(lax.dynamic_slice_in_dim(total, place * piece, piece))
        start += grad.shape[0]
    d_silu = lax.dot_general(
        d_group,
        ada_weight.astype(jnp.float32),
        (((1,), (1,)), ((), ())),
        precision=exact_mode,
    )
    cond_mine = lax.dynamic_slice_in_dim(cond_group, place * rows, rows, 1)
    cond_part = jax.vjp(jax.nn.silu, cond_mine)[1](d_silu)[0]
    cond_all = lax.all_gather(cond_part, GROUP, axis=1, tiled=True)
    cond_grad = lax.dynamic_slice_in_dim(cond_all, fsdp_index, 1, 0)

    packed = jnp.concatenate(
        [d_group.reshape(-1), silu_mine.astype(jnp.float32).reshape(-1)] + bias_mine
    )
    packed_all = lax.all_gather(packed, "rep", axis=0)
    d_all = packed_all[:, : 4 * ada_width].reshape(-1, ada_width)
    silu_all = packed_all[:, 4 * ada_width : 4 * ada_width + 4 * rows].reshape(-1, rows)
    ada_total = lax.dot_general(
        silu_all, d_all, (((0,), (0,)), ((), ())), precision=exact_mode
    )
    ada_bias_total = jnp.sum(
        lax.dynamic_slice_in_dim(d_all, place * ada_bias.shape[0], ada_bias.shape[0], 1), axis=0
    )
    bias_totals = jnp.sum(packed_all[:, 4 * ada_width + 4 * rows :], axis=0)
    cuts = [0]
    for piece in bias_mine:
        cuts.append(cuts[-1] + piece.shape[0])
    qv_total, out_bias_total, up_bias_total, down_bias_total = (
        bias_totals[low:high] for low, high in zip(cuts[:-1], cuts[1:])
    )
    return (
        block_out,
        latent_grad,
        cond_grad,
        ada_total,
        ada_bias_total,
        qkv_total,
        qv_total,
        out_total,
        out_bias_total,
        up_total,
        up_bias_total,
        down_total,
        down_bias_total,
    )


def solution(mesh):
    tokens = P(("rep", "fsdp"), "sp", None)
    rows = P(("rep", "fsdp"), None)
    matrix = P(GROUP, None)
    vector = P(GROUP)
    weights = (matrix, vector) * 5
    return jax.shard_map(
        per_device,
        mesh=mesh,
        in_specs=(tokens, rows, P(("rep", "fsdp"))) + weights + (tokens,),
        out_specs=(tokens, tokens, rows) + weights,
        check_vma=False,
    )
```

```python
import jax
import jax.numpy as jnp
from jax import lax
from jax.experimental import pallas as pl
from jax.experimental.pallas import tpu as pltpu
from jax.sharding import PartitionSpec as P

HEAD = 72
GROUP = ("fsdp", "sp")
SHARDS = 8

exact_mode = lax.Precision.HIGHEST
epsilon = 1e-06


def normalize(values):
    average = jnp.mean(values, -1, keepdims=True)
    centered = values - average
    inverse = lax.rsqrt(jnp.mean(centered * centered, -1, keepdims=True) + epsilon)
    return (centered * inverse, inverse)


def norm_back(upstream, normed, inverse):
    return (
        upstream
        - jnp.mean(upstream, -1, keepdims=True)
        - normed * jnp.mean(upstream * normed, -1, keepdims=True)
    ) * inverse


def matmul(left, right):
    return jnp.dot(left, right, preferred_element_type=jnp.float32)


def matmul_left(left, right):
    return lax.dot_general(
        left, right, (((0,), (0,)), ((), ())), preferred_element_type=jnp.float32
    )


def matmul_right(left, right):
    return lax.dot_general(
        left, right, (((1,), (1,)), ((), ())), preferred_element_type=jnp.float32
    )


def place_of():
    return lax.axis_index("fsdp") * 2 + lax.axis_index("sp")


def pairs_by(rule):
    return [(place, rule(place)) for place in range(SHARDS)]


def swap_rule(place):
    return (place & 4) | ((place & 1) << 1) | ((place >> 1) & 1)


def core_rule(place):
    return place ^ 2


def first_rule(place):
    return place ^ (1 if place & 2 else 4)


def second_rule(place):
    return place ^ (4 if place & 2 else 1)


def permute(values, rule):
    return lax.ppermute(values, GROUP, pairs_by(rule))


def swap_halves(values):
    place = place_of()
    pairs = [pair for pair in pairs_by(swap_rule) if pair[0] != pair[1]]
    received = lax.ppermute(values, GROUP, pairs)
    stays = ((place >> 1) & 1) == (place & 1)
    return jnp.where(stays, values, received)


def gather_group(values):
    place = place_of()
    stacked = values[None]
    for bit in (1, 2, 4):
        received = permute(stacked, lambda at: at ^ bit)
        stacked = jnp.where(
            (place & bit) == 0,
            jnp.concatenate([stacked, received]),
            jnp.concatenate([received, stacked]),
        )
    return stacked


def gather_replicas(values, replicas):
    stacked = [values]
    for shift in range(1, replicas):
        pairs = [(at, (at + shift) % replicas) for at in range(replicas)]
        stacked.append(lax.ppermute(values, "rep", pairs))
    return jnp.stack(stacked)


def reduce_replicas(partial, replicas):
    low = jnp.bfloat16
    rows, columns = partial.shape
    own = lax.axis_index("rep")
    pieces = partial.astype(low).reshape(replicas, rows // replicas, columns)
    total = lax.dynamic_index_in_dim(
        partial.reshape(pieces.shape), own, 0, keepdims=False
    )
    for shift in range(1, replicas):
        pairs = [(at, (at + shift) % replicas) for at in range(replicas)]
        piece = lax.dynamic_index_in_dim(pieces, (own + shift) % replicas, 0, keepdims=False)
        total = total + lax.ppermute(piece, "rep", pairs).astype(jnp.float32)
    stacked = gather_replicas(total.astype(low), replicas)
    ordered = [
        lax.dynamic_index_in_dim(stacked, (own - at) % replicas, 0, keepdims=False)
        for at in range(replicas)
    ]
    return jnp.stack(ordered).reshape(rows, columns).astype(jnp.float32)


def assemble_kernel(order_ref, *refs):
    pieces, whole, buffer, load_sems, store_sems = (
        refs[:SHARDS],
        refs[SHARDS],
        refs[SHARDS + 1],
        refs[SHARDS + 2],
        refs[SHARDS + 3],
    )
    rows = buffer.shape[1]
    loads = [
        pltpu.make_async_copy(piece, buffer.at[at], load_sems.at[at])
        for at, piece in enumerate(pieces)
    ]
    for load in loads:
        load.start()
    stores = []
    for at, load in enumerate(loads):
        load.wait()
        target = pl.ds(pl.multiple_of(order_ref[at] * rows, 16), rows)
        store = pltpu.make_async_copy(buffer.at[at], whole.at[target], store_sems.at[at])
        store.start()
        stores.append(store)
    for store in stores:
        store.wait()


def assemble(pieces, order):
    rows, columns = pieces[0].shape
    size = SHARDS * rows * columns * 2
    return pl.pallas_call(
        assemble_kernel,
        out_shape=jax.ShapeDtypeStruct((SHARDS * rows, columns), pieces[0].dtype),
        in_specs=[pl.BlockSpec(memory_space=pltpu.SMEM)]
        + [pl.BlockSpec(memory_space=pl.ANY)] * SHARDS,
        out_specs=pl.BlockSpec(memory_space=pl.ANY),
        scratch_shapes=[
            pltpu.VMEM((SHARDS, rows, columns), pieces[0].dtype),
            pltpu.SemaphoreType.DMA((SHARDS,)),
            pltpu.SemaphoreType.DMA((SHARDS,)),
        ],
        compiler_params=pltpu.CompilerParams(vmem_limit_bytes=size + (4 << 20)),
        cost_estimate=pl.CostEstimate(flops=0, bytes_accessed=2 * size, transcendentals=0),
    )(order, *pieces)


def gather_weight(shard):
    place = place_of()
    near = jnp.where((place & 2) == 0, 4, 1)
    far = 5 - near
    other = place ^ 2
    first = permute(shard, first_rule)
    second = permute(shard, second_rule)
    both = permute(first, second_rule)
    held = [shard, first, second, both]
    pieces = held + [permute(piece, core_rule) for piece in held]
    order = [place, place ^ near, place ^ far, place ^ 5]
    order += [other, other ^ far, other ^ near, other ^ 5]
    return assemble(pieces, jnp.stack(order).astype(jnp.int32))


def reduce_scatter(partial):
    low = partial.dtype
    place = place_of()
    core = (place >> 1) & 1
    _, rows, columns = partial.shape
    spread = partial.reshape(2, 2, 2, rows, columns)

    def core_half(which):
        return lax.dynamic_index_in_dim(spread, which, 1, keepdims=False)

    received = permute(core_half(1 - core), core_rule)
    kept = (core_half(core).astype(jnp.float32) + received.astype(jnp.float32)).astype(low)
    kept = kept.reshape(4, rows, columns)
    mine = ((place >> 2) << 1) | (place & 1)
    near = jnp.where(core == 0, 2, 1)
    far = 3 - near

    def block(which):
        return lax.dynamic_slice_in_dim(kept, which, 1, 0)

    received = permute(jnp.concatenate([block(mine ^ near), block(mine ^ 3)]), first_rule)
    halved = jnp.concatenate([block(mine), block(mine ^ far)]).astype(jnp.float32)
    halved = halved + received.astype(jnp.float32)
    received = permute(halved[1].astype(low), second_rule)
    return halved[0] + received.astype(jnp.float32)


def head_slice(values, group_index, group_width):
    number, length, model_width = values.shape
    piece = lax.dynamic_slice_in_dim(values, group_index * group_width, group_width, 2)
    return piece.reshape(number, length, 4, HEAD)


def join_groups(stacked):
    groups, number, length, group_width = stacked.shape
    return jnp.moveaxis(stacked, 0, 2).reshape(number, length, groups * group_width)


def attn_forward(query, keys, values, score_scale):
    group_width = 4 * HEAD
    groups = query.shape[2] // group_width

    def per_group(group_index):
        query_part = head_slice(query, group_index, group_width)
        keys_part = head_slice(keys, group_index, group_width)
        values_part = head_slice(values, group_index, group_width)
        scores = (
            jnp.einsum("lqhd,lkhd->lhqk", query_part, keys_part, preferred_element_type=jnp.float32)
            * score_scale
        )
        row_max = jnp.max(scores, -1, keepdims=True)
        weights = jnp.exp(scores - row_max)
        row_total = jnp.sum(weights, -1, keepdims=True)
        probs = (weights / row_total).astype(jnp.bfloat16)
        mixed = jnp.einsum(
            "lhqk,lkhd->lqhd", probs, values_part, preferred_element_type=jnp.float32
        )
        log_total = row_max[..., 0] + jnp.log(row_total[..., 0])
        return (mixed.reshape(mixed.shape[0], mixed.shape[1], group_width), log_total)

    mixed_all, log_totals = lax.map(per_group, jnp.arange(groups))
    return (join_groups(mixed_all), log_totals)


def attn_backward(query, keys, values, upstream, log_totals, score_scale):
    group_width = 4 * HEAD
    groups = query.shape[2] // group_width

    def per_group(group_item):
        group_index, log_total = group_item
        query_part = head_slice(query, group_index, group_width)
        keys_part = head_slice(keys, group_index, group_width)
        values_part = head_slice(values, group_index, group_width)
        upstream_part = head_slice(upstream, group_index, group_width)
        scores = (
            jnp.einsum("lqhd,lkhd->lhqk", query_part, keys_part, preferred_element_type=jnp.float32)
            * score_scale
        )
        probs = jnp.exp(scores - log_total[..., None])
        d_probs = jnp.einsum(
            "lqhd,lkhd->lhqk", upstream_part, values_part, preferred_element_type=jnp.float32
        )
        d_scores = (probs * (d_probs - jnp.sum(probs * d_probs, -1, keepdims=True))).astype(
            jnp.bfloat16
        )
        d_query = (
            jnp.einsum("lhqk,lkhd->lqhd", d_scores, keys_part, preferred_element_type=jnp.float32)
            * score_scale
        )
        d_keys = (
            jnp.einsum("lhqk,lqhd->lkhd", d_scores, query_part, preferred_element_type=jnp.float32)
            * score_scale
        )
        d_values = jnp.einsum(
            "lhqk,lqhd->lkhd",
            probs.astype(jnp.bfloat16),
            upstream_part,
            preferred_element_type=jnp.float32,
        )
        number = d_query.shape[0]
        return (
            d_query.reshape(number, d_query.shape[1], group_width),
            d_keys.reshape(number, d_keys.shape[1], group_width),
            d_values.reshape(number, d_values.shape[1], group_width),
        )

    d_query, d_keys, d_values = lax.map(per_group, (jnp.arange(groups), log_totals))
    return (join_groups(d_query), join_groups(d_keys), join_groups(d_values))


def per_device(
    latent_in,
    condition,
    valid_slots,
    ada_weight,
    ada_bias,
    qkv_weight,
    qv_bias,
    out_weight,
    out_bias,
    up_weight,
    up_bias,
    down_weight,
    down_bias,
    cotangent,
):
    number, length, width = latent_in.shape
    hidden_width = up_weight.shape[1]
    score_scale = float(HEAD) ** (-0.5)
    place = place_of()
    fsdp_index = lax.axis_index("fsdp")
    held = (place >> 2) * 2 + (place & 1)
    rows = width // SHARDS
    replicas = lax.axis_size("rep")

    small = jnp.concatenate(
        [
            condition[0],
            qv_bias,
            out_bias,
            up_bias,
            down_bias,
            jnp.broadcast_to(valid_slots.astype(jnp.bfloat16), (128,)),
        ]
    )
    small_all = gather_group(small)
    full_qkv = gather_weight(qkv_weight)
    latent_low = swap_halves(latent_in)
    full_out = gather_weight(out_weight)
    cotangent_low = swap_halves(cotangent)
    full_up = gather_weight(up_weight)
    full_down = gather_weight(down_weight)

    bounds = [0, width]
    for bias in (qv_bias, out_bias, up_bias, down_bias):
        bounds.append(bounds[-1] + bias.shape[0])
    cond_group = small_all[::2, :width].astype(jnp.float32)
    full_qv_bias, full_out_bias, full_up_bias, full_down_bias = (
        small_all[:, low:high].reshape(-1).astype(jnp.float32)
        for low, high in zip(bounds[1:-1], bounds[2:])
    )
    valid_group = small_all[::2, bounds[-1]].astype(jnp.float32)
    slot_mask = lax.dynamic_slice_in_dim(valid_group, held, 1)[:, None, None]

    silu_group = jax.nn.silu(cond_group).astype(jnp.bfloat16)
    silu_mine = lax.dynamic_slice_in_dim(silu_group, place * rows, rows, 1)
    ada_bias_row = lax.dynamic_update_slice_in_dim(
        jnp.zeros((ada_weight.shape[1],), jnp.float32),
        ada_bias.astype(jnp.float32),
        place * ada_bias.shape[0],
        0,
    )
    modulation = matmul(silu_mine, ada_weight) + ada_bias_row
    for bit, count in ((4, 2), (1, 1)):
        upper = (place & bit) != 0
        sent = jnp.where(upper, modulation[:count], modulation[count:])
        kept = jnp.where(upper, modulation[count:], modulation[:count])
        modulation = kept + permute(sent, lambda at: at ^ bit)
    modulation = modulation + permute(modulation, core_rule)
    shift_one, scale_one, gate_one, shift_two, scale_two, gate_two = jnp.split(
        modulation, 6, axis=-1
    )

    latent = latent_low[0].astype(jnp.float32)
    normed_one, inverse_one = normalize(latent)
    hidden_one = (normed_one * (1.0 + scale_one) + shift_one).astype(jnp.bfloat16)
    bias_full = jnp.concatenate(
        [full_qv_bias[:width], jnp.zeros((width,), jnp.float32), full_qv_bias[width:]]
    )
    projected = (matmul(hidden_one, full_qkv) + bias_full).astype(jnp.bfloat16)
    query = projected[:, :width]
    pair_own = projected[:, width:]
    pair_other = permute(pair_own, core_rule)
    pair_all = jnp.concatenate([pair_own, pair_other], axis=0)[None]
    keys = pair_all[..., :width]
    values = pair_all[..., width:]
    attended, log_totals = attn_forward(query[None], keys, values, score_scale)
    attended_low = attended[0].astype(jnp.bfloat16)
    branch_one = matmul(attended_low, full_out) + full_out_bias
    middle = latent + gate_one * branch_one

    normed_two, inverse_two = normalize(middle)
    hidden_two = (normed_two * (1.0 + scale_two) + shift_two).astype(jnp.bfloat16)
    preact = matmul(hidden_two, full_up) + full_up_bias
    activated, gelu_pull = jax.vjp(lambda inner: jax.nn.gelu(inner, approximate=True), preact)
    activated_low = activated.astype(jnp.bfloat16)
    branch_two = matmul(activated_low, full_down) + full_down_bias
    mask_row = slot_mask[0]
    block_out = (mask_row * (middle + gate_two * branch_two)).astype(jnp.bfloat16)
    block_out = swap_halves(block_out[None])

    d_out = cotangent_low[0].astype(jnp.float32) * mask_row
    d_gate_two = jnp.sum(d_out * branch_two, axis=0)
    d_branch_two = (gate_two * d_out).astype(jnp.bfloat16)
    down_grad = matmul_left(activated_low, d_branch_two).astype(jnp.bfloat16)
    down_shard = reduce_scatter(down_grad.reshape(SHARDS, hidden_width // SHARDS, width))
    down_total = reduce_replicas(down_shard, replicas)
    down_bias_grad = jnp.sum(d_branch_two.astype(jnp.float32), axis=0)
    d_activated = matmul_right(d_branch_two, full_down)
    d_preact = gelu_pull(d_activated)[0].astype(jnp.bfloat16)

    up_grad = matmul_left(hidden_two, d_preact).astype(jnp.bfloat16)
    up_shard = reduce_scatter(up_grad.reshape(SHARDS, rows, hidden_width))
    up_total = reduce_replicas(up_shard, replicas)
    up_bias_grad = jnp.sum(d_preact.astype(jnp.float32), axis=0)
    d_hidden_two = matmul_right(d_preact, full_up)
    d_shift_two = jnp.sum(d_hidden_two, axis=0)
    d_scale_two = jnp.sum(d_hidden_two * normed_two, axis=0)
    d_middle = d_out + norm_back(d_hidden_two * (1.0 + scale_two), normed_two, inverse_two)
    d_gate_one = jnp.sum(d_middle * branch_one, axis=0)
    d_branch_one = (gate_one * d_middle).astype(jnp.bfloat16)

    out_grad = matmul_left(attended_low, d_branch_one).astype(jnp.bfloat16)
    out_shard = reduce_scatter(out_grad.reshape(SHARDS, rows, width))
    out_total = reduce_replicas(out_shard, replicas)
    out_bias_grad = jnp.sum(d_branch_one.astype(jnp.float32), axis=0)
    d_attended = matmul_right(d_branch_one, full_out).astype(jnp.bfloat16)
    d_query, d_keys_all, d_values_all = attn_backward(
        query[None], keys, values, d_attended[None], log_totals, score_scale
    )
    d_pair = jnp.concatenate([d_keys_all[0], d_values_all[0]], axis=-1)
    d_pair_other = permute(d_pair[length:].astype(jnp.bfloat16), core_rule)
    d_pair = d_pair[:length] + d_pair_other.astype(jnp.float32)
    d_projected = jnp.concatenate([d_query[0], d_pair], axis=-1).astype(jnp.bfloat16)

    qkv_grad = matmul_left(hidden_one, d_projected).astype(jnp.bfloat16)
    qkv_shard = reduce_scatter(qkv_grad.reshape(SHARDS, rows, 3 * width))
    qkv_total = reduce_replicas(qkv_shard, replicas)
    column_sums = jnp.sum(d_projected.astype(jnp.float32), axis=0)
    d_hidden_one = matmul_right(d_projected, full_qkv)
    d_shift_one = jnp.sum(d_hidden_one, axis=0)
    d_scale_one = jnp.sum(d_hidden_one * normed_one, axis=0)
    latent_grad = d_middle + norm_back(d_hidden_one * (1.0 + scale_one), normed_one, inverse_one)
    latent_grad = swap_halves(latent_grad.astype(jnp.bfloat16)[None]).astype(jnp.float32)

    bias_grads = (
        jnp.concatenate([column_sums[:width], column_sums[2 * width :]]),
        out_bias_grad,
        up_bias_grad,
        down_bias_grad,
    )
    sums = [d_shift_one, d_scale_one, d_gate_one, d_shift_two, d_scale_two, d_gate_two]
    ada_width = 6 * width
    sums_all = gather_group(jnp.concatenate(sums + list(bias_grads)))
    d_group = sums_all[:, :ada_width].reshape(2, 2, 2, ada_width).sum(1).reshape(4, ada_width)
    bias_mine = []
    start = ada_width
    for grad in bias_grads:
        total = jnp.sum(sums_all[:, start : start + grad.shape[0]], axis=0)
        piece = grad.shape[0] // SHARDS
        bias_mine.append(lax.dynamic_slice_in_dim(total, place * piece, piece))
        start += grad.shape[0]
    d_silu = lax.dot_general(
        d_group,
        ada_weight.astype(jnp.float32),
        (((1,), (1,)), ((), ())),
        precision=exact_mode,
    )
    cond_mine = lax.dynamic_slice_in_dim(cond_group, place * rows, rows, 1)
    cond_part = jax.vjp(jax.nn.silu, cond_mine)[1](d_silu)[0]
    cond_all = gather_group(cond_part)
    cond_grad = lax.dynamic_index_in_dim(cond_all, fsdp_index, 1, keepdims=False)
    cond_grad = cond_grad.reshape(1, width)

    packed = jnp.concatenate(
        [d_group.reshape(-1), silu_mine.astype(jnp.float32).reshape(-1)] + bias_mine
    )
    packed_all = gather_replicas(packed, replicas)
    d_all = packed_all[:, : 4 * ada_width].reshape(-1, ada_width)
    silu_all = packed_all[:, 4 * ada_width : 4 * ada_width + 4 * rows].reshape(-1, rows)
    ada_total = lax.dot_general(
        silu_all, d_all, (((0,), (0,)), ((), ())), precision=exact_mode
    )
    ada_bias_total = jnp.sum(
        lax.dynamic_slice_in_dim(d_all, place * ada_bias.shape[0], ada_bias.shape[0], 1), axis=0
    )
    bias_totals = jnp.sum(packed_all[:, 4 * ada_width + 4 * rows :], axis=0)
    cuts = [0]
    for piece in bias_mine:
        cuts.append(cuts[-1] + piece.shape[0])
    qv_total, out_bias_total, up_bias_total, down_bias_total = (
        bias_totals[low:high] for low, high in zip(cuts[:-1], cuts[1:])
    )
    return (
        block_out,
        latent_grad,
        cond_grad,
        ada_total,
        ada_bias_total,
        qkv_total,
        qv_total,
        out_total,
        out_bias_total,
        up_total,
        up_bias_total,
        down_total,
        down_bias_total,
    )


def solution(mesh):
    tokens = P(("rep", "fsdp"), "sp", None)
    rows = P(("rep", "fsdp"), None)
    matrix = P(GROUP, None)
    vector = P(GROUP)
    weights = (matrix, vector) * 5
    return jax.shard_map(
        per_device,
        mesh=mesh,
        in_specs=(tokens, rows, P(("rep", "fsdp"))) + weights + (tokens,),
        out_specs=(tokens, tokens, rows) + weights,
        check_vma=False,
    )
```

```python
import jax
import jax.numpy as jnp
from jax import lax
from jax.experimental import pallas as pl
from jax.experimental.pallas import tpu as pltpu
from jax.sharding import PartitionSpec as P

HEAD = 72
GROUP = ("fsdp", "sp")
SHARDS = 8

exact_mode = lax.Precision.HIGHEST
epsilon = 1e-06


def normalize(values):
    average = jnp.mean(values, -1, keepdims=True)
    centered = values - average
    inverse = lax.rsqrt(jnp.mean(centered * centered, -1, keepdims=True) + epsilon)
    return (centered * inverse, inverse)


def norm_back(upstream, normed, inverse):
    return (
        upstream
        - jnp.mean(upstream, -1, keepdims=True)
        - normed * jnp.mean(upstream * normed, -1, keepdims=True)
    ) * inverse


def matmul(left, right):
    return jnp.dot(left, right, preferred_element_type=jnp.float32)


def matmul_left(left, right):
    return lax.dot_general(
        left, right, (((0,), (0,)), ((), ())), preferred_element_type=jnp.float32
    )


def matmul_right(left, right):
    return lax.dot_general(
        left, right, (((1,), (1,)), ((), ())), preferred_element_type=jnp.float32
    )


def place_of():
    return lax.axis_index("fsdp") * 2 + lax.axis_index("sp")


def pairs_by(rule):
    return [(place, rule(place)) for place in range(SHARDS)]


def swap_rule(place):
    return (place & 4) | ((place & 1) << 1) | ((place >> 1) & 1)


def core_rule(place):
    return place ^ 2


def first_rule(place):
    return place ^ (1 if place & 2 else 4)


def second_rule(place):
    return place ^ (4 if place & 2 else 1)


def permute(values, rule):
    return lax.ppermute(values, GROUP, pairs_by(rule))


def swap_halves(values):
    place = place_of()
    pairs = [pair for pair in pairs_by(swap_rule) if pair[0] != pair[1]]
    received = lax.ppermute(values, GROUP, pairs)
    stays = ((place >> 1) & 1) == (place & 1)
    return jnp.where(stays, values, received)


def gather_group(values):
    place = place_of()
    stacked = values[None]
    for bit in (1, 2, 4):
        received = permute(stacked, lambda at: at ^ bit)
        stacked = jnp.where(
            (place & bit) == 0,
            jnp.concatenate([stacked, received]),
            jnp.concatenate([received, stacked]),
        )
    return stacked


def gather_replicas(values, replicas):
    stacked = [values]
    for shift in range(1, replicas):
        pairs = [(at, (at + shift) % replicas) for at in range(replicas)]
        stacked.append(lax.ppermute(values, "rep", pairs))
    return jnp.stack(stacked)


def assemble_kernel(order_ref, *refs):
    pieces, whole, buffer, load_sems, store_sems = (
        refs[:SHARDS],
        refs[SHARDS],
        refs[SHARDS + 1],
        refs[SHARDS + 2],
        refs[SHARDS + 3],
    )
    rows = buffer.shape[1]
    loads = [
        pltpu.make_async_copy(piece, buffer.at[at], load_sems.at[at])
        for at, piece in enumerate(pieces)
    ]
    for load in loads:
        load.start()
    stores = []
    for at, load in enumerate(loads):
        load.wait()
        target = pl.ds(pl.multiple_of(order_ref[at] * rows, 16), rows)
        store = pltpu.make_async_copy(buffer.at[at], whole.at[target], store_sems.at[at])
        store.start()
        stores.append(store)
    for store in stores:
        store.wait()


def assemble(pieces, order):
    rows, columns = pieces[0].shape
    size = SHARDS * rows * columns * 2
    return pl.pallas_call(
        assemble_kernel,
        out_shape=jax.ShapeDtypeStruct((SHARDS * rows, columns), pieces[0].dtype),
        in_specs=[pl.BlockSpec(memory_space=pltpu.SMEM)]
        + [pl.BlockSpec(memory_space=pl.ANY)] * SHARDS,
        out_specs=pl.BlockSpec(memory_space=pl.ANY),
        scratch_shapes=[
            pltpu.VMEM((SHARDS, rows, columns), pieces[0].dtype),
            pltpu.SemaphoreType.DMA((SHARDS,)),
            pltpu.SemaphoreType.DMA((SHARDS,)),
        ],
        compiler_params=pltpu.CompilerParams(vmem_limit_bytes=size + (4 << 20)),
        cost_estimate=pl.CostEstimate(flops=0, bytes_accessed=2 * size, transcendentals=0),
    )(order, *pieces)


def gather_weight(shard):
    place = place_of()
    near = jnp.where((place & 2) == 0, 4, 1)
    far = 5 - near
    other = place ^ 2
    first = permute(shard, first_rule)
    second = permute(shard, second_rule)
    both = permute(first, second_rule)
    held = [shard, first, second, both]
    pieces = held + [permute(piece, core_rule) for piece in held]
    order = [place, place ^ near, place ^ far, place ^ 5]
    order += [other, other ^ far, other ^ near, other ^ 5]
    return assemble(pieces, jnp.stack(order).astype(jnp.int32))


def reduce_scatter(partial):
    low = partial.dtype
    place = place_of()
    core = (place >> 1) & 1
    _, rows, columns = partial.shape
    spread = partial.reshape(2, 2, 2, rows, columns)

    def core_half(which):
        return lax.dynamic_index_in_dim(spread, which, 1, keepdims=False)

    received = permute(core_half(1 - core), core_rule)
    kept = (core_half(core).astype(jnp.float32) + received.astype(jnp.float32)).astype(low)
    kept = kept.reshape(4, rows, columns)
    mine = ((place >> 2) << 1) | (place & 1)
    near = jnp.where(core == 0, 2, 1)
    far = 3 - near

    def block(which):
        return lax.dynamic_slice_in_dim(kept, which, 1, 0)

    received = permute(jnp.concatenate([block(mine ^ near), block(mine ^ 3)]), first_rule)
    halved = jnp.concatenate([block(mine), block(mine ^ far)]).astype(jnp.float32)
    halved = halved + received.astype(jnp.float32)
    received = permute(halved[1].astype(low), second_rule)
    return halved[0] + received.astype(jnp.float32)


WINDOW = 256


def head_window(width):
    first = pl.program_id(0) * HEAD
    start = jnp.minimum(first // 128 * 128, width - WINDOW)
    start = pl.multiple_of(start, 128)
    lane = lax.broadcasted_iota(jnp.int32, (1, WINDOW), 1) + start
    inside = (lane >= first) & (lane < first + HEAD)
    mask = jnp.where(inside, 1.0, 0.0).astype(jnp.bfloat16)
    return pl.ds(start, WINDOW), pl.ds(pl.multiple_of(start + width, 128), WINDOW), mask


def dot_last(left, right):
    return lax.dot_general(
        left, right, (((1,), (1,)), ((), ())), preferred_element_type=jnp.float32
    )


def dot_first(left, right):
    return lax.dot_general(
        left, right, (((0,), (0,)), ((), ())), preferred_element_type=jnp.float32
    )


def attend_kernel(query_ref, own_ref, other_ref, out_ref, log_ref, total_ref):
    length, width = query_ref.shape
    head = pl.program_id(0)
    key_lanes, value_lanes, mask = head_window(width)
    score_scale = float(HEAD) ** (-0.5)

    @pl.when(head == 0)
    def _():
        total_ref[...] = jnp.zeros_like(total_ref)
        log_ref[...] = jnp.zeros_like(log_ref)

    keys = jnp.concatenate([own_ref[:, key_lanes], other_ref[:, key_lanes]]) * mask
    values = jnp.concatenate([own_ref[:, value_lanes], other_ref[:, value_lanes]]) * mask
    rows = min(256, length)
    for at in range(0, length, rows):
        block = pl.ds(at, rows)
        scores = dot_last(query_ref[block, key_lanes], keys)
        row_max = jnp.max(scores, -1, keepdims=True)
        weights = jnp.exp((scores - row_max) * score_scale)
        row_total = jnp.sum(weights, -1, keepdims=True)
        probs = (weights * (1.0 / row_total)).astype(jnp.bfloat16)
        total_ref[block, key_lanes] += jnp.dot(
            probs, values, preferred_element_type=jnp.float32
        )
        log_total = row_max * score_scale + jnp.log(row_total)
        lane = lax.broadcasted_iota(jnp.int32, (rows, 128), 1)
        log_ref[block, :] = jnp.where(lane == head, log_total, log_ref[block, :])

    @pl.when(head == pl.num_programs(0) - 1)
    def _():
        out_ref[...] = total_ref[...].astype(out_ref.dtype)


def attend(query, own, other):
    length, width = query.shape
    heads = width // HEAD
    keys = own.shape[0] + other.shape[0]
    return pl.pallas_call(
        attend_kernel,
        grid=(heads,),
        out_shape=(
            jax.ShapeDtypeStruct((length, width), jnp.bfloat16),
            jax.ShapeDtypeStruct((length, 128), jnp.float32),
        ),
        in_specs=[
            pl.BlockSpec((length, width), lambda head: (0, 0)),
            pl.BlockSpec(own.shape, lambda head: (0, 0)),
            pl.BlockSpec(other.shape, lambda head: (0, 0)),
        ],
        out_specs=(
            pl.BlockSpec((length, width), lambda head: (0, 0)),
            pl.BlockSpec((length, 128), lambda head: (0, 0)),
        ),
        scratch_shapes=[pltpu.VMEM((length, width), jnp.float32)],
        compiler_params=pltpu.CompilerParams(vmem_limit_bytes=48 << 20),
        cost_estimate=pl.CostEstimate(
            flops=4 * heads * length * keys * WINDOW,
            bytes_accessed=4 * length * width * 4,
            transcendentals=heads * length * keys,
        ),
    )(query, own, other)


def attend_back_kernel(
    query_ref, own_ref, other_ref, upstream_ref, log_ref, d_query_ref, d_own_ref, d_other_ref,
    query_total, pair_total,
):
    length, width = query_ref.shape
    head = pl.program_id(0)
    key_lanes, value_lanes, mask = head_window(width)
    score_scale = float(HEAD) ** (-0.5)

    @pl.when(head == 0)
    def _():
        query_total[...] = jnp.zeros_like(query_total)
        pair_total[...] = jnp.zeros_like(pair_total)

    keys = jnp.concatenate([own_ref[:, key_lanes], other_ref[:, key_lanes]]) * mask
    values = jnp.concatenate([own_ref[:, value_lanes], other_ref[:, value_lanes]]) * mask
    rows = min(256, length)
    for at in range(0, length, rows):
        block = pl.ds(at, rows)
        query = query_ref[block, key_lanes] * mask
        upstream = upstream_ref[block, key_lanes] * mask
        scores = dot_last(keys, query)
        probs = jnp.exp(scores * score_scale - log_ref[0, :, block])
        d_probs = dot_last(values, upstream)
        weighted = probs * d_probs
        row_sum = jnp.sum(weighted, 0, keepdims=True)
        d_scores = (weighted - probs * row_sum).astype(jnp.bfloat16)
        pair_total[:, value_lanes] += jnp.dot(
            probs.astype(jnp.bfloat16), upstream, preferred_element_type=jnp.float32
        )
        pair_total[:, key_lanes] += score_scale * jnp.dot(
            d_scores, query, preferred_element_type=jnp.float32
        )
        query_total[block, key_lanes] += dot_first(d_scores, keys)

    @pl.when(head == pl.num_programs(0) - 1)
    def _():
        d_query_ref[...] = (query_total[...] * score_scale).astype(d_query_ref.dtype)
        d_own_ref[...] = pair_total[: own_ref.shape[0]]
        d_other_ref[...] = pair_total[own_ref.shape[0] :].astype(d_other_ref.dtype)


def attend_back(query, own, other, upstream, log_totals):
    length, width = query.shape
    heads = width // HEAD
    keys = own.shape[0] + other.shape[0]
    whole = lambda head: (0, 0)
    return pl.pallas_call(
        attend_back_kernel,
        grid=(heads,),
        out_shape=(
            jax.ShapeDtypeStruct((length, width), jnp.bfloat16),
            jax.ShapeDtypeStruct(own.shape, jnp.float32),
            jax.ShapeDtypeStruct(other.shape, jnp.bfloat16),
        ),
        in_specs=[
            pl.BlockSpec((length, width), whole),
            pl.BlockSpec(own.shape, whole),
            pl.BlockSpec(other.shape, whole),
            pl.BlockSpec((length, width), whole),
            pl.BlockSpec((1, 1, length), lambda head: (head, 0, 0)),
        ],
        out_specs=(
            pl.BlockSpec((length, width), whole),
            pl.BlockSpec(own.shape, whole),
            pl.BlockSpec(other.shape, whole),
        ),
        scratch_shapes=[
            pltpu.VMEM((length, width), jnp.float32),
            pltpu.VMEM((keys, own.shape[1]), jnp.float32),
        ],
        compiler_params=pltpu.CompilerParams(vmem_limit_bytes=56 << 20),
        cost_estimate=pl.CostEstimate(
            flops=10 * heads * length * keys * WINDOW,
            bytes_accessed=12 * length * width * 4,
            transcendentals=heads * length * keys,
        ),
    )(query, own, other, upstream, log_totals)


def per_device(
    latent_in,
    condition,
    valid_slots,
    ada_weight,
    ada_bias,
    qkv_weight,
    qv_bias,
    out_weight,
    out_bias,
    up_weight,
    up_bias,
    down_weight,
    down_bias,
    cotangent,
):
    number, length, width = latent_in.shape
    hidden_width = up_weight.shape[1]
    place = place_of()
    fsdp_index = lax.axis_index("fsdp")
    held = (place >> 2) * 2 + (place & 1)
    rows = width // SHARDS
    replicas = lax.axis_size("rep")

    small = jnp.concatenate(
        [
            condition[0],
            qv_bias,
            out_bias,
            up_bias,
            down_bias,
            jnp.broadcast_to(valid_slots.astype(jnp.bfloat16), (128,)),
        ]
    )
    small_all = gather_group(small)
    full_qkv = gather_weight(qkv_weight)
    latent_low = swap_halves(latent_in)
    full_out = gather_weight(out_weight)
    cotangent_low = swap_halves(cotangent)
    full_up = lax.all_gather(up_weight, GROUP, axis=0, tiled=True)
    full_down = lax.all_gather(down_weight, GROUP, axis=0, tiled=True)

    bounds = [0, width]
    for bias in (qv_bias, out_bias, up_bias, down_bias):
        bounds.append(bounds[-1] + bias.shape[0])
    cond_group = small_all[::2, :width].astype(jnp.float32)
    full_qv_bias, full_out_bias, full_up_bias, full_down_bias = (
        small_all[:, low:high].reshape(-1).astype(jnp.float32)
        for low, high in zip(bounds[1:-1], bounds[2:])
    )
    valid_group = small_all[::2, bounds[-1]].astype(jnp.float32)
    slot_mask = lax.dynamic_slice_in_dim(valid_group, held, 1)[:, None, None]

    silu_group = jax.nn.silu(cond_group).astype(jnp.bfloat16)
    silu_mine = lax.dynamic_slice_in_dim(silu_group, place * rows, rows, 1)
    ada_bias_row = lax.dynamic_update_slice_in_dim(
        jnp.zeros((ada_weight.shape[1],), jnp.float32),
        ada_bias.astype(jnp.float32),
        place * ada_bias.shape[0],
        0,
    )
    modulation = matmul(silu_mine, ada_weight) + ada_bias_row
    for bit, count in ((4, 2), (1, 1)):
        upper = (place & bit) != 0
        sent = jnp.where(upper, modulation[:count], modulation[count:])
        kept = jnp.where(upper, modulation[count:], modulation[:count])
        modulation = kept + permute(sent, lambda at: at ^ bit)
    modulation = modulation + permute(modulation, core_rule)
    shift_one, scale_one, gate_one, shift_two, scale_two, gate_two = jnp.split(
        modulation, 6, axis=-1
    )

    latent = latent_low[0].astype(jnp.float32)
    normed_one, inverse_one = normalize(latent)
    hidden_one = (normed_one * (1.0 + scale_one) + shift_one).astype(jnp.bfloat16)
    bias_full = jnp.concatenate(
        [full_qv_bias[:width], jnp.zeros((width,), jnp.float32), full_qv_bias[width:]]
    )
    projected = (matmul(hidden_one, full_qkv) + bias_full).astype(jnp.bfloat16)
    query = projected[:, :width]
    pair_own = projected[:, width:]
    pair_other = permute(pair_own, core_rule)
    attended_low, log_totals = attend(query, pair_own, pair_other)
    log_rows = log_totals[:, : width // HEAD].T[:, None, :]
    branch_one = matmul(attended_low, full_out) + full_out_bias
    middle = latent + gate_one * branch_one

    normed_two, inverse_two = normalize(middle)
    hidden_two = (normed_two * (1.0 + scale_two) + shift_two).astype(jnp.bfloat16)
    preact = matmul(hidden_two, full_up) + full_up_bias
    activated, gelu_pull = jax.vjp(lambda inner: jax.nn.gelu(inner, approximate=True), preact)
    activated_low = activated.astype(jnp.bfloat16)
    branch_two = matmul(activated_low, full_down) + full_down_bias
    mask_row = slot_mask[0]
    block_out = (mask_row * (middle + gate_two * branch_two)).astype(jnp.bfloat16)
    block_out = swap_halves(block_out[None])

    d_out = cotangent_low[0].astype(jnp.float32) * mask_row
    d_gate_two = jnp.sum(d_out * branch_two, axis=0)
    d_branch_two = (gate_two * d_out).astype(jnp.bfloat16)
    down_grad = matmul_left(activated_low, d_branch_two).astype(jnp.bfloat16)
    down_shard = lax.psum_scatter(down_grad, GROUP, scatter_dimension=0, tiled=True)
    down_total = lax.psum(down_shard, "rep")
    down_bias_grad = jnp.sum(d_branch_two.astype(jnp.float32), axis=0)
    d_activated = matmul_right(d_branch_two, full_down)
    d_preact = gelu_pull(d_activated)[0].astype(jnp.bfloat16)

    up_grad = matmul_left(hidden_two, d_preact).astype(jnp.bfloat16)
    up_shard = reduce_scatter(up_grad.reshape(SHARDS, rows, hidden_width))
    up_shard, down_total = lax.optimization_barrier((up_shard.astype(jnp.bfloat16), down_total))
    up_total = lax.psum(up_shard, "rep")
    up_bias_grad = jnp.sum(d_preact.astype(jnp.float32), axis=0)
    d_hidden_two = matmul_right(d_preact, full_up)
    d_shift_two = jnp.sum(d_hidden_two, axis=0)
    d_scale_two = jnp.sum(d_hidden_two * normed_two, axis=0)
    d_middle = d_out + norm_back(d_hidden_two * (1.0 + scale_two), normed_two, inverse_two)
    d_gate_one = jnp.sum(d_middle * branch_one, axis=0)
    d_branch_one = (gate_one * d_middle).astype(jnp.bfloat16)

    out_grad = matmul_left(attended_low, d_branch_one).astype(jnp.bfloat16)
    out_shard = reduce_scatter(out_grad.reshape(SHARDS, rows, width))
    out_bias_grad = jnp.sum(d_branch_one.astype(jnp.float32), axis=0)
    d_attended = matmul_right(d_branch_one, full_out).astype(jnp.bfloat16)
    d_query, d_pair, d_pair_other = attend_back(
        query, pair_own, pair_other, d_attended, log_rows
    )
    d_pair = d_pair + permute(d_pair_other, core_rule).astype(jnp.float32)
    d_projected = jnp.concatenate([d_query, d_pair.astype(jnp.bfloat16)], axis=-1)

    qkv_grad = matmul_left(hidden_one, d_projected).astype(jnp.bfloat16)
    qkv_shard = reduce_scatter(qkv_grad.reshape(SHARDS, rows, 3 * width))
    out_shard, qkv_shard, up_total = lax.optimization_barrier(
        (out_shard.astype(jnp.bfloat16), qkv_shard.astype(jnp.bfloat16), up_total)
    )
    out_total, qkv_total = lax.psum((out_shard, qkv_shard), "rep")
    column_sums = jnp.sum(d_projected.astype(jnp.float32), axis=0)
    d_hidden_one = matmul_right(d_projected, full_qkv)
    d_shift_one = jnp.sum(d_hidden_one, axis=0)
    d_scale_one = jnp.sum(d_hidden_one * normed_one, axis=0)
    latent_grad = d_middle + norm_back(d_hidden_one * (1.0 + scale_one), normed_one, inverse_one)
    latent_grad = swap_halves(latent_grad.astype(jnp.bfloat16)[None]).astype(jnp.float32)

    bias_grads = (
        jnp.concatenate([column_sums[:width], column_sums[2 * width :]]),
        out_bias_grad,
        up_bias_grad,
        down_bias_grad,
    )
    sums = [d_shift_one, d_scale_one, d_gate_one, d_shift_two, d_scale_two, d_gate_two]
    ada_width = 6 * width
    sums_all = gather_group(jnp.concatenate(sums + list(bias_grads)))
    d_group = sums_all[:, :ada_width].reshape(2, 2, 2, ada_width).sum(1).reshape(4, ada_width)
    bias_mine = []
    start = ada_width
    for grad in bias_grads:
        total = jnp.sum(sums_all[:, start : start + grad.shape[0]], axis=0)
        piece = grad.shape[0] // SHARDS
        bias_mine.append(lax.dynamic_slice_in_dim(total, place * piece, piece))
        start += grad.shape[0]
    d_silu = lax.dot_general(
        d_group,
        ada_weight.astype(jnp.float32),
        (((1,), (1,)), ((), ())),
        precision=exact_mode,
    )
    cond_mine = lax.dynamic_slice_in_dim(cond_group, place * rows, rows, 1)
    cond_part = jax.vjp(jax.nn.silu, cond_mine)[1](d_silu)[0]
    cond_all = gather_group(cond_part)
    cond_grad = lax.dynamic_index_in_dim(cond_all, fsdp_index, 1, keepdims=False)
    cond_grad = cond_grad.reshape(1, width)

    packed = jnp.concatenate(
        [d_group.reshape(-1), silu_mine.astype(jnp.float32).reshape(-1)] + bias_mine
    )
    packed_all = gather_replicas(packed, replicas)
    d_all = packed_all[:, : 4 * ada_width].reshape(-1, ada_width)
    silu_all = packed_all[:, 4 * ada_width : 4 * ada_width + 4 * rows].reshape(-1, rows)
    ada_total = lax.dot_general(
        silu_all, d_all, (((0,), (0,)), ((), ())), precision=exact_mode
    )
    ada_bias_total = jnp.sum(
        lax.dynamic_slice_in_dim(d_all, place * ada_bias.shape[0], ada_bias.shape[0], 1), axis=0
    )
    bias_totals = jnp.sum(packed_all[:, 4 * ada_width + 4 * rows :], axis=0)
    cuts = [0]
    for piece in bias_mine:
        cuts.append(cuts[-1] + piece.shape[0])
    qv_total, out_bias_total, up_bias_total, down_bias_total = (
        bias_totals[low:high] for low, high in zip(cuts[:-1], cuts[1:])
    )
    return (
        block_out,
        latent_grad,
        cond_grad,
        ada_total,
        ada_bias_total,
        qkv_total.astype(jnp.float32),
        qv_total,
        out_total.astype(jnp.float32),
        out_bias_total,
        up_total.astype(jnp.float32),
        up_bias_total,
        down_total.astype(jnp.float32),
        down_bias_total,
    )


def solution(mesh):
    tokens = P(("rep", "fsdp"), "sp", None)
    rows = P(("rep", "fsdp"), None)
    matrix = P(GROUP, None)
    vector = P(GROUP)
    weights = (matrix, vector) * 5
    return jax.shard_map(
        per_device,
        mesh=mesh,
        in_specs=(tokens, rows, P(("rep", "fsdp"))) + weights + (tokens,),
        out_specs=(tokens, tokens, rows) + weights,
        check_vma=False,
    )
```

```python
import functools

import jax
import jax.numpy as jnp
from jax import lax
from jax.experimental import pallas as pl
from jax.experimental.pallas import tpu as pltpu
from jax.sharding import PartitionSpec as P

HEAD = 72
GROUP = ("fsdp", "sp")
SHARDS = 8

exact_mode = lax.Precision.HIGHEST
epsilon = 1e-06


def normalize(values):
    average = jnp.mean(values, -1, keepdims=True)
    centered = values - average
    inverse = lax.rsqrt(jnp.mean(centered * centered, -1, keepdims=True) + epsilon)
    return (centered * inverse, inverse)


def norm_back(upstream, normed, inverse):
    return (
        upstream
        - jnp.mean(upstream, -1, keepdims=True)
        - normed * jnp.mean(upstream * normed, -1, keepdims=True)
    ) * inverse


def matmul(left, right):
    return jnp.dot(left, right, preferred_element_type=jnp.float32)


def matmul_left(left, right):
    return lax.dot_general(
        left, right, (((0,), (0,)), ((), ())), preferred_element_type=jnp.float32
    )


def matmul_right(left, right):
    return lax.dot_general(
        left, right, (((1,), (1,)), ((), ())), preferred_element_type=jnp.float32
    )


def place_of():
    return lax.axis_index("fsdp") * 2 + lax.axis_index("sp")


def pairs_by(rule):
    return [(place, rule(place)) for place in range(SHARDS)]


def swap_rule(place):
    return (place & 4) | ((place & 1) << 1) | ((place >> 1) & 1)


def core_rule(place):
    return place ^ 2


def first_rule(place):
    return place ^ (1 if place & 2 else 4)


def second_rule(place):
    return place ^ (4 if place & 2 else 1)


def permute(values, rule):
    return lax.ppermute(values, GROUP, pairs_by(rule))


def swap_halves(values):
    place = place_of()
    pairs = [pair for pair in pairs_by(swap_rule) if pair[0] != pair[1]]
    received = lax.ppermute(values, GROUP, pairs)
    stays = ((place >> 1) & 1) == (place & 1)
    return jnp.where(stays, values, received)


def gather_group(values):
    place = place_of()
    stacked = values[None]
    for bit in (1, 2, 4):
        received = permute(stacked, lambda at: at ^ bit)
        stacked = jnp.where(
            (place & bit) == 0,
            jnp.concatenate([stacked, received]),
            jnp.concatenate([received, stacked]),
        )
    return stacked


def gather_replicas(values, replicas):
    stacked = [values]
    for shift in range(1, replicas):
        pairs = [(at, (at + shift) % replicas) for at in range(replicas)]
        stacked.append(lax.ppermute(values, "rep", pairs))
    return jnp.stack(stacked)


def assemble_kernel(order_ref, *refs):
    pieces, whole, buffer, load_sems, store_sems = (
        refs[:SHARDS],
        refs[SHARDS],
        refs[SHARDS + 1],
        refs[SHARDS + 2],
        refs[SHARDS + 3],
    )
    rows = buffer.shape[1]
    loads = [
        pltpu.make_async_copy(piece, buffer.at[at], load_sems.at[at])
        for at, piece in enumerate(pieces)
    ]
    for load in loads:
        load.start()
    stores = []
    for at, load in enumerate(loads):
        load.wait()
        target = pl.ds(pl.multiple_of(order_ref[at] * rows, 16), rows)
        store = pltpu.make_async_copy(buffer.at[at], whole.at[target], store_sems.at[at])
        store.start()
        stores.append(store)
    for store in stores:
        store.wait()


def assemble(pieces, order):
    rows, columns = pieces[0].shape
    size = SHARDS * rows * columns * 2
    return pl.pallas_call(
        assemble_kernel,
        out_shape=jax.ShapeDtypeStruct((SHARDS * rows, columns), pieces[0].dtype),
        in_specs=[pl.BlockSpec(memory_space=pltpu.SMEM)]
        + [pl.BlockSpec(memory_space=pl.ANY)] * SHARDS,
        out_specs=pl.BlockSpec(memory_space=pl.ANY),
        scratch_shapes=[
            pltpu.VMEM((SHARDS, rows, columns), pieces[0].dtype),
            pltpu.SemaphoreType.DMA((SHARDS,)),
            pltpu.SemaphoreType.DMA((SHARDS,)),
        ],
        compiler_params=pltpu.CompilerParams(vmem_limit_bytes=size + (4 << 20)),
        cost_estimate=pl.CostEstimate(flops=0, bytes_accessed=2 * size, transcendentals=0),
    )(order, *pieces)


def gather_pieces(shard):
    place = place_of()
    near = jnp.where((place & 2) == 0, 4, 1)
    far = 5 - near
    other = place ^ 2
    first = permute(shard, first_rule)
    second = permute(shard, second_rule)
    both = permute(first, second_rule)
    held = [shard, first, second, both]
    pieces = held + [permute(piece, core_rule) for piece in held]
    order = [place, place ^ near, place ^ far, place ^ 5]
    order += [other, other ^ far, other ^ near, other ^ 5]
    return pieces, jnp.stack(order).astype(jnp.int32)


def tie(*values):
    return lax.optimization_barrier(values)


class Scatter:
    def __init__(self, partial):
        _, rows, columns = partial.shape
        self.place = place_of()
        self.core = (self.place >> 1) & 1
        self.partial = partial.reshape(2, 2, 2, rows, columns)
        self.received = permute(self.half(1 - self.core), core_rule)

    def half(self, core):
        return lax.dynamic_index_in_dim(self.partial, core, 1, keepdims=False)

    def second(self):
        _, _, _, rows, columns = self.partial.shape
        kept = self.half(self.core).astype(jnp.float32) + self.received.astype(jnp.float32)
        kept = kept.astype(self.partial.dtype).reshape(4, rows, columns)
        mine = ((self.place >> 2) << 1) | (self.place & 1)
        near = jnp.where(self.core == 0, 2, 1)

        def pair(which):
            parts = [which, which ^ 3 ^ near]
            return jnp.concatenate([lax.dynamic_slice_in_dim(kept, at, 1, 0) for at in parts])

        self.kept = pair(mine)
        self.received = permute(pair(mine ^ near), first_rule)

    def third(self):
        kept = self.kept.astype(jnp.float32) + self.received.astype(jnp.float32)
        self.kept = kept[0]
        self.received = permute(kept[1].astype(self.partial.dtype), second_rule)

    def result(self):
        return self.kept + self.received.astype(jnp.float32)


def reduce_replicas(partial, replicas):
    span = partial.shape[1] // replicas
    own = lax.axis_index("rep")

    def piece(values, which):
        return lax.dynamic_slice_in_dim(values, which % replicas * span, span, 1)

    low = partial.astype(jnp.bfloat16)
    total = piece(partial, own)
    for shift in range(1, replicas):
        pairs = [(at, (at + shift) % replicas) for at in range(replicas)]
        received = lax.ppermute(piece(low, own + shift), "rep", pairs)
        total = total + received.astype(jnp.float32)
    stacked = gather_replicas(total.astype(jnp.bfloat16), replicas)
    whole = jnp.zeros(partial.shape, jnp.float32)
    for shift in range(replicas):
        whole = lax.dynamic_update_slice_in_dim(
            whole, stacked[shift].astype(jnp.float32), (own - shift) % replicas * span, 1
        )
    return whole


WINDOW = 256
SHORT = pl.CostEstimate(flops=1 << 20, bytes_accessed=1 << 20, transcendentals=0)
GELU_RATE = 0.7978845608028654
GELU_CUBE = 0.044715


def head_lanes(heads, width):
    low = heads[0] * HEAD // 128 * 128
    high = -(-(heads[-1] + 1) * HEAD // 128) * 128
    return min(low, width - WINDOW), high


def head_window(first_head, width, base):
    first = (first_head + pl.program_id(0)) * HEAD
    start = jnp.minimum(first // 128 * 128, width - WINDOW)
    start = pl.multiple_of(start, 128)
    lane = lax.broadcasted_iota(jnp.int32, (1, WINDOW), 1) + start
    inside = (lane >= first) & (lane < first + HEAD)
    mask = jnp.where(inside, 1.0, 0.0).astype(jnp.bfloat16)
    lanes = [pl.ds(pl.multiple_of(start + at, 128), WINDOW) for at in (0, width, -base)]
    return (*lanes, mask)


def dot_last(left, right):
    return lax.dot_general(
        left, right, (((1,), (1,)), ((), ())), preferred_element_type=jnp.float32
    )


def dot_first(left, right):
    return lax.dot_general(
        left, right, (((0,), (0,)), ((), ())), preferred_element_type=jnp.float32
    )


def attend_kernel(first_head, base, query_ref, own_ref, other_ref, out_ref, log_ref, total_ref):
    length, width = query_ref.shape
    head = pl.program_id(0)
    key_lanes, value_lanes, out_lanes, mask = head_window(first_head, width, base)
    score_scale = float(HEAD) ** (-0.5)

    @pl.when(head == 0)
    def _():
        total_ref[...] = jnp.zeros_like(total_ref)
        log_ref[...] = jnp.zeros_like(log_ref)

    keys = jnp.concatenate([own_ref[:, key_lanes], other_ref[:, key_lanes]]) * mask
    values = jnp.concatenate([own_ref[:, value_lanes], other_ref[:, value_lanes]]) * mask
    rows = min(256, length)
    for at in range(0, length, rows):
        block = pl.ds(at, rows)
        scores = dot_last(query_ref[block, key_lanes], keys)
        row_max = jnp.max(scores, -1, keepdims=True)
        weights = jnp.exp((scores - row_max) * score_scale)
        row_total = jnp.sum(weights, -1, keepdims=True)
        probs = (weights * (1.0 / row_total)).astype(jnp.bfloat16)
        total_ref[block, out_lanes] += jnp.dot(
            probs, values, preferred_element_type=jnp.float32
        )
        log_total = row_max * score_scale + jnp.log(row_total)
        lane = lax.broadcasted_iota(jnp.int32, (rows, 128), 1)
        log_ref[block, :] = jnp.where(lane == first_head + head, log_total, log_ref[block, :])

    @pl.when(head == pl.num_programs(0) - 1)
    def _():
        out_ref[...] = total_ref[...].astype(out_ref.dtype)


def attend(query, own, other, heads):
    length, width = query.shape
    low, high = head_lanes(heads, width)
    return pl.pallas_call(
        functools.partial(attend_kernel, heads[0], low),
        grid=(len(heads),),
        out_shape=(
            jax.ShapeDtypeStruct((length, high - low), jnp.bfloat16),
            jax.ShapeDtypeStruct((length, 128), jnp.float32),
        ),
        in_specs=[
            pl.BlockSpec((length, width), lambda head: (0, 0)),
            pl.BlockSpec(own.shape, lambda head: (0, 0)),
            pl.BlockSpec(other.shape, lambda head: (0, 0)),
        ],
        out_specs=(
            pl.BlockSpec((length, high - low), lambda head: (0, 0)),
            pl.BlockSpec((length, 128), lambda head: (0, 0)),
        ),
        scratch_shapes=[pltpu.VMEM((length, high - low), jnp.float32)],
        compiler_params=pltpu.CompilerParams(vmem_limit_bytes=48 << 20),
        cost_estimate=SHORT,
    )(query, own, other)


def attend_back_kernel(
    first_head, base, query_ref, own_ref, other_ref, upstream_ref, log_ref, d_query_ref, d_own_ref, d_other_ref,
    query_total, key_total, value_total,
):
    length, width = query_ref.shape
    head = pl.program_id(0)
    key_lanes, value_lanes, out_lanes, mask = head_window(first_head, width, base)
    score_scale = float(HEAD) ** (-0.5)

    @pl.when(head == 0)
    def _():
        query_total[...] = jnp.zeros_like(query_total)
        key_total[...] = jnp.zeros_like(key_total)
        value_total[...] = jnp.zeros_like(value_total)

    keys = jnp.concatenate([own_ref[:, key_lanes], other_ref[:, key_lanes]]) * mask
    values = jnp.concatenate([own_ref[:, value_lanes], other_ref[:, value_lanes]]) * mask
    rows = min(256, length)
    for at in range(0, length, rows):
        block = pl.ds(at, rows)
        query = query_ref[block, key_lanes] * mask
        upstream = upstream_ref[block, key_lanes] * mask
        scores = dot_last(keys, query)
        probs = jnp.exp(scores * score_scale - log_ref[0, :, block])
        d_probs = dot_last(values, upstream)
        weighted = probs * d_probs
        row_sum = jnp.sum(weighted, 0, keepdims=True)
        d_scores = (weighted - probs * row_sum).astype(jnp.bfloat16)
        value_total[:, out_lanes] += jnp.dot(
            probs.astype(jnp.bfloat16), upstream, preferred_element_type=jnp.float32
        )
        key_total[:, out_lanes] += score_scale * jnp.dot(
            d_scores, query, preferred_element_type=jnp.float32
        )
        query_total[block, out_lanes] += dot_first(d_scores, keys)

    @pl.when(head == pl.num_programs(0) - 1)
    def _():
        d_query_ref[...] = (query_total[...] * score_scale).astype(d_query_ref.dtype)
        for at, total in enumerate((key_total, value_total)):
            d_own_ref[at] = total[: own_ref.shape[0]]
            d_other_ref[at] = total[own_ref.shape[0] :].astype(d_other_ref.dtype)


def attend_back(query, own, other, upstream, log_totals, heads):
    length, width = query.shape
    low, high = head_lanes(heads, width)
    span = high - low
    whole = lambda head: (0, 0)
    halves = pl.BlockSpec((2, own.shape[0], span), lambda head: (0, 0, 0))
    return pl.pallas_call(
        functools.partial(attend_back_kernel, heads[0], low),
        grid=(len(heads),),
        out_shape=(
            jax.ShapeDtypeStruct((length, span), jnp.bfloat16),
            jax.ShapeDtypeStruct((2, own.shape[0], span), jnp.float32),
            jax.ShapeDtypeStruct((2, other.shape[0], span), jnp.bfloat16),
        ),
        in_specs=[
            pl.BlockSpec((length, width), whole),
            pl.BlockSpec(own.shape, whole),
            pl.BlockSpec(other.shape, whole),
            pl.BlockSpec((length, width), whole),
            pl.BlockSpec((1, 1, length), lambda head: (heads[0] + head, 0, 0)),
        ],
        out_specs=(pl.BlockSpec((length, span), whole), halves, halves),
        scratch_shapes=[
            pltpu.VMEM((length, span), jnp.float32),
            pltpu.VMEM((own.shape[0] + other.shape[0], span), jnp.float32),
            pltpu.VMEM((own.shape[0] + other.shape[0], span), jnp.float32),
        ],
        compiler_params=pltpu.CompilerParams(vmem_limit_bytes=56 << 20),
        cost_estimate=SHORT,
    )(query, own, other, upstream, log_totals)


def join_heads(left, right, width):
    shared = left.shape[-1] + right.shape[-1] - width
    if shared == 0:
        return jnp.concatenate([left, right], axis=-1)
    edge = left.shape[-1] - shared
    middle = left[..., edge:] + right[..., :shared]
    return jnp.concatenate([left[..., :edge], middle, right[..., shared:]], axis=-1)


def mlp_kernel(
    hidden_ref, upstream_ref, up_ref, bias_ref, down_ref,
    branch_ref, d_hidden_ref, up_grad_ref, down_grad_ref, bias_grad_ref,
):
    @pl.when(pl.program_id(0) == 0)
    def _():
        branch_ref[...] = jnp.zeros_like(branch_ref)
        d_hidden_ref[...] = jnp.zeros_like(d_hidden_ref)

    hidden = hidden_ref[...]
    upstream = upstream_ref[...]
    preact = (
        jnp.dot(hidden, up_ref[...], preferred_element_type=jnp.float32) + bias_ref[...]
    )
    square = preact * preact
    bent = jnp.tanh(GELU_RATE * preact * (1.0 + GELU_CUBE * square))
    half = 0.5 * (1.0 + bent)
    slope = half + (0.5 * GELU_RATE) * preact * (1.0 - bent * bent) * (
        1.0 + (3.0 * GELU_CUBE) * square
    )
    activated = (preact * half).astype(jnp.bfloat16)
    branch_ref[...] += jnp.dot(activated, down_ref[...], preferred_element_type=jnp.float32)
    d_preact = dot_last(upstream, down_ref[...]) * slope
    d_preact = d_preact.astype(jnp.bfloat16)
    bias_grad_ref[...] = jnp.sum(d_preact.astype(jnp.float32), 0, keepdims=True)
    down_grad_ref[...] = dot_first(activated, upstream).astype(jnp.bfloat16)
    d_hidden_ref[...] += dot_last(d_preact, up_ref[...])
    up_grad_ref[...] = dot_first(hidden, d_preact).astype(jnp.bfloat16)


def mlp(hidden, upstream, up, bias, down):
    length, width = hidden.shape
    units = up.shape[1]
    block = 512
    fixed = pl.BlockSpec((length, width), lambda at: (0, 0))
    columns = pl.BlockSpec((width, block), lambda at: (0, at))
    lanes = pl.BlockSpec((1, block), lambda at: (0, at))
    rows = pl.BlockSpec((block, width), lambda at: (at, 0))
    return pl.pallas_call(
        mlp_kernel,
        grid=(units // block,),
        out_shape=(
            jax.ShapeDtypeStruct((length, width), jnp.float32),
            jax.ShapeDtypeStruct((length, width), jnp.float32),
            jax.ShapeDtypeStruct(up.shape, jnp.bfloat16),
            jax.ShapeDtypeStruct(down.shape, jnp.bfloat16),
            jax.ShapeDtypeStruct((1, units), jnp.float32),
        ),
        in_specs=[fixed, fixed, columns, lanes, rows],
        out_specs=(fixed, fixed, columns, rows, lanes),
        compiler_params=pltpu.CompilerParams(vmem_limit_bytes=56 << 20),
        cost_estimate=SHORT,
    )(hidden, upstream, up, bias, down)


def per_device(
    latent_in,
    condition,
    valid_slots,
    ada_weight,
    ada_bias,
    qkv_weight,
    qv_bias,
    out_weight,
    out_bias,
    up_weight,
    up_bias,
    down_weight,
    down_bias,
    cotangent,
):
    number, length, width = latent_in.shape
    hidden_width = up_weight.shape[1]
    place = place_of()
    fsdp_index = lax.axis_index("fsdp")
    held = (place >> 2) * 2 + (place & 1)
    rows = width // SHARDS
    replicas = lax.axis_size("rep")

    small = jnp.concatenate(
        [
            condition[0],
            qv_bias,
            out_bias,
            up_bias,
            down_bias,
            jnp.broadcast_to(valid_slots.astype(jnp.bfloat16), (128,)),
        ]
    )
    small_all = gather_group(small)
    latent_low = swap_halves(latent_in)
    qkv_pieces, order = gather_pieces(qkv_weight)
    qkv_pieces[3], up_weight, out_weight, down_weight, cotangent = tie(
        qkv_pieces[3], up_weight, out_weight, down_weight, cotangent
    )
    full_up = lax.all_gather(up_weight, GROUP, axis=0, tiled=True)
    out_pieces, _ = gather_pieces(out_weight)
    down_pieces, _ = gather_pieces(down_weight)
    cotangent_low = swap_halves(cotangent)
    full_qkv = assemble(qkv_pieces, order)

    bounds = [0, width]
    for bias in (qv_bias, out_bias, up_bias, down_bias):
        bounds.append(bounds[-1] + bias.shape[0])
    cond_group = small_all[::2, :width].astype(jnp.float32)
    full_qv_bias, full_out_bias, full_up_bias, full_down_bias = (
        small_all[:, low:high].reshape(-1).astype(jnp.float32)
        for low, high in zip(bounds[1:-1], bounds[2:])
    )
    valid_group = small_all[::2, bounds[-1]].astype(jnp.float32)
    slot_mask = lax.dynamic_slice_in_dim(valid_group, held, 1)[:, None, None]

    silu_group = jax.nn.silu(cond_group).astype(jnp.bfloat16)
    silu_mine = lax.dynamic_slice_in_dim(silu_group, place * rows, rows, 1)
    ada_bias_row = lax.dynamic_update_slice_in_dim(
        jnp.zeros((ada_weight.shape[1],), jnp.float32),
        ada_bias.astype(jnp.float32),
        place * ada_bias.shape[0],
        0,
    )
    modulation = matmul(silu_mine, ada_weight) + ada_bias_row
    for bit, count in ((4, 2), (1, 1)):
        upper = (place & bit) != 0
        sent = jnp.where(upper, modulation[:count], modulation[count:])
        kept = jnp.where(upper, modulation[count:], modulation[:count])
        modulation = kept + permute(sent, lambda at: at ^ bit)
    modulation = modulation + permute(modulation, core_rule)
    shift_one, scale_one, gate_one, shift_two, scale_two, gate_two = jnp.split(
        modulation, 6, axis=-1
    )

    latent = latent_low[0].astype(jnp.float32)
    normed_one, inverse_one = normalize(latent)
    hidden_one = (normed_one * (1.0 + scale_one) + shift_one).astype(jnp.bfloat16)
    bias_full = jnp.concatenate(
        [full_qv_bias[:width], jnp.zeros((width,), jnp.float32), full_qv_bias[width:]]
    )
    projected = (matmul(hidden_one, full_qkv) + bias_full).astype(jnp.bfloat16)
    query = projected[:, :width]
    pair_own = projected[:, width:]
    pair_other = permute(pair_own, core_rule)
    heads = range(width // HEAD)
    halves = heads[: len(heads) // 2], heads[len(heads) // 2 :]
    attended, log_totals = attend(query, pair_own, pair_other, halves[0])
    attended, query, down_pieces[1], down_pieces[2] = tie(
        attended, query, down_pieces[1], down_pieces[2]
    )
    attended_right, log_right = attend(query, pair_own, pair_other, halves[1])
    attended_low = join_heads(attended, attended_right, width)
    log_rows = (log_totals + log_right)[:, : len(heads)].T[:, None, :]
    full_out = assemble(out_pieces, order)
    branch_one = matmul(attended_low, full_out) + full_out_bias
    middle = latent + gate_one * branch_one

    normed_two, inverse_two = normalize(middle)
    hidden_two = (normed_two * (1.0 + scale_two) + shift_two).astype(jnp.bfloat16)
    full_down = assemble(down_pieces, order)
    mask_row = slot_mask[0]
    d_out = cotangent_low[0].astype(jnp.float32) * mask_row
    d_branch_two = (gate_two * d_out).astype(jnp.bfloat16)
    branch_two, d_hidden_two, up_grad, down_grad, up_bias_grad = mlp(
        hidden_two, d_branch_two, full_up, full_up_bias[None], full_down
    )
    up_scatter = Scatter(up_grad.reshape(SHARDS, rows, hidden_width))
    down_shard = lax.psum_scatter(down_grad, GROUP, scatter_dimension=0, tiled=True)
    branch_two = branch_two + full_down_bias
    block_out = (mask_row * (middle + gate_two * branch_two)).astype(jnp.bfloat16)
    block_out = swap_halves(block_out[None])
    d_gate_two = jnp.sum(d_out * branch_two, axis=0)
    down_bias_grad = jnp.sum(d_branch_two.astype(jnp.float32), axis=0)
    up_bias_grad = up_bias_grad[0]
    d_shift_two = jnp.sum(d_hidden_two, axis=0)
    d_scale_two = jnp.sum(d_hidden_two * normed_two, axis=0)
    d_middle = d_out + norm_back(d_hidden_two * (1.0 + scale_two), normed_two, inverse_two)
    d_gate_one = jnp.sum(d_middle * branch_one, axis=0)
    d_branch_one = (gate_one * d_middle).astype(jnp.bfloat16)

    out_grad = matmul_left(attended_low, d_branch_one).astype(jnp.bfloat16)
    out_scatter = Scatter(out_grad.reshape(SHARDS, rows, width))
    out_bias_grad = jnp.sum(d_branch_one.astype(jnp.float32), axis=0)
    d_attended = matmul_right(d_branch_one, full_out).astype(jnp.bfloat16)
    left = attend_back(query, pair_own, pair_other, d_attended, log_rows, halves[0])
    d_query, d_attended, up_scatter.received, out_scatter.received = tie(
        left[0], d_attended, up_scatter.received, out_scatter.received
    )
    up_scatter.second()
    out_scatter.second()
    right = attend_back(query, pair_own, pair_other, d_attended, log_rows, halves[1])
    d_query = join_heads(d_query, right[0], width)
    d_own = join_heads(left[1], right[1], width)
    d_other = permute(join_heads(left[2], right[2], width), core_rule)
    d_own = (d_own + d_other.astype(jnp.float32)).astype(jnp.bfloat16)
    d_projected = jnp.concatenate([d_query, d_own[0], d_own[1]], axis=-1)

    qkv_grad = matmul_left(hidden_one, d_projected).astype(jnp.bfloat16)
    qkv_scatter = Scatter(qkv_grad.reshape(SHARDS, rows, 3 * width))
    column_sums = jnp.sum(d_projected.astype(jnp.float32), axis=0)
    d_hidden_one = matmul_right(d_projected, full_qkv)
    d_hidden_one, up_scatter.received, out_scatter.received, qkv_scatter.received = tie(
        d_hidden_one, up_scatter.received, out_scatter.received, qkv_scatter.received
    )
    up_scatter.third()
    out_scatter.third()
    qkv_scatter.second()
    d_shift_one = jnp.sum(d_hidden_one, axis=0)
    d_scale_one = jnp.sum(d_hidden_one * normed_one, axis=0)
    latent_grad = d_middle + norm_back(d_hidden_one * (1.0 + scale_one), normed_one, inverse_one)
    latent_grad = swap_halves(latent_grad.astype(jnp.bfloat16)[None]).astype(jnp.float32)

    down_total = lax.psum(down_shard, "rep")
    up_shard, down_total = tie(up_scatter.result().astype(jnp.bfloat16), down_total)
    up_total = lax.psum(up_shard, "rep")
    qkv_scatter.third()
    late = jnp.concatenate([out_scatter.result(), qkv_scatter.result()], axis=1)
    late_total = reduce_replicas(late, replicas)
    out_total, qkv_total = late_total[:, :width], late_total[:, width:]

    bias_grads = (
        jnp.concatenate([column_sums[:width], column_sums[2 * width :]]),
        out_bias_grad,
        up_bias_grad,
        down_bias_grad,
    )
    sums = [d_shift_one, d_scale_one, d_gate_one, d_shift_two, d_scale_two, d_gate_two]
    ada_width = 6 * width
    sums_all = gather_group(jnp.concatenate(sums + list(bias_grads)))
    d_group = sums_all[:, :ada_width].reshape(2, 2, 2, ada_width).sum(1).reshape(4, ada_width)
    bias_mine = []
    start = ada_width
    for grad in bias_grads:
        total = jnp.sum(sums_all[:, start : start + grad.shape[0]], axis=0)
        piece = grad.shape[0] // SHARDS
        bias_mine.append(lax.dynamic_slice_in_dim(total, place * piece, piece))
        start += grad.shape[0]
    d_silu = lax.dot_general(
        d_group,
        ada_weight.astype(jnp.float32),
        (((1,), (1,)), ((), ())),
        precision=exact_mode,
    )
    cond_mine = lax.dynamic_slice_in_dim(cond_group, place * rows, rows, 1)
    cond_part = jax.vjp(jax.nn.silu, cond_mine)[1](d_silu)[0]
    cond_all = gather_group(cond_part)
    cond_grad = lax.dynamic_index_in_dim(cond_all, fsdp_index, 1, keepdims=False)
    cond_grad = cond_grad.reshape(1, width)

    packed = jnp.concatenate(
        [d_group.reshape(-1), silu_mine.astype(jnp.float32).reshape(-1)] + bias_mine
    )
    packed_all = gather_replicas(packed, replicas)
    d_all = packed_all[:, : 4 * ada_width].reshape(-1, ada_width)
    silu_all = packed_all[:, 4 * ada_width : 4 * ada_width + 4 * rows].reshape(-1, rows)
    ada_total = lax.dot_general(
        silu_all, d_all, (((0,), (0,)), ((), ())), precision=exact_mode
    )
    ada_bias_total = jnp.sum(
        lax.dynamic_slice_in_dim(d_all, place * ada_bias.shape[0], ada_bias.shape[0], 1), axis=0
    )
    bias_totals = jnp.sum(packed_all[:, 4 * ada_width + 4 * rows :], axis=0)
    cuts = [0]
    for piece in bias_mine:
        cuts.append(cuts[-1] + piece.shape[0])
    qv_total, out_bias_total, up_bias_total, down_bias_total = (
        bias_totals[low:high] for low, high in zip(cuts[:-1], cuts[1:])
    )
    return (
        block_out,
        latent_grad,
        cond_grad,
        ada_total,
        ada_bias_total,
        qkv_total.astype(jnp.float32),
        qv_total,
        out_total.astype(jnp.float32),
        out_bias_total,
        up_total.astype(jnp.float32),
        up_bias_total,
        down_total.astype(jnp.float32),
        down_bias_total,
    )


def solution(mesh):
    tokens = P(("rep", "fsdp"), "sp", None)
    rows = P(("rep", "fsdp"), None)
    matrix = P(GROUP, None)
    vector = P(GROUP)
    weights = (matrix, vector) * 5
    return jax.shard_map(
        per_device,
        mesh=mesh,
        in_specs=(tokens, rows, P(("rep", "fsdp"))) + weights + (tokens,),
        out_specs=(tokens, tokens, rows) + weights,
        check_vma=False,
    )
```

```python
import functools

import jax
import jax.numpy as jnp
from jax import lax
from jax.experimental import pallas as pl
from jax.experimental.pallas import tpu as pltpu
from jax.sharding import PartitionSpec as P

HEAD = 72
GROUP = ("fsdp", "sp")
SHARDS = 8

exact_mode = lax.Precision.HIGHEST
epsilon = 1e-06


def normalize(values):
    average = jnp.mean(values, -1, keepdims=True)
    centered = values - average
    inverse = lax.rsqrt(jnp.mean(centered * centered, -1, keepdims=True) + epsilon)
    return (centered * inverse, inverse)


def norm_back(upstream, normed, inverse):
    return (
        upstream
        - jnp.mean(upstream, -1, keepdims=True)
        - normed * jnp.mean(upstream * normed, -1, keepdims=True)
    ) * inverse


def matmul(left, right):
    return jnp.dot(left, right, preferred_element_type=jnp.float32)


def place_of():
    return lax.axis_index("fsdp") * 2 + lax.axis_index("sp")


def pairs_by(rule):
    return [(place, rule(place)) for place in range(SHARDS)]


def swap_rule(place):
    return (place & 4) | ((place & 1) << 1) | ((place >> 1) & 1)


def core_rule(place):
    return place ^ 2


def first_rule(place):
    return place ^ (1 if place & 2 else 4)


def second_rule(place):
    return place ^ (4 if place & 2 else 1)


def permute(values, rule):
    return lax.ppermute(values, GROUP, pairs_by(rule))


def swap_halves(values):
    place = place_of()
    pairs = [pair for pair in pairs_by(swap_rule) if pair[0] != pair[1]]
    received = lax.ppermute(values, GROUP, pairs)
    stays = ((place >> 1) & 1) == (place & 1)
    return jnp.where(stays, values, received)


def gather_group(values):
    place = place_of()
    stacked = values[None]
    for bit in (1, 2, 4):
        received = permute(stacked, lambda at: at ^ bit)
        stacked = jnp.where(
            (place & bit) == 0,
            jnp.concatenate([stacked, received]),
            jnp.concatenate([received, stacked]),
        )
    return stacked


def gather_replicas(values, replicas):
    stacked = [values]
    for shift in range(1, replicas):
        pairs = [(at, (at + shift) % replicas) for at in range(replicas)]
        stacked.append(lax.ppermute(values, "rep", pairs))
    return jnp.stack(stacked)


def assemble_kernel(order_ref, *refs):
    pieces, whole, buffer, load_sems, store_sems = (
        refs[:SHARDS],
        refs[SHARDS],
        refs[SHARDS + 1],
        refs[SHARDS + 2],
        refs[SHARDS + 3],
    )
    rows = buffer.shape[1]
    loads = [
        pltpu.make_async_copy(piece, buffer.at[at], load_sems.at[at])
        for at, piece in enumerate(pieces)
    ]
    for load in loads:
        load.start()
    stores = []
    for at, load in enumerate(loads):
        load.wait()
        target = pl.ds(pl.multiple_of(order_ref[at] * rows, 16), rows)
        store = pltpu.make_async_copy(buffer.at[at], whole.at[target], store_sems.at[at])
        store.start()
        stores.append(store)
    for store in stores:
        store.wait()


def assemble(pieces, order):
    rows, columns = pieces[0].shape
    size = SHARDS * rows * columns * 2
    return pl.pallas_call(
        assemble_kernel,
        out_shape=jax.ShapeDtypeStruct((SHARDS * rows, columns), pieces[0].dtype),
        in_specs=[pl.BlockSpec(memory_space=pltpu.SMEM)]
        + [pl.BlockSpec(memory_space=pl.ANY)] * SHARDS,
        out_specs=pl.BlockSpec(memory_space=pl.ANY),
        scratch_shapes=[
            pltpu.VMEM((SHARDS, rows, columns), pieces[0].dtype),
            pltpu.SemaphoreType.DMA((SHARDS,)),
            pltpu.SemaphoreType.DMA((SHARDS,)),
        ],
        compiler_params=pltpu.CompilerParams(vmem_limit_bytes=size + (4 << 20)),
        cost_estimate=SHORT,
    )(order, *pieces)


def gather_pieces(shard):
    place = place_of()
    near = jnp.where((place & 2) == 0, 4, 1)
    far = 5 - near
    other = place ^ 2
    first = permute(shard, first_rule)
    second = permute(shard, second_rule)
    both = permute(first, second_rule)
    held = [shard, first, second, both]
    pieces = held + [permute(piece, core_rule) for piece in held]
    order = [place, place ^ near, place ^ far, place ^ 5]
    order += [other, other ^ far, other ^ near, other ^ 5]
    return pieces, jnp.stack(order).astype(jnp.int32)


def tie(*values):
    return lax.optimization_barrier(values)


class Scatter:
    def __init__(self, halves):
        self.place = place_of()
        self.core = (self.place >> 1) & 1
        self.kept, sent = halves
        self.low = sent.dtype
        self.received = permute(sent, core_rule)

    def second(self):
        kept = self.kept.astype(jnp.float32) + self.received.astype(jnp.float32)
        kept = kept.astype(self.low)
        mine = ((self.place >> 2) << 1) | (self.place & 1)
        near = jnp.where(self.core == 0, 2, 1)

        def pair(which):
            parts = [which, which ^ 3 ^ near]
            return jnp.concatenate([lax.dynamic_slice_in_dim(kept, at, 1, 0) for at in parts])

        self.kept = pair(mine)
        self.received = permute(pair(mine ^ near), first_rule)

    def third(self):
        kept = self.kept.astype(jnp.float32) + self.received.astype(jnp.float32)
        self.kept = kept[0]
        self.received = permute(kept[1].astype(self.low), second_rule)

    def result(self):
        return self.kept + self.received.astype(jnp.float32)


def reduce_replicas(partial, replicas):
    span = partial.shape[1] // replicas
    own = lax.axis_index("rep")

    def piece(values, which):
        return lax.dynamic_slice_in_dim(values, which % replicas * span, span, 1)

    low = partial.astype(jnp.bfloat16)
    total = piece(partial, own)
    for shift in range(1, replicas):
        pairs = [(at, (at + shift) % replicas) for at in range(replicas)]
        received = lax.ppermute(piece(low, own + shift), "rep", pairs)
        total = total + received.astype(jnp.float32)
    stacked = gather_replicas(total.astype(jnp.bfloat16), replicas)
    whole = jnp.zeros(partial.shape, jnp.float32)
    for shift in range(replicas):
        whole = lax.dynamic_update_slice_in_dim(
            whole, stacked[shift].astype(jnp.float32), (own - shift) % replicas * span, 1
        )
    return whole


WINDOW = 256
GELU_RATE = 0.7978845608028654
GELU_CUBE = 0.044715
SHORT = pl.CostEstimate(flops=1 << 20, bytes_accessed=1 << 20, transcendentals=0)


def head_lanes(heads, width):
    low = heads[0] * HEAD // 128 * 128
    high = -(-(heads[-1] + 1) * HEAD // 128) * 128
    return min(low, width - WINDOW), high


def head_window(first_head, width, base):
    first = (first_head + pl.program_id(0)) * HEAD
    start = jnp.minimum(first // 128 * 128, width - WINDOW)
    start = pl.multiple_of(start, 128)
    lane = lax.broadcasted_iota(jnp.int32, (1, WINDOW), 1) + start
    inside = (lane >= first) & (lane < first + HEAD)
    mask = jnp.where(inside, 1.0, 0.0).astype(jnp.bfloat16)
    lanes = [pl.ds(pl.multiple_of(start + at, 128), WINDOW) for at in (0, width, -base)]
    return (*lanes, mask)


def dot_last(left, right):
    return lax.dot_general(
        left, right, (((1,), (1,)), ((), ())), preferred_element_type=jnp.float32
    )


def dot_first(left, right):
    return lax.dot_general(
        left, right, (((0,), (0,)), ((), ())), preferred_element_type=jnp.float32
    )


def attend_kernel(first_head, base, query_ref, own_ref, other_ref, out_ref, log_ref, total_ref):
    length, width = query_ref.shape
    head = pl.program_id(0)
    key_lanes, value_lanes, out_lanes, mask = head_window(first_head, width, base)
    score_scale = float(HEAD) ** (-0.5)

    @pl.when(head == 0)
    def _():
        total_ref[...] = jnp.zeros_like(total_ref)
        log_ref[...] = jnp.zeros_like(log_ref)

    keys = jnp.concatenate([own_ref[:, key_lanes], other_ref[:, key_lanes]]) * mask
    values = jnp.concatenate([own_ref[:, value_lanes], other_ref[:, value_lanes]]) * mask
    rows = min(256, length)
    for at in range(0, length, rows):
        block = pl.ds(at, rows)
        scores = dot_last(query_ref[block, key_lanes], keys)
        row_max = jnp.max(scores, -1, keepdims=True)
        weights = jnp.exp((scores - row_max) * score_scale)
        row_total = jnp.sum(weights, -1, keepdims=True)
        probs = (weights * (1.0 / row_total)).astype(jnp.bfloat16)
        total_ref[block, out_lanes] += jnp.dot(
            probs, values, preferred_element_type=jnp.float32
        )
        log_total = row_max * score_scale + jnp.log(row_total)
        lane = lax.broadcasted_iota(jnp.int32, (rows, 128), 1)
        log_ref[block, :] = jnp.where(lane == first_head + head, log_total, log_ref[block, :])

    @pl.when(head == pl.num_programs(0) - 1)
    def _():
        out_ref[...] = total_ref[...].astype(out_ref.dtype)


def attend(query, own, other, heads):
    length, width = query.shape
    low, high = head_lanes(heads, width)
    return pl.pallas_call(
        functools.partial(attend_kernel, heads[0], low),
        grid=(len(heads),),
        out_shape=(
            jax.ShapeDtypeStruct((length, high - low), jnp.bfloat16),
            jax.ShapeDtypeStruct((length, 128), jnp.float32),
        ),
        in_specs=[
            pl.BlockSpec((length, width), lambda head: (0, 0)),
            pl.BlockSpec(own.shape, lambda head: (0, 0)),
            pl.BlockSpec(other.shape, lambda head: (0, 0)),
        ],
        out_specs=(
            pl.BlockSpec((length, high - low), lambda head: (0, 0)),
            pl.BlockSpec((length, 128), lambda head: (0, 0)),
        ),
        scratch_shapes=[pltpu.VMEM((length, high - low), jnp.float32)],
        compiler_params=pltpu.CompilerParams(vmem_limit_bytes=48 << 20),
        cost_estimate=SHORT,
    )(query, own, other)


def attend_back_kernel(
    first_head, base, query_ref, own_ref, other_ref, upstream_ref, log_ref, d_query_ref, d_own_ref, d_other_ref,
    query_total, key_total, value_total,
):
    length, width = query_ref.shape
    head = pl.program_id(0)
    key_lanes, value_lanes, out_lanes, mask = head_window(first_head, width, base)
    score_scale = float(HEAD) ** (-0.5)

    @pl.when(head == 0)
    def _():
        query_total[...] = jnp.zeros_like(query_total)
        key_total[...] = jnp.zeros_like(key_total)
        value_total[...] = jnp.zeros_like(value_total)

    keys = jnp.concatenate([own_ref[:, key_lanes], other_ref[:, key_lanes]]) * mask
    values = jnp.concatenate([own_ref[:, value_lanes], other_ref[:, value_lanes]]) * mask
    rows = min(256, length)
    for at in range(0, length, rows):
        block = pl.ds(at, rows)
        query = query_ref[block, key_lanes] * mask
        upstream = upstream_ref[block, key_lanes] * mask
        scores = dot_last(keys, query)
        probs = jnp.exp(scores * score_scale - log_ref[0, :, block])
        d_probs = dot_last(values, upstream)
        weighted = probs * d_probs
        row_sum = jnp.sum(weighted, 0, keepdims=True)
        d_scores = (weighted - probs * row_sum).astype(jnp.bfloat16)
        value_total[:, out_lanes] += jnp.dot(
            probs.astype(jnp.bfloat16), upstream, preferred_element_type=jnp.float32
        )
        key_total[:, out_lanes] += score_scale * jnp.dot(
            d_scores, query, preferred_element_type=jnp.float32
        )
        query_total[block, out_lanes] += dot_first(d_scores, keys)

    @pl.when(head == pl.num_programs(0) - 1)
    def _():
        d_query_ref[...] = (query_total[...] * score_scale).astype(d_query_ref.dtype)
        for at, total in enumerate((key_total, value_total)):
            d_own_ref[at] = total[: own_ref.shape[0]]
            d_other_ref[at] = total[own_ref.shape[0] :].astype(d_other_ref.dtype)


def attend_back(query, own, other, upstream, log_totals, heads):
    length, width = query.shape
    low, high = head_lanes(heads, width)
    span = high - low
    whole = lambda head: (0, 0)
    halves = pl.BlockSpec((2, own.shape[0], span), lambda head: (0, 0, 0))
    return pl.pallas_call(
        functools.partial(attend_back_kernel, heads[0], low),
        grid=(len(heads),),
        out_shape=(
            jax.ShapeDtypeStruct((length, span), jnp.bfloat16),
            jax.ShapeDtypeStruct((2, own.shape[0], span), jnp.float32),
            jax.ShapeDtypeStruct((2, other.shape[0], span), jnp.bfloat16),
        ),
        in_specs=[
            pl.BlockSpec((length, width), whole),
            pl.BlockSpec(own.shape, whole),
            pl.BlockSpec(other.shape, whole),
            pl.BlockSpec((length, width), whole),
            pl.BlockSpec((1, 1, length), lambda head: (heads[0] + head, 0, 0)),
        ],
        out_specs=(pl.BlockSpec((length, span), whole), halves, halves),
        scratch_shapes=[
            pltpu.VMEM((length, span), jnp.float32),
            pltpu.VMEM((own.shape[0] + other.shape[0], span), jnp.float32),
            pltpu.VMEM((own.shape[0] + other.shape[0], span), jnp.float32),
        ],
        compiler_params=pltpu.CompilerParams(vmem_limit_bytes=56 << 20),
        cost_estimate=SHORT,
    )(query, own, other, upstream, log_totals)


def join_heads(left, right, width):
    shared = left.shape[-1] + right.shape[-1] - width
    if shared == 0:
        return jnp.concatenate([left, right], axis=-1)
    edge = left.shape[-1] - shared
    middle = left[..., edge:] + right[..., :shared]
    return jnp.concatenate([left[..., :edge], middle, right[..., shared:]], axis=-1)


def store_halves(grad, kept_ref, sent_ref):
    core = lax.axis_index("fsdp") % 2
    rows = grad.shape[0] // SHARDS
    low = grad.astype(kept_ref.dtype)
    for owner in (0, 1):
        blocks = [at for at in range(SHARDS) if (at >> 1) & 1 == owner]

        @pl.when(core == owner)
        def _():
            for slot, at in enumerate(blocks):
                kept_ref[slot] = low[at * rows : (at + 1) * rows]

        @pl.when(core != owner)
        def _():
            for slot, at in enumerate(blocks):
                sent_ref[slot] = low[at * rows : (at + 1) * rows]


def product_back_kernel(left_ref, upstream_ref, weight_ref, d_left_ref, kept_ref, sent_ref):
    @pl.when(pl.program_id(0) == 0)
    def _():
        d_left_ref[...] = jnp.zeros_like(d_left_ref)

    upstream = upstream_ref[...]
    store_halves(dot_first(left_ref[...], upstream), kept_ref, sent_ref)
    d_left_ref[...] += dot_last(upstream, weight_ref[...])


def product_back(left, upstream, weight):
    length, width = left.shape
    columns = weight.shape[1]
    block = 384
    fixed = pl.BlockSpec((length, width), lambda at: (0, 0))
    half = pl.BlockSpec((SHARDS // 2, width // SHARDS, block), lambda at: (0, 0, at))
    half_shape = jax.ShapeDtypeStruct((SHARDS // 2, width // SHARDS, columns), jnp.bfloat16)
    d_left, kept, sent = pl.pallas_call(
        product_back_kernel,
        grid=(columns // block,),
        out_shape=(
            jax.ShapeDtypeStruct((length, width), jnp.float32),
            half_shape,
            half_shape,
        ),
        in_specs=[
            fixed,
            pl.BlockSpec((length, block), lambda at: (0, at)),
            pl.BlockSpec((width, block), lambda at: (0, at)),
        ],
        out_specs=(fixed, half, half),
        compiler_params=pltpu.CompilerParams(vmem_limit_bytes=32 << 20),
        cost_estimate=SHORT,
    )(left, upstream, weight)
    return d_left, (kept, sent)


def mlp_kernel(
    hidden_ref, upstream_ref, up_ref, bias_ref, down_ref,
    branch_ref, d_hidden_ref, up_kept_ref, up_sent_ref, down_grad_ref, bias_grad_ref,
):
    @pl.when(pl.program_id(0) == 0)
    def _():
        branch_ref[...] = jnp.zeros_like(branch_ref)
        d_hidden_ref[...] = jnp.zeros_like(d_hidden_ref)

    hidden = hidden_ref[...]
    upstream = upstream_ref[...]
    preact = (
        jnp.dot(hidden, up_ref[...], preferred_element_type=jnp.float32) + bias_ref[...]
    )
    square = preact * preact
    bent = jnp.tanh(GELU_RATE * preact * (1.0 + GELU_CUBE * square))
    half = 0.5 * (1.0 + bent)
    slope = half + (0.5 * GELU_RATE) * preact * (1.0 - bent * bent) * (
        1.0 + (3.0 * GELU_CUBE) * square
    )
    activated = (preact * half).astype(jnp.bfloat16)
    branch_ref[...] += jnp.dot(activated, down_ref[...], preferred_element_type=jnp.float32)
    d_preact = dot_last(upstream, down_ref[...]) * slope
    d_preact = d_preact.astype(jnp.bfloat16)
    bias_grad_ref[...] = jnp.sum(d_preact.astype(jnp.float32), 0, keepdims=True)
    down_grad_ref[...] = dot_first(activated, upstream).astype(jnp.bfloat16)
    d_hidden_ref[...] += dot_last(d_preact, up_ref[...])
    store_halves(dot_first(hidden, d_preact), up_kept_ref, up_sent_ref)


def mlp(hidden, upstream, up, bias, down):
    length, width = hidden.shape
    units = up.shape[1]
    block = 512
    fixed = pl.BlockSpec((length, width), lambda at: (0, 0))
    columns = pl.BlockSpec((width, block), lambda at: (0, at))
    lanes = pl.BlockSpec((1, block), lambda at: (0, at))
    rows = pl.BlockSpec((block, width), lambda at: (at, 0))
    half = pl.BlockSpec((SHARDS // 2, width // SHARDS, block), lambda at: (0, 0, at))
    half_shape = jax.ShapeDtypeStruct((SHARDS // 2, width // SHARDS, units), jnp.bfloat16)
    return pl.pallas_call(
        mlp_kernel,
        grid=(units // block,),
        out_shape=(
            jax.ShapeDtypeStruct((length, width), jnp.float32),
            jax.ShapeDtypeStruct((length, width), jnp.float32),
            half_shape,
            half_shape,
            jax.ShapeDtypeStruct(down.shape, jnp.bfloat16),
            jax.ShapeDtypeStruct((1, units), jnp.float32),
        ),
        in_specs=[fixed, fixed, columns, lanes, rows],
        out_specs=(fixed, fixed, half, half, rows, lanes),
        compiler_params=pltpu.CompilerParams(vmem_limit_bytes=56 << 20),
        cost_estimate=SHORT,
    )(hidden, upstream, up, bias, down)


def per_device(
    latent_in,
    condition,
    valid_slots,
    ada_weight,
    ada_bias,
    qkv_weight,
    qv_bias,
    out_weight,
    out_bias,
    up_weight,
    up_bias,
    down_weight,
    down_bias,
    cotangent,
):
    number, length, width = latent_in.shape
    place = place_of()
    fsdp_index = lax.axis_index("fsdp")
    held = (place >> 2) * 2 + (place & 1)
    rows = width // SHARDS
    replicas = lax.axis_size("rep")

    small = jnp.concatenate(
        [
            condition[0],
            qv_bias,
            out_bias,
            up_bias,
            down_bias,
            jnp.broadcast_to(valid_slots.astype(jnp.bfloat16), (128,)),
        ]
    )
    small_all = gather_group(small)
    latent_low = swap_halves(latent_in)
    qkv_pieces, order = gather_pieces(qkv_weight)
    full_up = lax.all_gather(up_weight, GROUP, axis=0, tiled=True)
    out_pieces, _ = gather_pieces(out_weight)
    cotangent_low = swap_halves(cotangent)
    full_qkv = assemble(qkv_pieces, order)
    full_down = lax.all_gather(down_weight, GROUP, axis=0, tiled=True)

    bounds = [0, width]
    for bias in (qv_bias, out_bias, up_bias, down_bias):
        bounds.append(bounds[-1] + bias.shape[0])
    cond_group = small_all[::2, :width].astype(jnp.float32)
    full_qv_bias, full_out_bias, full_up_bias, full_down_bias = (
        small_all[:, low:high].reshape(-1).astype(jnp.float32)
        for low, high in zip(bounds[1:-1], bounds[2:])
    )
    valid_group = small_all[::2, bounds[-1]].astype(jnp.float32)
    slot_mask = lax.dynamic_slice_in_dim(valid_group, held, 1)[:, None, None]

    silu_group = jax.nn.silu(cond_group).astype(jnp.bfloat16)
    silu_mine = lax.dynamic_slice_in_dim(silu_group, place * rows, rows, 1)
    ada_bias_row = lax.dynamic_update_slice_in_dim(
        jnp.zeros((ada_weight.shape[1],), jnp.float32),
        ada_bias.astype(jnp.float32),
        place * ada_bias.shape[0],
        0,
    )
    modulation = matmul(silu_mine, ada_weight) + ada_bias_row
    for bit, count in ((4, 2), (1, 1)):
        upper = (place & bit) != 0
        sent = jnp.where(upper, modulation[:count], modulation[count:])
        kept = jnp.where(upper, modulation[count:], modulation[:count])
        modulation = kept + permute(sent, lambda at: at ^ bit)
    modulation = modulation + permute(modulation, core_rule)
    shift_one, scale_one, gate_one, shift_two, scale_two, gate_two = jnp.split(
        modulation, 6, axis=-1
    )

    latent = latent_low[0].astype(jnp.float32)
    normed_one, inverse_one = normalize(latent)
    hidden_one = (normed_one * (1.0 + scale_one) + shift_one).astype(jnp.bfloat16)
    bias_full = jnp.concatenate(
        [full_qv_bias[:width], jnp.zeros((width,), jnp.float32), full_qv_bias[width:]]
    )
    projected = (matmul(hidden_one, full_qkv) + bias_full).astype(jnp.bfloat16)
    query = projected[:, :width]
    pair_own = projected[:, width:]
    pair_other = permute(pair_own, core_rule)
    heads = range(width // HEAD)
    halves = heads[: len(heads) // 2], heads[len(heads) // 2 :]
    attended_low, log_totals = attend(query, pair_own, pair_other, heads)
    log_rows = log_totals[:, : len(heads)].T[:, None, :]
    full_out = assemble(out_pieces, order)
    branch_one = matmul(attended_low, full_out) + full_out_bias
    middle = latent + gate_one * branch_one

    normed_two, inverse_two = normalize(middle)
    hidden_two = (normed_two * (1.0 + scale_two) + shift_two).astype(jnp.bfloat16)
    mask_row = slot_mask[0]
    d_out = cotangent_low[0].astype(jnp.float32) * mask_row
    d_branch_two = (gate_two * d_out).astype(jnp.bfloat16)
    branch_two, d_hidden_two, up_kept, up_sent, down_grad, up_bias_grad = mlp(
        hidden_two, d_branch_two, full_up, full_up_bias[None], full_down
    )
    up_scatter = Scatter((up_kept, up_sent))
    down_shard = lax.psum_scatter(down_grad, GROUP, scatter_dimension=0, tiled=True)
    branch_two = branch_two + full_down_bias
    block_out = (mask_row * (middle + gate_two * branch_two)).astype(jnp.bfloat16)
    block_out = swap_halves(block_out[None])
    d_gate_two = jnp.sum(d_out * branch_two, axis=0)
    down_bias_grad = jnp.sum(d_branch_two.astype(jnp.float32), axis=0)
    up_bias_grad = up_bias_grad[0]
    d_shift_two = jnp.sum(d_hidden_two, axis=0)
    d_scale_two = jnp.sum(d_hidden_two * normed_two, axis=0)
    d_middle = d_out + norm_back(d_hidden_two * (1.0 + scale_two), normed_two, inverse_two)
    d_gate_one = jnp.sum(d_middle * branch_one, axis=0)
    d_branch_one = (gate_one * d_middle).astype(jnp.bfloat16)

    d_attended, out_halves = product_back(attended_low, d_branch_one, full_out)
    d_attended = d_attended.astype(jnp.bfloat16)
    out_scatter = Scatter(out_halves)
    out_bias_grad = jnp.sum(d_branch_one.astype(jnp.float32), axis=0)
    left = attend_back(query, pair_own, pair_other, d_attended, log_rows, halves[0])
    d_query, d_attended, up_scatter.received, out_scatter.received = tie(
        left[0], d_attended, up_scatter.received, out_scatter.received
    )
    up_scatter.second()
    out_scatter.second()
    right = attend_back(query, pair_own, pair_other, d_attended, log_rows, halves[1])
    d_query = join_heads(d_query, right[0], width)
    d_own = join_heads(left[1], right[1], width)
    d_other = permute(join_heads(left[2], right[2], width), core_rule)
    d_own = (d_own + d_other.astype(jnp.float32)).astype(jnp.bfloat16)
    d_projected = jnp.concatenate([d_query, d_own[0], d_own[1]], axis=-1)

    d_projected, up_scatter.received = tie(d_projected, up_scatter.received)
    d_hidden_one, qkv_halves = product_back(hidden_one, d_projected, full_qkv)
    qkv_scatter = Scatter(qkv_halves)
    column_sums = jnp.sum(d_projected.astype(jnp.float32), axis=0)
    d_hidden_one, out_scatter.received, down_shard = tie(
        d_hidden_one, out_scatter.received, down_shard
    )
    up_scatter.third()
    out_scatter.third()
    qkv_scatter.second()
    d_shift_one = jnp.sum(d_hidden_one, axis=0)
    d_scale_one = jnp.sum(d_hidden_one * normed_one, axis=0)
    latent_grad = d_middle + norm_back(d_hidden_one * (1.0 + scale_one), normed_one, inverse_one)
    latent_grad = swap_halves(latent_grad.astype(jnp.bfloat16)[None]).astype(jnp.float32)

    down_total = lax.psum(down_shard, "rep")
    qkv_scatter.third()
    up_shard, down_total, qkv_scatter.received = tie(
        up_scatter.result().astype(jnp.bfloat16), down_total, qkv_scatter.received
    )
    up_total = lax.psum(up_shard, "rep")
    late = jnp.concatenate([out_scatter.result(), qkv_scatter.result()], axis=1)
    late_total = reduce_replicas(late, replicas)
    out_total, qkv_total = late_total[:, :width], late_total[:, width:]

    bias_grads = (
        jnp.concatenate([column_sums[:width], column_sums[2 * width :]]),
        out_bias_grad,
        up_bias_grad,
        down_bias_grad,
    )
    sums = [d_shift_one, d_scale_one, d_gate_one, d_shift_two, d_scale_two, d_gate_two]
    ada_width = 6 * width
    sums_all = gather_group(jnp.concatenate(sums + list(bias_grads)))
    d_group = sums_all[:, :ada_width].reshape(2, 2, 2, ada_width).sum(1).reshape(4, ada_width)
    bias_mine = []
    start = ada_width
    for grad in bias_grads:
        total = jnp.sum(sums_all[:, start : start + grad.shape[0]], axis=0)
        piece = grad.shape[0] // SHARDS
        bias_mine.append(lax.dynamic_slice_in_dim(total, place * piece, piece))
        start += grad.shape[0]
    d_silu = lax.dot_general(
        d_group,
        ada_weight.astype(jnp.float32),
        (((1,), (1,)), ((), ())),
        precision=exact_mode,
    )
    cond_mine = lax.dynamic_slice_in_dim(cond_group, place * rows, rows, 1)
    cond_part = jax.vjp(jax.nn.silu, cond_mine)[1](d_silu)[0]
    cond_all = gather_group(cond_part)
    cond_grad = lax.dynamic_index_in_dim(cond_all, fsdp_index, 1, keepdims=False)
    cond_grad = cond_grad.reshape(1, width)

    packed = jnp.concatenate(
        [d_group.reshape(-1), silu_mine.astype(jnp.float32).reshape(-1)] + bias_mine
    )
    packed_all = gather_replicas(packed, replicas)
    d_all = packed_all[:, : 4 * ada_width].reshape(-1, ada_width)
    silu_all = packed_all[:, 4 * ada_width : 4 * ada_width + 4 * rows].reshape(-1, rows)
    ada_total = lax.dot_general(
        silu_all, d_all, (((0,), (0,)), ((), ())), precision=exact_mode
    )
    ada_bias_total = jnp.sum(
        lax.dynamic_slice_in_dim(d_all, place * ada_bias.shape[0], ada_bias.shape[0], 1), axis=0
    )
    bias_totals = jnp.sum(packed_all[:, 4 * ada_width + 4 * rows :], axis=0)
    cuts = [0]
    for piece in bias_mine:
        cuts.append(cuts[-1] + piece.shape[0])
    qv_total, out_bias_total, up_bias_total, down_bias_total = (
        bias_totals[low:high] for low, high in zip(cuts[:-1], cuts[1:])
    )
    return (
        block_out,
        latent_grad,
        cond_grad,
        ada_total,
        ada_bias_total,
        qkv_total.astype(jnp.float32),
        qv_total,
        out_total.astype(jnp.float32),
        out_bias_total,
        up_total.astype(jnp.float32),
        up_bias_total,
        down_total.astype(jnp.float32),
        down_bias_total,
    )


def solution(mesh):
    tokens = P(("rep", "fsdp"), "sp", None)
    rows = P(("rep", "fsdp"), None)
    matrix = P(GROUP, None)
    vector = P(GROUP)
    weights = (matrix, vector) * 5
    return jax.shard_map(
        per_device,
        mesh=mesh,
        in_specs=(tokens, rows, P(("rep", "fsdp"))) + weights + (tokens,),
        out_specs=(tokens, tokens, rows) + weights,
        check_vma=False,
    )
```

```python
import functools

import jax
import jax.numpy as jnp
from jax import lax
from jax.experimental import pallas as pl
from jax.experimental.pallas import tpu as pltpu
from jax.sharding import PartitionSpec as P

HEAD = 72
GROUP = ("fsdp", "sp")
SHARDS = 8

exact_mode = lax.Precision.HIGHEST
epsilon = 1e-06


def normalize(values):
    average = jnp.mean(values, -1, keepdims=True)
    centered = values - average
    inverse = lax.rsqrt(jnp.mean(centered * centered, -1, keepdims=True) + epsilon)
    return (centered * inverse, inverse)


def norm_back(upstream, normed, inverse):
    return (
        upstream
        - jnp.mean(upstream, -1, keepdims=True)
        - normed * jnp.mean(upstream * normed, -1, keepdims=True)
    ) * inverse


def matmul(left, right):
    return jnp.dot(left, right, preferred_element_type=jnp.float32)


def place_of():
    return lax.axis_index("fsdp") * 2 + lax.axis_index("sp")


def pairs_by(rule):
    return [(place, rule(place)) for place in range(SHARDS)]


def swap_rule(place):
    return (place & 4) | ((place & 1) << 1) | ((place >> 1) & 1)


def core_rule(place):
    return place ^ 2


def first_rule(place):
    return place ^ (1 if place & 2 else 4)


def second_rule(place):
    return place ^ (4 if place & 2 else 1)


def permute(values, rule):
    return lax.ppermute(values, GROUP, pairs_by(rule))


def swap_halves(values):
    place = place_of()
    pairs = [pair for pair in pairs_by(swap_rule) if pair[0] != pair[1]]
    received = lax.ppermute(values, GROUP, pairs)
    stays = ((place >> 1) & 1) == (place & 1)
    return jnp.where(stays, values, received)


def gather_group(values):
    place = place_of()
    stacked = values[None]
    for bit in (1, 2, 4):
        received = permute(stacked, lambda at: at ^ bit)
        stacked = jnp.where(
            (place & bit) == 0,
            jnp.concatenate([stacked, received]),
            jnp.concatenate([received, stacked]),
        )
    return stacked


def gather_replicas(values, replicas):
    stacked = [values]
    for shift in range(1, replicas):
        pairs = [(at, (at + shift) % replicas) for at in range(replicas)]
        stacked.append(lax.ppermute(values, "rep", pairs))
    return jnp.stack(stacked)


def assemble_kernel(order_ref, *refs):
    pieces, whole, buffer, load_sems, store_sems = (
        refs[:SHARDS],
        refs[SHARDS],
        refs[SHARDS + 1],
        refs[SHARDS + 2],
        refs[SHARDS + 3],
    )
    rows = buffer.shape[1]
    loads = [
        pltpu.make_async_copy(piece, buffer.at[at], load_sems.at[at])
        for at, piece in enumerate(pieces)
    ]
    for load in loads:
        load.start()
    stores = []
    for at, load in enumerate(loads):
        load.wait()
        target = pl.ds(pl.multiple_of(order_ref[at] * rows, 16), rows)
        store = pltpu.make_async_copy(buffer.at[at], whole.at[target], store_sems.at[at])
        store.start()
        stores.append(store)
    for store in stores:
        store.wait()


def assemble(pieces, order):
    rows, columns = pieces[0].shape
    size = SHARDS * rows * columns * 2
    return pl.pallas_call(
        assemble_kernel,
        out_shape=jax.ShapeDtypeStruct((SHARDS * rows, columns), pieces[0].dtype),
        in_specs=[pl.BlockSpec(memory_space=pltpu.SMEM)]
        + [pl.BlockSpec(memory_space=pl.ANY)] * SHARDS,
        out_specs=pl.BlockSpec(memory_space=pl.ANY),
        scratch_shapes=[
            pltpu.VMEM((SHARDS, rows, columns), pieces[0].dtype),
            pltpu.SemaphoreType.DMA((SHARDS,)),
            pltpu.SemaphoreType.DMA((SHARDS,)),
        ],
        compiler_params=pltpu.CompilerParams(vmem_limit_bytes=size + (4 << 20)),
        cost_estimate=SHORT,
    )(order, *pieces)


def gather_pieces(shard):
    place = place_of()
    near = jnp.where((place & 2) == 0, 4, 1)
    far = 5 - near
    other = place ^ 2
    first = permute(shard, first_rule)
    second = permute(shard, second_rule)
    both = permute(first, second_rule)
    held = [shard, first, second, both]
    pieces = held + [permute(piece, core_rule) for piece in held]
    order = [place, place ^ near, place ^ far, place ^ 5]
    order += [other, other ^ far, other ^ near, other ^ 5]
    return pieces, jnp.stack(order).astype(jnp.int32)


def tie(*values):
    return lax.optimization_barrier(values)


class Scatter:
    def __init__(self, halves):
        self.place = place_of()
        self.core = (self.place >> 1) & 1
        self.kept, sent = halves
        self.low = sent.dtype
        self.received = permute(sent, core_rule)

    def second(self):
        kept = self.kept.astype(jnp.float32) + self.received.astype(jnp.float32)
        kept = kept.astype(self.low)
        mine = ((self.place >> 2) << 1) | (self.place & 1)
        near = jnp.where(self.core == 0, 2, 1)

        def pair(which):
            parts = [which, which ^ 3 ^ near]
            return jnp.concatenate([lax.dynamic_slice_in_dim(kept, at, 1, 0) for at in parts])

        self.kept = pair(mine)
        self.received = permute(pair(mine ^ near), first_rule)

    def third(self):
        kept = self.kept.astype(jnp.float32) + self.received.astype(jnp.float32)
        self.kept = kept[0]
        self.received = permute(kept[1].astype(self.low), second_rule)

    def result(self):
        return self.kept + self.received.astype(jnp.float32)


class ReplicaSum:
    def __init__(self, partial, replicas):
        self.replicas = replicas
        self.own = lax.axis_index("rep")
        self.shape = partial.shape
        self.span = partial.shape[1] // replicas
        low = partial.astype(jnp.bfloat16)
        self.kept = self.piece(partial, self.own)
        self.received = [
            self.send(self.piece(low, self.own + shift), shift) for shift in range(1, replicas)
        ]

    def piece(self, values, which):
        return lax.dynamic_slice_in_dim(values, which % self.replicas * self.span, self.span, 1)

    def send(self, values, shift):
        pairs = [(at, (at + shift) % self.replicas) for at in range(self.replicas)]
        return lax.ppermute(values, "rep", pairs)

    def second(self):
        total = self.kept
        for received in self.received:
            total = total + received.astype(jnp.float32)
        low = total.astype(jnp.bfloat16)
        self.received = [low] + [self.send(low, shift) for shift in range(1, self.replicas)]

    def result(self):
        whole = jnp.zeros(self.shape, jnp.float32)
        for shift, received in enumerate(self.received):
            start = (self.own - shift) % self.replicas * self.span
            whole = lax.dynamic_update_slice_in_dim(whole, received.astype(jnp.float32), start, 1)
        return whole


WINDOW = 256
GELU_RATE = 0.7978845608028654
GELU_CUBE = 0.044715
SHORT = pl.CostEstimate(flops=1 << 20, bytes_accessed=1 << 20, transcendentals=0)


def head_lanes(heads, width):
    low = heads[0] * HEAD // 128 * 128
    high = -(-(heads[-1] + 1) * HEAD // 128) * 128
    return min(low, width - WINDOW), high


def head_window(first_head, width, base):
    first = (first_head + pl.program_id(0)) * HEAD
    start = jnp.minimum(first // 128 * 128, width - WINDOW)
    start = pl.multiple_of(start, 128)
    lane = lax.broadcasted_iota(jnp.int32, (1, WINDOW), 1) + start
    inside = (lane >= first) & (lane < first + HEAD)
    mask = jnp.where(inside, 1.0, 0.0).astype(jnp.bfloat16)
    lanes = [pl.ds(pl.multiple_of(start + at, 128), WINDOW) for at in (0, width, -base)]
    return (*lanes, mask)


def dot_last(left, right):
    return lax.dot_general(
        left, right, (((1,), (1,)), ((), ())), preferred_element_type=jnp.float32
    )


def dot_first(left, right):
    return lax.dot_general(
        left, right, (((0,), (0,)), ((), ())), preferred_element_type=jnp.float32
    )


def attend_kernel(first_head, base, query_ref, own_ref, other_ref, out_ref, log_ref, total_ref):
    length, width = query_ref.shape
    head = pl.program_id(0)
    key_lanes, value_lanes, out_lanes, mask = head_window(first_head, width, base)
    score_scale = float(HEAD) ** (-0.5)

    @pl.when(head == 0)
    def _():
        total_ref[...] = jnp.zeros_like(total_ref)
        log_ref[...] = jnp.zeros_like(log_ref)

    keys = jnp.concatenate([own_ref[:, key_lanes], other_ref[:, key_lanes]]) * mask
    values = jnp.concatenate([own_ref[:, value_lanes], other_ref[:, value_lanes]]) * mask
    rows = min(256, length)
    for at in range(0, length, rows):
        block = pl.ds(at, rows)
        scores = dot_last(query_ref[block, key_lanes], keys)
        row_max = jnp.max(scores, -1, keepdims=True)
        weights = jnp.exp((scores - row_max) * score_scale)
        row_total = jnp.sum(weights, -1, keepdims=True)
        probs = (weights * (1.0 / row_total)).astype(jnp.bfloat16)
        total_ref[block, out_lanes] += jnp.dot(
            probs, values, preferred_element_type=jnp.float32
        )
        log_total = row_max * score_scale + jnp.log(row_total)
        lane = lax.broadcasted_iota(jnp.int32, (rows, 128), 1)
        log_ref[block, :] = jnp.where(lane == first_head + head, log_total, log_ref[block, :])

    @pl.when(head == pl.num_programs(0) - 1)
    def _():
        out_ref[...] = total_ref[...].astype(out_ref.dtype)


def attend(query, own, other, heads):
    length, width = query.shape
    low, high = head_lanes(heads, width)
    return pl.pallas_call(
        functools.partial(attend_kernel, heads[0], low),
        grid=(len(heads),),
        out_shape=(
            jax.ShapeDtypeStruct((length, high - low), jnp.bfloat16),
            jax.ShapeDtypeStruct((length, 128), jnp.float32),
        ),
        in_specs=[
            pl.BlockSpec((length, width), lambda head: (0, 0)),
            pl.BlockSpec(own.shape, lambda head: (0, 0)),
            pl.BlockSpec(other.shape, lambda head: (0, 0)),
        ],
        out_specs=(
            pl.BlockSpec((length, high - low), lambda head: (0, 0)),
            pl.BlockSpec((length, 128), lambda head: (0, 0)),
        ),
        scratch_shapes=[pltpu.VMEM((length, high - low), jnp.float32)],
        compiler_params=pltpu.CompilerParams(vmem_limit_bytes=48 << 20),
        cost_estimate=SHORT,
    )(query, own, other)


def attend_back_kernel(
    first_head, base, query_ref, own_ref, other_ref, upstream_ref, log_ref, d_query_ref, d_own_ref, d_other_ref,
    query_total, key_total, value_total,
):
    length, width = query_ref.shape
    head = pl.program_id(0)
    key_lanes, value_lanes, out_lanes, mask = head_window(first_head, width, base)
    score_scale = float(HEAD) ** (-0.5)

    @pl.when(head == 0)
    def _():
        query_total[...] = jnp.zeros_like(query_total)
        key_total[...] = jnp.zeros_like(key_total)
        value_total[...] = jnp.zeros_like(value_total)

    keys = jnp.concatenate([own_ref[:, key_lanes], other_ref[:, key_lanes]]) * mask
    values = jnp.concatenate([own_ref[:, value_lanes], other_ref[:, value_lanes]]) * mask
    rows = min(256, length)
    for at in range(0, length, rows):
        block = pl.ds(at, rows)
        query = query_ref[block, key_lanes] * mask
        upstream = upstream_ref[block, key_lanes] * mask
        scores = dot_last(keys, query)
        probs = jnp.exp(scores * score_scale - log_ref[0, :, block])
        d_probs = dot_last(values, upstream)
        weighted = probs * d_probs
        row_sum = jnp.sum(weighted, 0, keepdims=True)
        d_scores = (weighted - probs * row_sum).astype(jnp.bfloat16)
        value_total[:, out_lanes] += jnp.dot(
            probs.astype(jnp.bfloat16), upstream, preferred_element_type=jnp.float32
        )
        key_total[:, out_lanes] += score_scale * jnp.dot(
            d_scores, query, preferred_element_type=jnp.float32
        )
        query_total[block, out_lanes] += dot_first(d_scores, keys)

    @pl.when(head == pl.num_programs(0) - 1)
    def _():
        d_query_ref[...] = (query_total[...] * score_scale).astype(d_query_ref.dtype)
        for at, total in enumerate((key_total, value_total)):
            d_own_ref[at] = total[: own_ref.shape[0]]
            d_other_ref[at] = total[own_ref.shape[0] :].astype(d_other_ref.dtype)


def attend_back(query, own, other, upstream, log_totals, heads):
    length, width = query.shape
    low, high = head_lanes(heads, width)
    span = high - low
    whole = lambda head: (0, 0)
    halves = pl.BlockSpec((2, own.shape[0], span), lambda head: (0, 0, 0))
    return pl.pallas_call(
        functools.partial(attend_back_kernel, heads[0], low),
        grid=(len(heads),),
        out_shape=(
            jax.ShapeDtypeStruct((length, span), jnp.bfloat16),
            jax.ShapeDtypeStruct((2, own.shape[0], span), jnp.float32),
            jax.ShapeDtypeStruct((2, other.shape[0], span), jnp.bfloat16),
        ),
        in_specs=[
            pl.BlockSpec((length, width), whole),
            pl.BlockSpec(own.shape, whole),
            pl.BlockSpec(other.shape, whole),
            pl.BlockSpec((length, width), whole),
            pl.BlockSpec((1, 1, length), lambda head: (heads[0] + head, 0, 0)),
        ],
        out_specs=(pl.BlockSpec((length, span), whole), halves, halves),
        scratch_shapes=[
            pltpu.VMEM((length, span), jnp.float32),
            pltpu.VMEM((own.shape[0] + other.shape[0], span), jnp.float32),
            pltpu.VMEM((own.shape[0] + other.shape[0], span), jnp.float32),
        ],
        compiler_params=pltpu.CompilerParams(vmem_limit_bytes=56 << 20),
        cost_estimate=SHORT,
    )(query, own, other, upstream, log_totals)


def join_heads(left, right, width):
    shared = left.shape[-1] + right.shape[-1] - width
    if shared == 0:
        return jnp.concatenate([left, right], axis=-1)
    edge = left.shape[-1] - shared
    middle = left[..., edge:] + right[..., :shared]
    return jnp.concatenate([left[..., :edge], middle, right[..., shared:]], axis=-1)


def store_halves(grad, kept_ref, sent_ref):
    core = lax.axis_index("fsdp") % 2
    rows = grad.shape[0] // SHARDS
    low = grad.astype(kept_ref.dtype)
    for owner in (0, 1):
        blocks = [at for at in range(SHARDS) if (at >> 1) & 1 == owner]

        @pl.when(core == owner)
        def _():
            for slot, at in enumerate(blocks):
                kept_ref[slot] = low[at * rows : (at + 1) * rows]

        @pl.when(core != owner)
        def _():
            for slot, at in enumerate(blocks):
                sent_ref[slot] = low[at * rows : (at + 1) * rows]


def product_back_kernel(left_ref, upstream_ref, weight_ref, d_left_ref, kept_ref, sent_ref):
    @pl.when(pl.program_id(0) == 0)
    def _():
        d_left_ref[...] = jnp.zeros_like(d_left_ref)

    upstream = upstream_ref[...]
    store_halves(dot_first(left_ref[...], upstream), kept_ref, sent_ref)
    d_left_ref[...] += dot_last(upstream, weight_ref[...])


def product_back(left, upstream, weight):
    length, width = left.shape
    columns = weight.shape[1]
    block = 384
    fixed = pl.BlockSpec((length, width), lambda at: (0, 0))
    half = pl.BlockSpec((SHARDS // 2, width // SHARDS, block), lambda at: (0, 0, at))
    half_shape = jax.ShapeDtypeStruct((SHARDS // 2, width // SHARDS, columns), jnp.bfloat16)
    d_left, kept, sent = pl.pallas_call(
        product_back_kernel,
        grid=(columns // block,),
        out_shape=(
            jax.ShapeDtypeStruct((length, width), jnp.float32),
            half_shape,
            half_shape,
        ),
        in_specs=[
            fixed,
            pl.BlockSpec((length, block), lambda at: (0, at)),
            pl.BlockSpec((width, block), lambda at: (0, at)),
        ],
        out_specs=(fixed, half, half),
        compiler_params=pltpu.CompilerParams(vmem_limit_bytes=32 << 20),
        cost_estimate=SHORT,
    )(left, upstream, weight)
    return d_left, (kept, sent)


def mlp_kernel(
    hidden_ref, upstream_ref, up_ref, bias_ref, down_ref,
    branch_ref, d_hidden_ref, up_kept_ref, up_sent_ref, down_grad_ref, bias_grad_ref,
):
    @pl.when(pl.program_id(0) == 0)
    def _():
        branch_ref[...] = jnp.zeros_like(branch_ref)
        d_hidden_ref[...] = jnp.zeros_like(d_hidden_ref)

    hidden = hidden_ref[...]
    upstream = upstream_ref[...]
    preact = (
        jnp.dot(hidden, up_ref[...], preferred_element_type=jnp.float32) + bias_ref[...]
    )
    square = preact * preact
    bent = jnp.tanh(GELU_RATE * preact * (1.0 + GELU_CUBE * square))
    half = 0.5 * (1.0 + bent)
    slope = half + (0.5 * GELU_RATE) * preact * (1.0 - bent * bent) * (
        1.0 + (3.0 * GELU_CUBE) * square
    )
    activated = (preact * half).astype(jnp.bfloat16)
    branch_ref[...] += jnp.dot(activated, down_ref[...], preferred_element_type=jnp.float32)
    d_preact = dot_last(upstream, down_ref[...]) * slope
    d_preact = d_preact.astype(jnp.bfloat16)
    bias_grad_ref[...] = jnp.sum(d_preact.astype(jnp.float32), 0, keepdims=True)
    down_grad_ref[...] = dot_first(activated, upstream).astype(jnp.bfloat16)
    d_hidden_ref[...] += dot_last(d_preact, up_ref[...])
    store_halves(dot_first(hidden, d_preact), up_kept_ref, up_sent_ref)


def mlp(hidden, upstream, up, bias, down):
    length, width = hidden.shape
    units = up.shape[1]
    block = 512
    fixed = pl.BlockSpec((length, width), lambda at: (0, 0))
    columns = pl.BlockSpec((width, block), lambda at: (0, at))
    lanes = pl.BlockSpec((1, block), lambda at: (0, at))
    rows = pl.BlockSpec((block, width), lambda at: (at, 0))
    half = pl.BlockSpec((SHARDS // 2, width // SHARDS, block), lambda at: (0, 0, at))
    half_shape = jax.ShapeDtypeStruct((SHARDS // 2, width // SHARDS, units), jnp.bfloat16)
    return pl.pallas_call(
        mlp_kernel,
        grid=(units // block,),
        out_shape=(
            jax.ShapeDtypeStruct((length, width), jnp.float32),
            jax.ShapeDtypeStruct((length, width), jnp.float32),
            half_shape,
            half_shape,
            jax.ShapeDtypeStruct(down.shape, jnp.bfloat16),
            jax.ShapeDtypeStruct((1, units), jnp.float32),
        ),
        in_specs=[fixed, fixed, columns, lanes, rows],
        out_specs=(fixed, fixed, half, half, rows, lanes),
        compiler_params=pltpu.CompilerParams(vmem_limit_bytes=56 << 20),
        cost_estimate=SHORT,
    )(hidden, upstream, up, bias, down)


def per_device(
    latent_in,
    condition,
    valid_slots,
    ada_weight,
    ada_bias,
    qkv_weight,
    qv_bias,
    out_weight,
    out_bias,
    up_weight,
    up_bias,
    down_weight,
    down_bias,
    cotangent,
):
    number, length, width = latent_in.shape
    place = place_of()
    fsdp_index = lax.axis_index("fsdp")
    held = (place >> 2) * 2 + (place & 1)
    rows = width // SHARDS
    replicas = lax.axis_size("rep")

    small = jnp.concatenate(
        [
            condition[0],
            qv_bias,
            out_bias,
            up_bias,
            down_bias,
            jnp.broadcast_to(valid_slots.astype(jnp.bfloat16), (128,)),
        ]
    )
    small_all = gather_group(small)
    latent_low = swap_halves(latent_in)
    qkv_pieces, order = gather_pieces(qkv_weight)
    full_up = lax.all_gather(up_weight, GROUP, axis=0, tiled=True)
    full_out = lax.all_gather(out_weight, GROUP, axis=0, tiled=True)
    cotangent_low = swap_halves(cotangent)
    full_qkv = assemble(qkv_pieces, order)
    full_down = lax.all_gather(down_weight, GROUP, axis=0, tiled=True)

    bounds = [0, width]
    for bias in (qv_bias, out_bias, up_bias, down_bias):
        bounds.append(bounds[-1] + bias.shape[0])
    cond_group = small_all[::2, :width].astype(jnp.float32)
    full_qv_bias, full_out_bias, full_up_bias, full_down_bias = (
        small_all[:, low:high].reshape(-1).astype(jnp.float32)
        for low, high in zip(bounds[1:-1], bounds[2:])
    )
    valid_group = small_all[::2, bounds[-1]].astype(jnp.float32)
    slot_mask = lax.dynamic_slice_in_dim(valid_group, held, 1)[:, None, None]

    silu_group = jax.nn.silu(cond_group).astype(jnp.bfloat16)
    silu_mine = lax.dynamic_slice_in_dim(silu_group, place * rows, rows, 1)
    ada_bias_row = lax.dynamic_update_slice_in_dim(
        jnp.zeros((ada_weight.shape[1],), jnp.float32),
        ada_bias.astype(jnp.float32),
        place * ada_bias.shape[0],
        0,
    )
    modulation = matmul(silu_mine, ada_weight) + ada_bias_row
    for bit, count in ((4, 2), (1, 1)):
        upper = (place & bit) != 0
        sent = jnp.where(upper, modulation[:count], modulation[count:])
        kept = jnp.where(upper, modulation[count:], modulation[:count])
        modulation = kept + permute(sent, lambda at: at ^ bit)
    modulation = modulation + permute(modulation, core_rule)
    shift_one, scale_one, gate_one, shift_two, scale_two, gate_two = jnp.split(
        modulation, 6, axis=-1
    )

    latent = latent_low[0].astype(jnp.float32)
    normed_one, inverse_one = normalize(latent)
    hidden_one = (normed_one * (1.0 + scale_one) + shift_one).astype(jnp.bfloat16)
    bias_full = jnp.concatenate(
        [full_qv_bias[:width], jnp.zeros((width,), jnp.float32), full_qv_bias[width:]]
    )
    projected = (matmul(hidden_one, full_qkv) + bias_full).astype(jnp.bfloat16)
    query = projected[:, :width]
    pair_own = projected[:, width:]
    pair_other = permute(pair_own, core_rule)
    heads = range(width // HEAD)
    halves = heads[: len(heads) // 2], heads[len(heads) // 2 :]
    attended_low, log_totals = attend(query, pair_own, pair_other, heads)
    log_rows = log_totals[:, : len(heads)].T[:, None, :]
    branch_one = matmul(attended_low, full_out) + full_out_bias
    middle = latent + gate_one * branch_one

    normed_two, inverse_two = normalize(middle)
    hidden_two = (normed_two * (1.0 + scale_two) + shift_two).astype(jnp.bfloat16)
    mask_row = slot_mask[0]
    d_out = cotangent_low[0].astype(jnp.float32) * mask_row
    d_branch_two = (gate_two * d_out).astype(jnp.bfloat16)
    branch_two, d_hidden_two, up_kept, up_sent, down_grad, up_bias_grad = mlp(
        hidden_two, d_branch_two, full_up, full_up_bias[None], full_down
    )
    up_scatter = Scatter((up_kept, up_sent))
    down_shard = lax.psum_scatter(down_grad, GROUP, scatter_dimension=0, tiled=True)
    branch_two = branch_two + full_down_bias
    block_out = (mask_row * (middle + gate_two * branch_two)).astype(jnp.bfloat16)
    block_out = swap_halves(block_out[None])
    d_gate_two = jnp.sum(d_out * branch_two, axis=0)
    down_bias_grad = jnp.sum(d_branch_two.astype(jnp.float32), axis=0)
    up_bias_grad = up_bias_grad[0]
    d_shift_two = jnp.sum(d_hidden_two, axis=0)
    d_scale_two = jnp.sum(d_hidden_two * normed_two, axis=0)
    d_middle = d_out + norm_back(d_hidden_two * (1.0 + scale_two), normed_two, inverse_two)
    d_gate_one = jnp.sum(d_middle * branch_one, axis=0)
    d_branch_one = (gate_one * d_middle).astype(jnp.bfloat16)

    d_attended, out_halves = product_back(attended_low, d_branch_one, full_out)
    d_attended = d_attended.astype(jnp.bfloat16)
    out_scatter = Scatter(out_halves)
    out_bias_grad = jnp.sum(d_branch_one.astype(jnp.float32), axis=0)
    d_attended, up_scatter.received = tie(d_attended, up_scatter.received)
    up_scatter.second()
    left = attend_back(query, pair_own, pair_other, d_attended, log_rows, halves[0])
    d_query, d_attended, up_scatter.received, out_scatter.received = tie(
        left[0], d_attended, up_scatter.received, out_scatter.received
    )
    up_scatter.third()
    out_scatter.second()
    right = attend_back(query, pair_own, pair_other, d_attended, log_rows, halves[1])
    *right, up_scatter.received, out_scatter.received = tie(
        *right, up_scatter.received, out_scatter.received
    )
    d_query = join_heads(d_query, right[0], width)
    d_own = join_heads(left[1], right[1], width)
    d_other = permute(join_heads(left[2], right[2], width), core_rule)
    d_own = (d_own + d_other.astype(jnp.float32)).astype(jnp.bfloat16)
    d_projected = jnp.concatenate([d_query, d_own[0], d_own[1]], axis=-1)

    up_sum = ReplicaSum(up_scatter.result(), replicas)
    out_scatter.third()
    d_hidden_one, qkv_halves = product_back(hidden_one, d_projected, full_qkv)
    qkv_scatter = Scatter(qkv_halves)
    column_sums = jnp.sum(d_projected.astype(jnp.float32), axis=0)
    d_hidden_one, down_shard, qkv_scatter.received, *up_sum.received = tie(
        d_hidden_one, down_shard, qkv_scatter.received, *up_sum.received
    )
    qkv_scatter.second()
    up_sum.second()
    down_total = lax.psum(down_shard, "rep")
    d_shift_one = jnp.sum(d_hidden_one, axis=0)
    d_scale_one = jnp.sum(d_hidden_one * normed_one, axis=0)
    latent_grad = d_middle + norm_back(d_hidden_one * (1.0 + scale_one), normed_one, inverse_one)
    latent_grad = swap_halves(latent_grad.astype(jnp.bfloat16)[None]).astype(jnp.float32)

    qkv_scatter.third()
    late = jnp.concatenate([out_scatter.result(), qkv_scatter.result()], axis=1)
    late_sum = ReplicaSum(late, replicas)
    down_total, *late_sum.received = tie(down_total, *late_sum.received)
    late_sum.second()
    up_total = up_sum.result()
    late_total = late_sum.result()
    out_total, qkv_total = late_total[:, :width], late_total[:, width:]

    bias_grads = (
        jnp.concatenate([column_sums[:width], column_sums[2 * width :]]),
        out_bias_grad,
        up_bias_grad,
        down_bias_grad,
    )
    sums = [d_shift_one, d_scale_one, d_gate_one, d_shift_two, d_scale_two, d_gate_two]
    ada_width = 6 * width
    sums_all = gather_group(jnp.concatenate(sums + list(bias_grads)))
    d_group = sums_all[:, :ada_width].reshape(2, 2, 2, ada_width).sum(1).reshape(4, ada_width)
    bias_mine = []
    start = ada_width
    for grad in bias_grads:
        total = jnp.sum(sums_all[:, start : start + grad.shape[0]], axis=0)
        piece = grad.shape[0] // SHARDS
        bias_mine.append(lax.dynamic_slice_in_dim(total, place * piece, piece))
        start += grad.shape[0]
    d_silu = lax.dot_general(
        d_group,
        ada_weight.astype(jnp.float32),
        (((1,), (1,)), ((), ())),
        precision=exact_mode,
    )
    cond_mine = lax.dynamic_slice_in_dim(cond_group, place * rows, rows, 1)
    cond_part = jax.vjp(jax.nn.silu, cond_mine)[1](d_silu)[0]
    cond_all = gather_group(cond_part)
    cond_grad = lax.dynamic_index_in_dim(cond_all, fsdp_index, 1, keepdims=False)
    cond_grad = cond_grad.reshape(1, width)

    packed = jnp.concatenate(
        [d_group.reshape(-1), silu_mine.astype(jnp.float32).reshape(-1)] + bias_mine
    )
    packed_all = gather_replicas(packed, replicas)
    d_all = packed_all[:, : 4 * ada_width].reshape(-1, ada_width)
    silu_all = packed_all[:, 4 * ada_width : 4 * ada_width + 4 * rows].reshape(-1, rows)
    ada_total = lax.dot_general(
        silu_all, d_all, (((0,), (0,)), ((), ())), precision=exact_mode
    )
    ada_bias_total = jnp.sum(
        lax.dynamic_slice_in_dim(d_all, place * ada_bias.shape[0], ada_bias.shape[0], 1), axis=0
    )
    bias_totals = jnp.sum(packed_all[:, 4 * ada_width + 4 * rows :], axis=0)
    cuts = [0]
    for piece in bias_mine:
        cuts.append(cuts[-1] + piece.shape[0])
    qv_total, out_bias_total, up_bias_total, down_bias_total = (
        bias_totals[low:high] for low, high in zip(cuts[:-1], cuts[1:])
    )
    return (
        block_out,
        latent_grad,
        cond_grad,
        ada_total,
        ada_bias_total,
        qkv_total.astype(jnp.float32),
        qv_total,
        out_total.astype(jnp.float32),
        out_bias_total,
        up_total.astype(jnp.float32),
        up_bias_total,
        down_total.astype(jnp.float32),
        down_bias_total,
    )


def solution(mesh):
    tokens = P(("rep", "fsdp"), "sp", None)
    rows = P(("rep", "fsdp"), None)
    matrix = P(GROUP, None)
    vector = P(GROUP)
    weights = (matrix, vector) * 5
    return jax.shard_map(
        per_device,
        mesh=mesh,
        in_specs=(tokens, rows, P(("rep", "fsdp"))) + weights + (tokens,),
        out_specs=(tokens, tokens, rows) + weights,
        check_vma=False,
    )
```

```python
import functools

import jax
import jax.numpy as jnp
from jax import lax
from jax.experimental import pallas as pl
from jax.experimental.pallas import tpu as pltpu
from jax.sharding import PartitionSpec as P

HEAD = 72
GROUP = ("fsdp", "sp")
SHARDS = 8

exact_mode = lax.Precision.HIGHEST
epsilon = 1e-06


def normalize(values):
    average = jnp.mean(values, -1, keepdims=True)
    centered = values - average
    inverse = lax.rsqrt(jnp.mean(centered * centered, -1, keepdims=True) + epsilon)
    return (centered * inverse, inverse)


def norm_back(upstream, normed, inverse):
    return (
        upstream
        - jnp.mean(upstream, -1, keepdims=True)
        - normed * jnp.mean(upstream * normed, -1, keepdims=True)
    ) * inverse


def matmul(left, right):
    return jnp.dot(left, right, preferred_element_type=jnp.float32)


def place_of():
    return lax.axis_index("fsdp") * 2 + lax.axis_index("sp")


def pairs_by(rule):
    return [(place, rule(place)) for place in range(SHARDS)]


def swap_rule(place):
    return (place & 4) | ((place & 1) << 1) | ((place >> 1) & 1)


def core_rule(place):
    return place ^ 2


def first_rule(place):
    return place ^ (1 if place & 2 else 4)


def second_rule(place):
    return place ^ (4 if place & 2 else 1)


def permute(values, rule):
    return lax.ppermute(values, GROUP, pairs_by(rule))


def swap_halves(values):
    place = place_of()
    pairs = [pair for pair in pairs_by(swap_rule) if pair[0] != pair[1]]
    received = lax.ppermute(values, GROUP, pairs)
    stays = ((place >> 1) & 1) == (place & 1)
    return jnp.where(stays, values, received)


def gather_group(values):
    place = place_of()
    stacked = values[None]
    for bit in (1, 2, 4):
        received = permute(stacked, lambda at: at ^ bit)
        stacked = jnp.where(
            (place & bit) == 0,
            jnp.concatenate([stacked, received]),
            jnp.concatenate([received, stacked]),
        )
    return stacked


def gather_replicas(values, replicas):
    stacked = [values]
    for shift in range(1, replicas):
        pairs = [(at, (at + shift) % replicas) for at in range(replicas)]
        stacked.append(lax.ppermute(values, "rep", pairs))
    return jnp.stack(stacked)


def assemble_kernel(widths, order_ref, *refs):
    pieces, wholes = refs[:SHARDS], refs[SHARDS : SHARDS + len(widths)]
    buffer, load_sems, store_sems = refs[SHARDS + len(widths) :]
    rows = buffer.shape[1]
    loads = [
        pltpu.make_async_copy(piece, buffer.at[at], load_sems.at[at])
        for at, piece in enumerate(pieces)
    ]
    for load in loads:
        load.start()
    stores = []
    for at, load in enumerate(loads):
        load.wait()
        target = pl.ds(pl.multiple_of(order_ref[at] * rows, 16), rows)
        start = 0
        for which, width in enumerate(widths):
            store = pltpu.make_async_copy(
                buffer.at[at, :, pl.ds(start, width)],
                wholes[which].at[target],
                store_sems.at[which, at],
            )
            store.start()
            stores.append(store)
            start += width
    for store in stores:
        store.wait()


def assemble(pieces, order, widths):
    rows, columns = pieces[0].shape
    size = SHARDS * rows * columns * 2
    return pl.pallas_call(
        functools.partial(assemble_kernel, widths),
        out_shape=[
            jax.ShapeDtypeStruct((SHARDS * rows, width), pieces[0].dtype) for width in widths
        ],
        in_specs=[pl.BlockSpec(memory_space=pltpu.SMEM)]
        + [pl.BlockSpec(memory_space=pl.ANY)] * SHARDS,
        out_specs=[pl.BlockSpec(memory_space=pl.ANY)] * len(widths),
        scratch_shapes=[
            pltpu.VMEM((SHARDS, rows, columns), pieces[0].dtype),
            pltpu.SemaphoreType.DMA((SHARDS,)),
            pltpu.SemaphoreType.DMA((len(widths), SHARDS)),
        ],
        compiler_params=pltpu.CompilerParams(vmem_limit_bytes=size + (4 << 20)),
        cost_estimate=SHORT,
    )(order, *pieces)


def gather_pieces(shard):
    place = place_of()
    near = jnp.where((place & 2) == 0, 4, 1)
    far = 5 - near
    other = place ^ 2
    first = permute(shard, first_rule)
    second = permute(shard, second_rule)
    both = permute(first, second_rule)
    held = [shard, first, second, both]
    pieces = held + [permute(piece, core_rule) for piece in held]
    order = [place, place ^ near, place ^ far, place ^ 5]
    order += [other, other ^ far, other ^ near, other ^ 5]
    return pieces, jnp.stack(order).astype(jnp.int32)


def tie(*values):
    return lax.optimization_barrier(values)


class Scatter:
    def __init__(self, halves):
        self.place = place_of()
        self.core = (self.place >> 1) & 1
        self.kept, sent = halves
        self.low = sent.dtype
        self.received = permute(sent, core_rule)

    def second(self):
        kept = self.kept.astype(jnp.float32) + self.received.astype(jnp.float32)
        kept = kept.astype(self.low)
        mine = ((self.place >> 2) << 1) | (self.place & 1)
        near = jnp.where(self.core == 0, 2, 1)

        def pair(which):
            parts = [which, which ^ 3 ^ near]
            return jnp.concatenate([lax.dynamic_slice_in_dim(kept, at, 1, 0) for at in parts])

        self.kept = pair(mine)
        self.received = permute(pair(mine ^ near), first_rule)

    def third(self):
        kept = self.kept.astype(jnp.float32) + self.received.astype(jnp.float32)
        self.kept = kept[0]
        self.received = permute(kept[1].astype(self.low), second_rule)

    def result(self):
        return self.kept + self.received.astype(jnp.float32)


class ReplicaSum:
    def __init__(self, partial, replicas):
        self.replicas = replicas
        self.own = lax.axis_index("rep")
        self.shape = partial.shape
        self.span = partial.shape[1] // replicas
        low = partial.astype(jnp.bfloat16)
        self.kept = self.piece(partial, self.own)
        self.received = [
            self.send(self.piece(low, self.own + shift), shift) for shift in range(1, replicas)
        ]

    def piece(self, values, which):
        return lax.dynamic_slice_in_dim(values, which % self.replicas * self.span, self.span, 1)

    def send(self, values, shift):
        pairs = [(at, (at + shift) % self.replicas) for at in range(self.replicas)]
        return lax.ppermute(values, "rep", pairs)

    def second(self):
        total = self.kept
        for received in self.received:
            total = total + received.astype(jnp.float32)
        low = total.astype(jnp.bfloat16)
        self.received = [low] + [self.send(low, shift) for shift in range(1, self.replicas)]

    def result(self):
        whole = jnp.zeros(self.shape, jnp.float32)
        for shift, received in enumerate(self.received):
            start = (self.own - shift) % self.replicas * self.span
            whole = lax.dynamic_update_slice_in_dim(whole, received.astype(jnp.float32), start, 1)
        return whole


WINDOW = 256
GELU_RATE = 0.7978845608028654
GELU_CUBE = 0.044715
SHORT = pl.CostEstimate(flops=1 << 20, bytes_accessed=1 << 20, transcendentals=0)


def head_lanes(heads, width):
    low = heads[0] * HEAD // 128 * 128
    high = -(-(heads[-1] + 1) * HEAD // 128) * 128
    return min(low, width - WINDOW), high


def head_window(first_head, width, base):
    first = (first_head + pl.program_id(0)) * HEAD
    start = jnp.minimum(first // 128 * 128, width - WINDOW)
    start = pl.multiple_of(start, 128)
    lane = lax.broadcasted_iota(jnp.int32, (1, WINDOW), 1) + start
    inside = (lane >= first) & (lane < first + HEAD)
    mask = jnp.where(inside, 1.0, 0.0).astype(jnp.bfloat16)
    lanes = [pl.ds(pl.multiple_of(start + at, 128), WINDOW) for at in (0, width, -base)]
    return (*lanes, mask)


def dot_last(left, right):
    return lax.dot_general(
        left, right, (((1,), (1,)), ((), ())), preferred_element_type=jnp.float32
    )


def dot_first(left, right):
    return lax.dot_general(
        left, right, (((0,), (0,)), ((), ())), preferred_element_type=jnp.float32
    )


def attend_kernel(first_head, base, query_ref, own_ref, other_ref, out_ref, log_ref, total_ref):
    length, width = query_ref.shape
    head = pl.program_id(0)
    key_lanes, value_lanes, out_lanes, mask = head_window(first_head, width, base)
    score_scale = float(HEAD) ** (-0.5)

    @pl.when(head == 0)
    def _():
        total_ref[...] = jnp.zeros_like(total_ref)
        log_ref[...] = jnp.zeros_like(log_ref)

    keys = jnp.concatenate([own_ref[:, key_lanes], other_ref[:, key_lanes]]) * mask
    values = jnp.concatenate([own_ref[:, value_lanes], other_ref[:, value_lanes]]) * mask
    rows = min(256, length)
    for at in range(0, length, rows):
        block = pl.ds(at, rows)
        scores = dot_last(query_ref[block, key_lanes], keys)
        row_max = jnp.max(scores, -1, keepdims=True)
        weights = jnp.exp((scores - row_max) * score_scale)
        row_total = jnp.sum(weights, -1, keepdims=True)
        probs = (weights * (1.0 / row_total)).astype(jnp.bfloat16)
        total_ref[block, out_lanes] += jnp.dot(
            probs, values, preferred_element_type=jnp.float32
        )
        log_total = row_max * score_scale + jnp.log(row_total)
        lane = lax.broadcasted_iota(jnp.int32, (rows, 128), 1)
        log_ref[block, :] = jnp.where(lane == first_head + head, log_total, log_ref[block, :])

    @pl.when(head == pl.num_programs(0) - 1)
    def _():
        out_ref[...] = total_ref[...].astype(out_ref.dtype)


def attend(query, own, other, heads):
    length, width = query.shape
    low, high = head_lanes(heads, width)
    return pl.pallas_call(
        functools.partial(attend_kernel, heads[0], low),
        grid=(len(heads),),
        out_shape=(
            jax.ShapeDtypeStruct((length, high - low), jnp.bfloat16),
            jax.ShapeDtypeStruct((length, 128), jnp.float32),
        ),
        in_specs=[
            pl.BlockSpec((length, width), lambda head: (0, 0)),
            pl.BlockSpec(own.shape, lambda head: (0, 0)),
            pl.BlockSpec(other.shape, lambda head: (0, 0)),
        ],
        out_specs=(
            pl.BlockSpec((length, high - low), lambda head: (0, 0)),
            pl.BlockSpec((length, 128), lambda head: (0, 0)),
        ),
        scratch_shapes=[pltpu.VMEM((length, high - low), jnp.float32)],
        compiler_params=pltpu.CompilerParams(vmem_limit_bytes=48 << 20),
        cost_estimate=SHORT,
    )(query, own, other)


def attend_back_kernel(
    first_head, base, query_ref, own_ref, other_ref, upstream_ref, log_ref, d_query_ref, d_own_ref, d_other_ref,
    query_total, key_total, value_total,
):
    length, width = query_ref.shape
    head = pl.program_id(0)
    key_lanes, value_lanes, out_lanes, mask = head_window(first_head, width, base)
    score_scale = float(HEAD) ** (-0.5)

    @pl.when(head == 0)
    def _():
        query_total[...] = jnp.zeros_like(query_total)
        key_total[...] = jnp.zeros_like(key_total)
        value_total[...] = jnp.zeros_like(value_total)

    keys = jnp.concatenate([own_ref[:, key_lanes], other_ref[:, key_lanes]]) * mask
    values = jnp.concatenate([own_ref[:, value_lanes], other_ref[:, value_lanes]]) * mask
    rows = min(256, length)
    for at in range(0, length, rows):
        block = pl.ds(at, rows)
        query = query_ref[block, key_lanes] * mask
        upstream = upstream_ref[block, key_lanes] * mask
        scores = dot_last(keys, query)
        probs = jnp.exp(scores * score_scale - log_ref[0, :, block])
        d_probs = dot_last(values, upstream)
        weighted = probs * d_probs
        row_sum = jnp.sum(weighted, 0, keepdims=True)
        d_scores = (weighted - probs * row_sum).astype(jnp.bfloat16)
        value_total[:, out_lanes] += jnp.dot(
            probs.astype(jnp.bfloat16), upstream, preferred_element_type=jnp.float32
        )
        key_total[:, out_lanes] += score_scale * jnp.dot(
            d_scores, query, preferred_element_type=jnp.float32
        )
        query_total[block, out_lanes] += dot_first(d_scores, keys)

    @pl.when(head == pl.num_programs(0) - 1)
    def _():
        d_query_ref[...] = (query_total[...] * score_scale).astype(d_query_ref.dtype)
        for at, total in enumerate((key_total, value_total)):
            d_own_ref[at] = total[: own_ref.shape[0]]
            d_other_ref[at] = total[own_ref.shape[0] :].astype(d_other_ref.dtype)


def attend_back(query, own, other, upstream, log_totals, heads):
    length, width = query.shape
    low, high = head_lanes(heads, width)
    span = high - low
    whole = lambda head: (0, 0)
    halves = pl.BlockSpec((2, own.shape[0], span), lambda head: (0, 0, 0))
    return pl.pallas_call(
        functools.partial(attend_back_kernel, heads[0], low),
        grid=(len(heads),),
        out_shape=(
            jax.ShapeDtypeStruct((length, span), jnp.bfloat16),
            jax.ShapeDtypeStruct((2, own.shape[0], span), jnp.float32),
            jax.ShapeDtypeStruct((2, other.shape[0], span), jnp.bfloat16),
        ),
        in_specs=[
            pl.BlockSpec((length, width), whole),
            pl.BlockSpec(own.shape, whole),
            pl.BlockSpec(other.shape, whole),
            pl.BlockSpec((length, width), whole),
            pl.BlockSpec((1, 1, length), lambda head: (heads[0] + head, 0, 0)),
        ],
        out_specs=(pl.BlockSpec((length, span), whole), halves, halves),
        scratch_shapes=[
            pltpu.VMEM((length, span), jnp.float32),
            pltpu.VMEM((own.shape[0] + other.shape[0], span), jnp.float32),
            pltpu.VMEM((own.shape[0] + other.shape[0], span), jnp.float32),
        ],
        compiler_params=pltpu.CompilerParams(vmem_limit_bytes=56 << 20),
        cost_estimate=SHORT,
    )(query, own, other, upstream, log_totals)


def join_heads(left, right, width):
    shared = left.shape[-1] + right.shape[-1] - width
    if shared == 0:
        return jnp.concatenate([left, right], axis=-1)
    edge = left.shape[-1] - shared
    middle = left[..., edge:] + right[..., :shared]
    return jnp.concatenate([left[..., :edge], middle, right[..., shared:]], axis=-1)


def store_halves(grad, kept_ref, sent_ref):
    core = lax.axis_index("fsdp") % 2
    rows = grad.shape[0] // SHARDS
    low = grad.astype(kept_ref.dtype)
    for owner in (0, 1):
        blocks = [at for at in range(SHARDS) if (at >> 1) & 1 == owner]

        @pl.when(core == owner)
        def _():
            for slot, at in enumerate(blocks):
                kept_ref[slot] = low[at * rows : (at + 1) * rows]

        @pl.when(core != owner)
        def _():
            for slot, at in enumerate(blocks):
                sent_ref[slot] = low[at * rows : (at + 1) * rows]


def product_back_kernel(
    left_ref, upstream_ref, weight_ref, d_left_ref, kept_ref, sent_ref, turned_ref
):
    @pl.when(pl.program_id(0) == 0)
    def _():
        turned_ref[...] = left_ref[...].T
        d_left_ref[...] = jnp.zeros_like(d_left_ref)

    upstream = upstream_ref[...]
    grad = jnp.dot(turned_ref[...], upstream, preferred_element_type=jnp.float32)
    store_halves(grad, kept_ref, sent_ref)
    d_left_ref[...] += dot_last(upstream, weight_ref[...])


def product_back(left, upstream, weight):
    length, width = left.shape
    columns = weight.shape[1]
    block = 384
    fixed = pl.BlockSpec((length, width), lambda at: (0, 0))
    half = pl.BlockSpec((SHARDS // 2, width // SHARDS, block), lambda at: (0, 0, at))
    half_shape = jax.ShapeDtypeStruct((SHARDS // 2, width // SHARDS, columns), jnp.bfloat16)
    d_left, kept, sent = pl.pallas_call(
        product_back_kernel,
        grid=(columns // block,),
        out_shape=(
            jax.ShapeDtypeStruct((length, width), jnp.float32),
            half_shape,
            half_shape,
        ),
        in_specs=[
            fixed,
            pl.BlockSpec((length, block), lambda at: (0, at)),
            pl.BlockSpec((width, block), lambda at: (0, at)),
        ],
        out_specs=(fixed, half, half),
        scratch_shapes=[pltpu.VMEM((width, length), jnp.bfloat16)],
        compiler_params=pltpu.CompilerParams(vmem_limit_bytes=32 << 20),
        cost_estimate=SHORT,
    )(left, upstream, weight)
    return d_left, (kept, sent)


def mlp_kernel(
    hidden_ref, upstream_ref, up_ref, bias_ref, down_ref,
    branch_ref, d_hidden_ref, up_kept_ref, up_sent_ref, down_grad_ref, bias_grad_ref,
    turned_ref,
):
    @pl.when(pl.program_id(0) == 0)
    def _():
        turned_ref[...] = hidden_ref[...].T
        branch_ref[...] = jnp.zeros_like(branch_ref)
        d_hidden_ref[...] = jnp.zeros_like(d_hidden_ref)

    hidden = hidden_ref[...]
    upstream = upstream_ref[...]
    preact = (
        jnp.dot(hidden, up_ref[...], preferred_element_type=jnp.float32) + bias_ref[...]
    )
    square = preact * preact
    bent = jnp.tanh(GELU_RATE * preact * (1.0 + GELU_CUBE * square))
    half = 0.5 * (1.0 + bent)
    slope = half + (0.5 * GELU_RATE) * preact * (1.0 - bent * bent) * (
        1.0 + (3.0 * GELU_CUBE) * square
    )
    activated = (preact * half).astype(jnp.bfloat16)
    branch_ref[...] += jnp.dot(activated, down_ref[...], preferred_element_type=jnp.float32)
    d_preact = dot_last(upstream, down_ref[...]) * slope
    d_preact = d_preact.astype(jnp.bfloat16)
    bias_grad_ref[...] = jnp.sum(d_preact.astype(jnp.float32), 0, keepdims=True)
    down_grad_ref[...] = dot_first(activated, upstream).astype(jnp.bfloat16)
    d_hidden_ref[...] += dot_last(d_preact, up_ref[...])
    up_grad = jnp.dot(turned_ref[...], d_preact, preferred_element_type=jnp.float32)
    store_halves(up_grad, up_kept_ref, up_sent_ref)


def mlp(hidden, upstream, up, bias, down):
    length, width = hidden.shape
    units = up.shape[1]
    block = 512
    fixed = pl.BlockSpec((length, width), lambda at: (0, 0))
    columns = pl.BlockSpec((width, block), lambda at: (0, at))
    lanes = pl.BlockSpec((1, block), lambda at: (0, at))
    rows = pl.BlockSpec((block, width), lambda at: (at, 0))
    half = pl.BlockSpec((SHARDS // 2, width // SHARDS, block), lambda at: (0, 0, at))
    half_shape = jax.ShapeDtypeStruct((SHARDS // 2, width // SHARDS, units), jnp.bfloat16)
    return pl.pallas_call(
        mlp_kernel,
        grid=(units // block,),
        out_shape=(
            jax.ShapeDtypeStruct((length, width), jnp.float32),
            jax.ShapeDtypeStruct((length, width), jnp.float32),
            half_shape,
            half_shape,
            jax.ShapeDtypeStruct(down.shape, jnp.bfloat16),
            jax.ShapeDtypeStruct((1, units), jnp.float32),
        ),
        in_specs=[fixed, fixed, columns, lanes, rows],
        out_specs=(fixed, fixed, half, half, rows, lanes),
        scratch_shapes=[pltpu.VMEM((width, length), jnp.bfloat16)],
        compiler_params=pltpu.CompilerParams(vmem_limit_bytes=56 << 20),
        cost_estimate=SHORT,
    )(hidden, upstream, up, bias, down)


def per_device(
    latent_in,
    condition,
    valid_slots,
    ada_weight,
    ada_bias,
    qkv_weight,
    qv_bias,
    out_weight,
    out_bias,
    up_weight,
    up_bias,
    down_weight,
    down_bias,
    cotangent,
):
    number, length, width = latent_in.shape
    place = place_of()
    fsdp_index = lax.axis_index("fsdp")
    held = (place >> 2) * 2 + (place & 1)
    rows = width // SHARDS
    replicas = lax.axis_size("rep")

    small = jnp.concatenate(
        [
            condition[0],
            qv_bias,
            out_bias,
            up_bias,
            down_bias,
            jnp.broadcast_to(valid_slots.astype(jnp.bfloat16), (128,)),
        ]
    )
    small_all = gather_group(small)
    latent_low = swap_halves(latent_in)
    pieces, order = gather_pieces(jnp.concatenate([qkv_weight, out_weight], axis=1))
    full_up = lax.all_gather(up_weight, GROUP, axis=0, tiled=True)
    cotangent_low = swap_halves(cotangent)
    full_qkv, full_out = assemble(pieces, order, (3 * width, width))
    full_down = lax.all_gather(down_weight, GROUP, axis=0, tiled=True)

    bounds = [0, width]
    for bias in (qv_bias, out_bias, up_bias, down_bias):
        bounds.append(bounds[-1] + bias.shape[0])
    cond_group = small_all[::2, :width].astype(jnp.float32)
    full_qv_bias, full_out_bias, full_up_bias, full_down_bias = (
        small_all[:, low:high].reshape(-1).astype(jnp.float32)
        for low, high in zip(bounds[1:-1], bounds[2:])
    )
    valid_group = small_all[::2, bounds[-1]].astype(jnp.float32)
    slot_mask = lax.dynamic_slice_in_dim(valid_group, held, 1)[:, None, None]

    silu_group = jax.nn.silu(cond_group).astype(jnp.bfloat16)
    silu_mine = lax.dynamic_slice_in_dim(silu_group, place * rows, rows, 1)
    ada_bias_row = lax.dynamic_update_slice_in_dim(
        jnp.zeros((ada_weight.shape[1],), jnp.float32),
        ada_bias.astype(jnp.float32),
        place * ada_bias.shape[0],
        0,
    )
    modulation = matmul(silu_mine, ada_weight) + ada_bias_row
    for bit, count in ((4, 2), (1, 1)):
        upper = (place & bit) != 0
        sent = jnp.where(upper, modulation[:count], modulation[count:])
        kept = jnp.where(upper, modulation[count:], modulation[:count])
        modulation = kept + permute(sent, lambda at: at ^ bit)
    modulation = modulation + permute(modulation, core_rule)
    shift_one, scale_one, gate_one, shift_two, scale_two, gate_two = jnp.split(
        modulation, 6, axis=-1
    )

    latent = latent_low[0].astype(jnp.float32)
    normed_one, inverse_one = normalize(latent)
    hidden_one = (normed_one * (1.0 + scale_one) + shift_one).astype(jnp.bfloat16)
    bias_full = jnp.concatenate(
        [full_qv_bias[:width], jnp.zeros((width,), jnp.float32), full_qv_bias[width:]]
    )
    projected = (matmul(hidden_one, full_qkv) + bias_full).astype(jnp.bfloat16)
    query = projected[:, :width]
    pair_own = projected[:, width:]
    pair_other = permute(pair_own, core_rule)
    heads = range(width // HEAD)
    halves = heads[: len(heads) // 2], heads[len(heads) // 2 :]
    attended_low, log_totals = attend(query, pair_own, pair_other, heads)
    log_rows = log_totals[:, : len(heads)].T[:, None, :]
    branch_one = matmul(attended_low, full_out) + full_out_bias
    middle = latent + gate_one * branch_one

    normed_two, inverse_two = normalize(middle)
    hidden_two = (normed_two * (1.0 + scale_two) + shift_two).astype(jnp.bfloat16)
    mask_row = slot_mask[0]
    d_out = cotangent_low[0].astype(jnp.float32) * mask_row
    d_branch_two = (gate_two * d_out).astype(jnp.bfloat16)
    branch_two, d_hidden_two, up_kept, up_sent, down_grad, up_bias_grad = mlp(
        hidden_two, d_branch_two, full_up, full_up_bias[None], full_down
    )
    up_scatter = Scatter((up_kept, up_sent))
    down_shard = lax.psum_scatter(down_grad, GROUP, scatter_dimension=0, tiled=True)
    branch_two = branch_two + full_down_bias
    block_out = (mask_row * (middle + gate_two * branch_two)).astype(jnp.bfloat16)
    d_gate_two = jnp.sum(d_out * branch_two, axis=0)
    down_bias_grad = jnp.sum(d_branch_two.astype(jnp.float32), axis=0)
    up_bias_grad = up_bias_grad[0]
    d_shift_two = jnp.sum(d_hidden_two, axis=0)
    d_scale_two = jnp.sum(d_hidden_two * normed_two, axis=0)
    d_middle = d_out + norm_back(d_hidden_two * (1.0 + scale_two), normed_two, inverse_two)
    d_gate_one = jnp.sum(d_middle * branch_one, axis=0)
    d_branch_one = (gate_one * d_middle).astype(jnp.bfloat16)

    d_attended, out_halves = product_back(attended_low, d_branch_one, full_out)
    d_attended = d_attended.astype(jnp.bfloat16)
    out_scatter = Scatter(out_halves)
    out_bias_grad = jnp.sum(d_branch_one.astype(jnp.float32), axis=0)
    d_attended, up_scatter.received = tie(d_attended, up_scatter.received)
    up_scatter.second()
    left = attend_back(query, pair_own, pair_other, d_attended, log_rows, halves[0])
    d_query, d_attended, out_scatter.received = tie(left[0], d_attended, out_scatter.received)
    out_scatter.second()
    right = attend_back(query, pair_own, pair_other, d_attended, log_rows, halves[1])
    *right, up_scatter.received = tie(*right, up_scatter.received)
    up_scatter.third()
    d_query = join_heads(d_query, right[0], width)
    d_own = join_heads(left[1], right[1], width)
    d_other = permute(join_heads(left[2], right[2], width), core_rule)
    d_own = (d_own + d_other.astype(jnp.float32)).astype(jnp.bfloat16)
    d_projected = jnp.concatenate([d_query, d_own[0], d_own[1]], axis=-1)

    d_projected, down_shard = tie(d_projected, down_shard)
    d_hidden_one, qkv_halves = product_back(hidden_one, d_projected, full_qkv)
    qkv_scatter = Scatter(qkv_halves)
    column_sums = jnp.sum(d_projected.astype(jnp.float32), axis=0)
    d_hidden_one, *arrived = tie(
        d_hidden_one,
        qkv_scatter.received,
        up_scatter.received,
        out_scatter.received,
    )
    qkv_scatter.received, up_scatter.received, out_scatter.received = arrived
    qkv_scatter.second()
    down_total = lax.psum(down_shard, "rep")
    up_sum = ReplicaSum(up_scatter.result(), replicas)
    out_scatter.third()
    d_shift_one = jnp.sum(d_hidden_one, axis=0)
    d_scale_one = jnp.sum(d_hidden_one * normed_one, axis=0)
    latent_grad = d_middle + norm_back(d_hidden_one * (1.0 + scale_one), normed_one, inverse_one)
    bias_grads = (
        jnp.concatenate([column_sums[:width], column_sums[2 * width :]]),
        out_bias_grad,
        up_bias_grad,
        down_bias_grad,
    )
    sums = [d_shift_one, d_scale_one, d_gate_one, d_shift_two, d_scale_two, d_gate_two]
    ada_width = 6 * width
    small_sums = jnp.concatenate(sums + list(bias_grads))
    qkv_scatter.received, out_scatter.received, *up_sum.received = tie(
        qkv_scatter.received, out_scatter.received, *up_sum.received
    )
    qkv_scatter.third()
    up_sum.second()
    qkv_shard = qkv_scatter.result()
    qkv_shard, latent_grad, block_out, small_sums = tie(
        qkv_shard, latent_grad.astype(jnp.bfloat16), block_out, small_sums
    )
    late_sum = ReplicaSum(
        jnp.concatenate([out_scatter.result(), qkv_shard], axis=1), replicas
    )
    latent_grad = swap_halves(latent_grad[None]).astype(jnp.float32)
    block_out = swap_halves(block_out[None])
    sums_all = gather_group(small_sums)
    down_total, *late_sum.received = tie(down_total, *late_sum.received)
    late_sum.second()
    up_total = up_sum.result()
    late_total = late_sum.result()
    out_total, qkv_total = late_total[:, :width], late_total[:, width:]

    d_group = sums_all[:, :ada_width].reshape(2, 2, 2, ada_width).sum(1).reshape(4, ada_width)
    bias_mine = []
    start = ada_width
    for grad in bias_grads:
        total = jnp.sum(sums_all[:, start : start + grad.shape[0]], axis=0)
        piece = grad.shape[0] // SHARDS
        bias_mine.append(lax.dynamic_slice_in_dim(total, place * piece, piece))
        start += grad.shape[0]
    d_silu = lax.dot_general(
        d_group,
        ada_weight.astype(jnp.float32),
        (((1,), (1,)), ((), ())),
        precision=exact_mode,
    )
    cond_mine = lax.dynamic_slice_in_dim(cond_group, place * rows, rows, 1)
    cond_part = jax.vjp(jax.nn.silu, cond_mine)[1](d_silu)[0]
    cond_all = gather_group(cond_part)
    cond_grad = lax.dynamic_index_in_dim(cond_all, fsdp_index, 1, keepdims=False)
    cond_grad = cond_grad.reshape(1, width)

    packed = jnp.concatenate(
        [d_group.reshape(-1), silu_mine.astype(jnp.float32).reshape(-1)] + bias_mine
    )
    packed_all = gather_replicas(packed, replicas)
    d_all = packed_all[:, : 4 * ada_width].reshape(-1, ada_width)
    silu_all = packed_all[:, 4 * ada_width : 4 * ada_width + 4 * rows].reshape(-1, rows)
    ada_total = lax.dot_general(
        silu_all, d_all, (((0,), (0,)), ((), ())), precision=exact_mode
    )
    ada_bias_total = jnp.sum(
        lax.dynamic_slice_in_dim(d_all, place * ada_bias.shape[0], ada_bias.shape[0], 1), axis=0
    )
    bias_totals = jnp.sum(packed_all[:, 4 * ada_width + 4 * rows :], axis=0)
    cuts = [0]
    for piece in bias_mine:
        cuts.append(cuts[-1] + piece.shape[0])
    qv_total, out_bias_total, up_bias_total, down_bias_total = (
        bias_totals[low:high] for low, high in zip(cuts[:-1], cuts[1:])
    )
    return (
        block_out,
        latent_grad,
        cond_grad,
        ada_total,
        ada_bias_total,
        qkv_total.astype(jnp.float32),
        qv_total,
        out_total.astype(jnp.float32),
        out_bias_total,
        up_total.astype(jnp.float32),
        up_bias_total,
        down_total.astype(jnp.float32),
        down_bias_total,
    )


def solution(mesh):
    tokens = P(("rep", "fsdp"), "sp", None)
    rows = P(("rep", "fsdp"), None)
    matrix = P(GROUP, None)
    vector = P(GROUP)
    weights = (matrix, vector) * 5
    return jax.shard_map(
        per_device,
        mesh=mesh,
        in_specs=(tokens, rows, P(("rep", "fsdp"))) + weights + (tokens,),
        out_specs=(tokens, tokens, rows) + weights,
        check_vma=False,
    )
```

```python
import functools

import jax
import jax.numpy as jnp
from jax import lax
from jax.experimental import pallas as pl
from jax.experimental.pallas import tpu as pltpu
from jax.sharding import PartitionSpec as P

HEAD = 72
GROUP = ("fsdp", "sp")
SHARDS = 8

exact_mode = lax.Precision.HIGHEST
epsilon = 1e-06


def normalize(values):
    average = jnp.mean(values, -1, keepdims=True)
    centered = values - average
    inverse = lax.rsqrt(jnp.mean(centered * centered, -1, keepdims=True) + epsilon)
    return (centered * inverse, inverse)


def norm_back(upstream, normed, inverse):
    return (
        upstream
        - jnp.mean(upstream, -1, keepdims=True)
        - normed * jnp.mean(upstream * normed, -1, keepdims=True)
    ) * inverse


def matmul(left, right):
    return jnp.dot(left, right, preferred_element_type=jnp.float32)


def place_of():
    return lax.axis_index("fsdp") * 2 + lax.axis_index("sp")


def pairs_by(rule):
    return [(place, rule(place)) for place in range(SHARDS)]


def swap_rule(place):
    return (place & 4) | ((place & 1) << 1) | ((place >> 1) & 1)


def core_rule(place):
    return place ^ 2


def first_rule(place):
    return place ^ (1 if place & 2 else 4)


def second_rule(place):
    return place ^ (4 if place & 2 else 1)


def permute(values, rule):
    return lax.ppermute(values, GROUP, pairs_by(rule))


def swap_halves(values):
    place = place_of()
    pairs = [pair for pair in pairs_by(swap_rule) if pair[0] != pair[1]]
    received = lax.ppermute(values, GROUP, pairs)
    stays = ((place >> 1) & 1) == (place & 1)
    return jnp.where(stays, values, received)


def gather_group(values):
    place = place_of()
    stacked = values[None]
    for bit in (1, 2, 4):
        received = permute(stacked, lambda at: at ^ bit)
        stacked = jnp.where(
            (place & bit) == 0,
            jnp.concatenate([stacked, received]),
            jnp.concatenate([received, stacked]),
        )
    return stacked


def gather_replicas(values, replicas):
    stacked = [values]
    for shift in range(1, replicas):
        pairs = [(at, (at + shift) % replicas) for at in range(replicas)]
        stacked.append(lax.ppermute(values, "rep", pairs))
    return jnp.stack(stacked)


def assemble_kernel(widths, order_ref, *refs):
    pieces, wholes = refs[:SHARDS], refs[SHARDS : SHARDS + len(widths)]
    buffer, load_sems, store_sems = refs[SHARDS + len(widths) :]
    rows = buffer.shape[1]
    loads = [
        pltpu.make_async_copy(piece, buffer.at[at], load_sems.at[at])
        for at, piece in enumerate(pieces)
    ]
    for load in loads:
        load.start()
    stores = []
    for at, load in enumerate(loads):
        load.wait()
        target = pl.ds(pl.multiple_of(order_ref[at] * rows, 16), rows)
        start = 0
        for which, width in enumerate(widths):
            store = pltpu.make_async_copy(
                buffer.at[at, :, pl.ds(start, width)],
                wholes[which].at[target],
                store_sems.at[which, at],
            )
            store.start()
            stores.append(store)
            start += width
    for store in stores:
        store.wait()


def assemble(pieces, order, widths):
    rows, columns = pieces[0].shape
    size = SHARDS * rows * columns * 2
    return pl.pallas_call(
        functools.partial(assemble_kernel, widths),
        out_shape=[
            jax.ShapeDtypeStruct((SHARDS * rows, width), pieces[0].dtype) for width in widths
        ],
        in_specs=[pl.BlockSpec(memory_space=pltpu.SMEM)]
        + [pl.BlockSpec(memory_space=pl.ANY)] * SHARDS,
        out_specs=[pl.BlockSpec(memory_space=pl.ANY)] * len(widths),
        scratch_shapes=[
            pltpu.VMEM((SHARDS, rows, columns), pieces[0].dtype),
            pltpu.SemaphoreType.DMA((SHARDS,)),
            pltpu.SemaphoreType.DMA((len(widths), SHARDS)),
        ],
        compiler_params=pltpu.CompilerParams(vmem_limit_bytes=size + (4 << 20)),
        cost_estimate=SHORT,
    )(order, *pieces)


def gather_first(shard):
    place = place_of()
    near = jnp.where((place & 2) == 0, 4, 1)
    far = 5 - near
    other = place ^ 2
    order = [place, place ^ near, place ^ far, place ^ 5]
    order += [other, other ^ far, other ^ near, other ^ 5]
    pieces = [shard, permute(shard, first_rule), permute(shard, second_rule)]
    return pieces, jnp.stack(order).astype(jnp.int32)


def gather_second(pieces):
    return pieces + [permute(pieces[1], second_rule)]


def gather_third(pieces):
    return pieces + [permute(piece, core_rule) for piece in pieces]


def gather_pieces(shard):
    pieces, order = gather_first(shard)
    return gather_third(gather_second(pieces)), order


def tie(*values):
    return lax.optimization_barrier(values)


class Scatter:
    def __init__(self, halves):
        self.place = place_of()
        self.core = (self.place >> 1) & 1
        self.kept, sent = halves
        self.low = sent.dtype
        self.received = permute(sent, core_rule)

    def second(self):
        kept = self.kept.astype(jnp.float32) + self.received.astype(jnp.float32)
        kept = kept.astype(self.low)
        mine = ((self.place >> 2) << 1) | (self.place & 1)
        near = jnp.where(self.core == 0, 2, 1)

        def pair(which):
            parts = [which, which ^ 3 ^ near]
            return jnp.concatenate([lax.dynamic_slice_in_dim(kept, at, 1, 0) for at in parts])

        self.kept = pair(mine)
        self.received = permute(pair(mine ^ near), first_rule)

    def third(self):
        kept = self.kept.astype(jnp.float32) + self.received.astype(jnp.float32)
        self.kept = kept[0]
        self.received = permute(kept[1].astype(self.low), second_rule)

    def result(self):
        return self.kept + self.received.astype(jnp.float32)


class ReplicaSum:
    def __init__(self, partial, replicas):
        self.replicas = replicas
        self.own = lax.axis_index("rep")
        self.shape = partial.shape
        self.span = partial.shape[1] // replicas
        low = partial.astype(jnp.bfloat16)
        self.kept = self.piece(partial, self.own)
        self.received = [
            self.send(self.piece(low, self.own + shift), shift) for shift in range(1, replicas)
        ]

    def piece(self, values, which):
        return lax.dynamic_slice_in_dim(values, which % self.replicas * self.span, self.span, 1)

    def send(self, values, shift):
        pairs = [(at, (at + shift) % self.replicas) for at in range(self.replicas)]
        return lax.ppermute(values, "rep", pairs)

    def second(self):
        total = self.kept
        for received in self.received:
            total = total + received.astype(jnp.float32)
        low = total.astype(jnp.bfloat16)
        self.received = [low] + [self.send(low, shift) for shift in range(1, self.replicas)]

    def result(self):
        whole = jnp.zeros(self.shape, jnp.float32)
        for shift, received in enumerate(self.received):
            start = (self.own - shift) % self.replicas * self.span
            whole = lax.dynamic_update_slice_in_dim(whole, received.astype(jnp.float32), start, 1)
        return whole


WINDOW = 256
GELU_RATE = 0.7978845608028654
GELU_CUBE = 0.044715
SHORT = pl.CostEstimate(flops=1 << 20, bytes_accessed=1 << 20, transcendentals=0)


def head_lanes(heads, width):
    low = heads[0] * HEAD // 128 * 128
    high = -(-(heads[-1] + 1) * HEAD // 128) * 128
    return min(low, width - WINDOW), high


def head_window(first_head, width, base):
    first = (first_head + pl.program_id(0)) * HEAD
    start = jnp.minimum(first // 128 * 128, width - WINDOW)
    start = pl.multiple_of(start, 128)
    lane = lax.broadcasted_iota(jnp.int32, (1, WINDOW), 1) + start
    inside = (lane >= first) & (lane < first + HEAD)
    mask = jnp.where(inside, 1.0, 0.0).astype(jnp.bfloat16)
    lanes = [pl.ds(pl.multiple_of(start + at, 128), WINDOW) for at in (0, width, -base)]
    return (*lanes, mask)


def dot_last(left, right):
    return lax.dot_general(
        left, right, (((1,), (1,)), ((), ())), preferred_element_type=jnp.float32
    )


def dot_first(left, right):
    return lax.dot_general(
        left, right, (((0,), (0,)), ((), ())), preferred_element_type=jnp.float32
    )


def attend_kernel(first_head, base, query_ref, own_ref, other_ref, out_ref, log_ref, total_ref):
    length, width = query_ref.shape
    head = pl.program_id(0)
    key_lanes, value_lanes, out_lanes, mask = head_window(first_head, width, base)
    score_scale = float(HEAD) ** (-0.5)

    @pl.when(head == 0)
    def _():
        total_ref[...] = jnp.zeros_like(total_ref)
        log_ref[...] = jnp.zeros_like(log_ref)

    keys = jnp.concatenate([own_ref[:, key_lanes], other_ref[:, key_lanes]]) * mask
    values = jnp.concatenate([own_ref[:, value_lanes], other_ref[:, value_lanes]]) * mask
    rows = min(256, length)
    for at in range(0, length, rows):
        block = pl.ds(at, rows)
        scores = dot_last(query_ref[block, key_lanes], keys)
        row_max = jnp.max(scores, -1, keepdims=True)
        weights = jnp.exp((scores - row_max) * score_scale)
        row_total = jnp.sum(weights, -1, keepdims=True)
        probs = (weights * (1.0 / row_total)).astype(jnp.bfloat16)
        total_ref[block, out_lanes] += jnp.dot(
            probs, values, preferred_element_type=jnp.float32
        )
        log_total = row_max * score_scale + jnp.log(row_total)
        lane = lax.broadcasted_iota(jnp.int32, (rows, 128), 1)
        log_ref[block, :] = jnp.where(lane == first_head + head, log_total, log_ref[block, :])

    @pl.when(head == pl.num_programs(0) - 1)
    def _():
        out_ref[...] = total_ref[...].astype(out_ref.dtype)


def attend(query, own, other, heads):
    length, width = query.shape
    low, high = head_lanes(heads, width)
    return pl.pallas_call(
        functools.partial(attend_kernel, heads[0], low),
        grid=(len(heads),),
        out_shape=(
            jax.ShapeDtypeStruct((length, high - low), jnp.bfloat16),
            jax.ShapeDtypeStruct((length, 128), jnp.float32),
        ),
        in_specs=[
            pl.BlockSpec((length, width), lambda head: (0, 0)),
            pl.BlockSpec(own.shape, lambda head: (0, 0)),
            pl.BlockSpec(other.shape, lambda head: (0, 0)),
        ],
        out_specs=(
            pl.BlockSpec((length, high - low), lambda head: (0, 0)),
            pl.BlockSpec((length, 128), lambda head: (0, 0)),
        ),
        scratch_shapes=[pltpu.VMEM((length, high - low), jnp.float32)],
        compiler_params=pltpu.CompilerParams(vmem_limit_bytes=48 << 20),
        cost_estimate=SHORT,
    )(query, own, other)


def attend_back_kernel(
    first_head, base, query_ref, own_ref, other_ref, upstream_ref, log_ref, d_query_ref, d_own_ref, d_other_ref,
    query_total, key_total, value_total,
):
    length, width = query_ref.shape
    head = pl.program_id(0)
    key_lanes, value_lanes, out_lanes, mask = head_window(first_head, width, base)
    score_scale = float(HEAD) ** (-0.5)

    @pl.when(head == 0)
    def _():
        query_total[...] = jnp.zeros_like(query_total)
        key_total[...] = jnp.zeros_like(key_total)
        value_total[...] = jnp.zeros_like(value_total)

    keys = jnp.concatenate([own_ref[:, key_lanes], other_ref[:, key_lanes]]) * mask
    values = jnp.concatenate([own_ref[:, value_lanes], other_ref[:, value_lanes]]) * mask
    rows = min(256, length)
    for at in range(0, length, rows):
        block = pl.ds(at, rows)
        query = query_ref[block, key_lanes] * mask
        upstream = upstream_ref[block, key_lanes] * mask
        scores = dot_last(keys, query)
        probs = jnp.exp(scores * score_scale - log_ref[0, :, block])
        d_probs = dot_last(values, upstream)
        weighted = probs * d_probs
        row_sum = jnp.sum(weighted, 0, keepdims=True)
        d_scores = (weighted - probs * row_sum).astype(jnp.bfloat16)
        value_total[:, out_lanes] += jnp.dot(
            probs.astype(jnp.bfloat16), upstream, preferred_element_type=jnp.float32
        )
        key_total[:, out_lanes] += score_scale * jnp.dot(
            d_scores, query, preferred_element_type=jnp.float32
        )
        query_total[block, out_lanes] += dot_first(d_scores, keys)

    @pl.when(head == pl.num_programs(0) - 1)
    def _():
        d_query_ref[...] = (query_total[...] * score_scale).astype(d_query_ref.dtype)
        for at, total in enumerate((key_total, value_total)):
            d_own_ref[at] = total[: own_ref.shape[0]]
            d_other_ref[at] = total[own_ref.shape[0] :].astype(d_other_ref.dtype)


def attend_back(query, own, other, upstream, log_totals, heads):
    length, width = query.shape
    low, high = head_lanes(heads, width)
    span = high - low
    whole = lambda head: (0, 0)
    halves = pl.BlockSpec((2, own.shape[0], span), lambda head: (0, 0, 0))
    return pl.pallas_call(
        functools.partial(attend_back_kernel, heads[0], low),
        grid=(len(heads),),
        out_shape=(
            jax.ShapeDtypeStruct((length, span), jnp.bfloat16),
            jax.ShapeDtypeStruct((2, own.shape[0], span), jnp.float32),
            jax.ShapeDtypeStruct((2, other.shape[0], span), jnp.bfloat16),
        ),
        in_specs=[
            pl.BlockSpec((length, width), whole),
            pl.BlockSpec(own.shape, whole),
            pl.BlockSpec(other.shape, whole),
            pl.BlockSpec((length, width), whole),
            pl.BlockSpec((1, 1, length), lambda head: (heads[0] + head, 0, 0)),
        ],
        out_specs=(pl.BlockSpec((length, span), whole), halves, halves),
        scratch_shapes=[
            pltpu.VMEM((length, span), jnp.float32),
            pltpu.VMEM((own.shape[0] + other.shape[0], span), jnp.float32),
            pltpu.VMEM((own.shape[0] + other.shape[0], span), jnp.float32),
        ],
        compiler_params=pltpu.CompilerParams(vmem_limit_bytes=56 << 20),
        cost_estimate=SHORT,
    )(query, own, other, upstream, log_totals)


def join_heads(left, right, width):
    shared = left.shape[-1] + right.shape[-1] - width
    if shared == 0:
        return jnp.concatenate([left, right], axis=-1)
    edge = left.shape[-1] - shared
    middle = left[..., edge:] + right[..., :shared]
    return jnp.concatenate([left[..., :edge], middle, right[..., shared:]], axis=-1)


def store_halves(grad, kept_ref, sent_ref):
    core = lax.axis_index("fsdp") % 2
    rows = grad.shape[0] // SHARDS
    low = grad.astype(kept_ref.dtype)
    for owner in (0, 1):
        blocks = [at for at in range(SHARDS) if (at >> 1) & 1 == owner]

        @pl.when(core == owner)
        def _():
            for slot, at in enumerate(blocks):
                kept_ref[slot] = low[at * rows : (at + 1) * rows]

        @pl.when(core != owner)
        def _():
            for slot, at in enumerate(blocks):
                sent_ref[slot] = low[at * rows : (at + 1) * rows]


def product_back_kernel(
    left_ref, upstream_ref, weight_ref, d_left_ref, kept_ref, sent_ref, turned_ref
):
    @pl.when(pl.program_id(0) == 0)
    def _():
        turned_ref[...] = left_ref[...].T
        d_left_ref[...] = jnp.zeros_like(d_left_ref)

    upstream = upstream_ref[...]
    grad = jnp.dot(turned_ref[...], upstream, preferred_element_type=jnp.float32)
    store_halves(grad, kept_ref, sent_ref)
    d_left_ref[...] += dot_last(upstream, weight_ref[...])


def product_back(left, upstream, weight):
    length, width = left.shape
    columns = weight.shape[1]
    block = 384
    fixed = pl.BlockSpec((length, width), lambda at: (0, 0))
    half = pl.BlockSpec((SHARDS // 2, width // SHARDS, block), lambda at: (0, 0, at))
    half_shape = jax.ShapeDtypeStruct((SHARDS // 2, width // SHARDS, columns), jnp.bfloat16)
    d_left, kept, sent = pl.pallas_call(
        product_back_kernel,
        grid=(columns // block,),
        out_shape=(
            jax.ShapeDtypeStruct((length, width), jnp.float32),
            half_shape,
            half_shape,
        ),
        in_specs=[
            fixed,
            pl.BlockSpec((length, block), lambda at: (0, at)),
            pl.BlockSpec((width, block), lambda at: (0, at)),
        ],
        out_specs=(fixed, half, half),
        scratch_shapes=[pltpu.VMEM((width, length), jnp.bfloat16)],
        compiler_params=pltpu.CompilerParams(vmem_limit_bytes=32 << 20),
        cost_estimate=SHORT,
    )(left, upstream, weight)
    return d_left, (kept, sent)


def mlp_kernel(
    hidden_ref, upstream_ref, up_ref, bias_ref, down_ref,
    branch_ref, d_hidden_ref, up_kept_ref, up_sent_ref, down_grad_ref, bias_grad_ref,
    turned_ref,
):
    @pl.when(pl.program_id(0) == 0)
    def _():
        turned_ref[...] = hidden_ref[...].T
        branch_ref[...] = jnp.zeros_like(branch_ref)
        d_hidden_ref[...] = jnp.zeros_like(d_hidden_ref)

    hidden = hidden_ref[...]
    upstream = upstream_ref[...]
    preact = (
        jnp.dot(hidden, up_ref[...], preferred_element_type=jnp.float32) + bias_ref[...]
    )
    square = preact * preact
    bent = jnp.tanh(GELU_RATE * preact * (1.0 + GELU_CUBE * square))
    half = 0.5 * (1.0 + bent)
    slope = half + (0.5 * GELU_RATE) * preact * (1.0 - bent * bent) * (
        1.0 + (3.0 * GELU_CUBE) * square
    )
    activated = (preact * half).astype(jnp.bfloat16)
    branch_ref[...] += jnp.dot(activated, down_ref[...], preferred_element_type=jnp.float32)
    d_preact = dot_last(upstream, down_ref[...]) * slope
    d_preact = d_preact.astype(jnp.bfloat16)
    bias_grad_ref[...] = jnp.sum(d_preact.astype(jnp.float32), 0, keepdims=True)
    down_grad_ref[...] = dot_first(activated, upstream).astype(jnp.bfloat16)
    d_hidden_ref[...] += dot_last(d_preact, up_ref[...])
    up_grad = jnp.dot(turned_ref[...], d_preact, preferred_element_type=jnp.float32)
    store_halves(up_grad, up_kept_ref, up_sent_ref)


def split_units(values, axis):
    span = values.shape[axis] // SHARDS // 2
    cuts = [lax.slice_in_dim(values, at * span, at * span + span, axis=axis) for at in range(16)]
    return [jnp.concatenate(cuts[half::2], axis=axis) for half in (0, 1)]


def join_units(halves):
    span = halves[0].shape[-1] // SHARDS
    cuts = [half[..., at * span : at * span + span] for at in range(SHARDS) for half in halves]
    return jnp.concatenate(cuts, axis=-1)


def mlp(hidden, upstream, up, bias, down):
    length, width = hidden.shape
    units = up.shape[1]
    block = 768
    fixed = pl.BlockSpec((length, width), lambda at: (0, 0))
    columns = pl.BlockSpec((width, block), lambda at: (0, at))
    lanes = pl.BlockSpec((1, block), lambda at: (0, at))
    rows = pl.BlockSpec((block, width), lambda at: (at, 0))
    half = pl.BlockSpec((SHARDS // 2, width // SHARDS, block), lambda at: (0, 0, at))
    half_shape = jax.ShapeDtypeStruct((SHARDS // 2, width // SHARDS, units), jnp.bfloat16)
    return pl.pallas_call(
        mlp_kernel,
        grid=(units // block,),
        out_shape=(
            jax.ShapeDtypeStruct((length, width), jnp.float32),
            jax.ShapeDtypeStruct((length, width), jnp.float32),
            half_shape,
            half_shape,
            jax.ShapeDtypeStruct(down.shape, jnp.bfloat16),
            jax.ShapeDtypeStruct((1, units), jnp.float32),
        ),
        in_specs=[fixed, fixed, columns, lanes, rows],
        out_specs=(fixed, fixed, half, half, rows, lanes),
        scratch_shapes=[pltpu.VMEM((width, length), jnp.bfloat16)],
        compiler_params=pltpu.CompilerParams(vmem_limit_bytes=58 << 20),
        cost_estimate=SHORT,
    )(hidden, upstream, up, bias, down)


def per_device(
    latent_in,
    condition,
    valid_slots,
    ada_weight,
    ada_bias,
    qkv_weight,
    qv_bias,
    out_weight,
    out_bias,
    up_weight,
    up_bias,
    down_weight,
    down_bias,
    cotangent,
):
    number, length, width = latent_in.shape
    place = place_of()
    fsdp_index = lax.axis_index("fsdp")
    held = (place >> 2) * 2 + (place & 1)
    rows = width // SHARDS
    replicas = lax.axis_size("rep")

    small = jnp.concatenate(
        [
            condition[0],
            qv_bias,
            out_bias,
            up_bias,
            down_bias,
            jnp.broadcast_to(valid_slots.astype(jnp.bfloat16), (128,)),
        ]
    )
    small_all = gather_group(small)
    up_halves = split_units(up_weight, 1)
    down_rows = down_weight.shape[0] // 2
    full_up = [lax.all_gather(half, GROUP, axis=0, tiled=True) for half in up_halves]
    full_down = [lax.all_gather(down_weight[:down_rows], GROUP, axis=0, tiled=True)]
    late_down = down_weight[down_rows:]
    side_by_side = jnp.concatenate([qkv_weight, out_weight], axis=1)
    small_all, side_by_side, latent_in = tie(small_all, side_by_side, latent_in)
    latent_low = swap_halves(latent_in)
    pieces, order = gather_pieces(side_by_side)
    pieces[3], late_down, cotangent = tie(pieces[3], late_down, cotangent)
    down_pieces, _ = gather_first(late_down)
    cotangent_low = swap_halves(cotangent)
    full_qkv, full_out = assemble(pieces, order, (3 * width, width))

    bounds = [0, width]
    for bias in (qv_bias, out_bias, up_bias, down_bias):
        bounds.append(bounds[-1] + bias.shape[0])
    cond_group = small_all[::2, :width].astype(jnp.float32)
    full_qv_bias, full_out_bias, full_up_bias, full_down_bias = (
        small_all[:, low:high].reshape(-1).astype(jnp.float32)
        for low, high in zip(bounds[1:-1], bounds[2:])
    )
    valid_group = small_all[::2, bounds[-1]].astype(jnp.float32)
    slot_mask = lax.dynamic_slice_in_dim(valid_group, held, 1)[:, None, None]

    silu_group = jax.nn.silu(cond_group).astype(jnp.bfloat16)
    silu_mine = lax.dynamic_slice_in_dim(silu_group, place * rows, rows, 1)
    ada_bias_row = lax.dynamic_update_slice_in_dim(
        jnp.zeros((ada_weight.shape[1],), jnp.float32),
        ada_bias.astype(jnp.float32),
        place * ada_bias.shape[0],
        0,
    )
    modulation = matmul(silu_mine, ada_weight) + ada_bias_row
    modulation, pieces[3] = tie(modulation, pieces[3])
    for bit, count in ((4, 2), (1, 1)):
        upper = (place & bit) != 0
        sent = jnp.where(upper, modulation[:count], modulation[count:])
        kept = jnp.where(upper, modulation[count:], modulation[:count])
        modulation = kept + permute(sent, lambda at: at ^ bit)
    modulation = modulation + permute(modulation, core_rule)
    shift_one, scale_one, gate_one, shift_two, scale_two, gate_two = jnp.split(
        modulation, 6, axis=-1
    )

    latent = latent_low[0].astype(jnp.float32)
    normed_one, inverse_one = normalize(latent)
    hidden_one = (normed_one * (1.0 + scale_one) + shift_one).astype(jnp.bfloat16)
    bias_full = jnp.concatenate(
        [full_qv_bias[:width], jnp.zeros((width,), jnp.float32), full_qv_bias[width:]]
    )
    projected = (matmul(hidden_one, full_qkv) + bias_full).astype(jnp.bfloat16)
    query = projected[:, :width]
    pair_own = projected[:, width:]
    pair_other = permute(pair_own, core_rule)
    heads = range(width // HEAD)
    halves = heads[: len(heads) // 2], heads[len(heads) // 2 :]
    query, down_pieces[1], down_pieces[2] = tie(query, down_pieces[1], down_pieces[2])
    down_pieces = gather_second(down_pieces)
    attended_low, log_totals = attend(query, pair_own, pair_other, heads)
    attended_low, down_pieces[3] = tie(attended_low, down_pieces[3])
    down_pieces = gather_third(down_pieces)
    log_rows = log_totals[:, : len(heads)].T[:, None, :]
    branch_one = matmul(attended_low, full_out) + full_out_bias
    middle = latent + gate_one * branch_one

    normed_two, inverse_two = normalize(middle)
    hidden_two = (normed_two * (1.0 + scale_two) + shift_two).astype(jnp.bfloat16)
    mask_row = slot_mask[0]
    d_out = cotangent_low[0].astype(jnp.float32) * mask_row
    d_branch_two = (gate_two * d_out).astype(jnp.bfloat16)
    full_down += assemble(down_pieces, order, (width,))
    bias_halves = split_units(full_up_bias[None], 1)
    parts, up_scatters, down_shards = [], [], []
    for half in (0, 1):
        branch, d_hidden, kept, sent, down_grad, bias_grad = mlp(
            hidden_two, d_branch_two, full_up[half], bias_halves[half], full_down[half]
        )
        if half == 1:
            branch, up_scatters[0].received = tie(branch, up_scatters[0].received)
            up_scatters[0].second()
        up_scatters.append(Scatter((kept, sent)))
        down_shards.append(
            lax.psum_scatter(down_grad, GROUP, scatter_dimension=0, tiled=True)
        )
        parts.append((branch, d_hidden, bias_grad))
    branch_two = parts[0][0] + parts[1][0] + full_down_bias
    d_hidden_two = parts[0][1] + parts[1][1]
    block_out = (mask_row * (middle + gate_two * branch_two)).astype(jnp.bfloat16)
    d_gate_two = jnp.sum(d_out * branch_two, axis=0)
    down_bias_grad = jnp.sum(d_branch_two.astype(jnp.float32), axis=0)
    up_bias_grad = join_units([part[2] for part in parts])[0]
    d_shift_two = jnp.sum(d_hidden_two, axis=0)
    d_scale_two = jnp.sum(d_hidden_two * normed_two, axis=0)
    d_middle = d_out + norm_back(d_hidden_two * (1.0 + scale_two), normed_two, inverse_two)
    d_gate_one = jnp.sum(d_middle * branch_one, axis=0)
    d_branch_one = (gate_one * d_middle).astype(jnp.bfloat16)

    d_attended, out_halves = product_back(attended_low, d_branch_one, full_out)
    d_attended = d_attended.astype(jnp.bfloat16)
    out_scatter = Scatter(out_halves)
    out_bias_grad = jnp.sum(d_branch_one.astype(jnp.float32), axis=0)
    d_attended, up_scatters[0].received, up_scatters[1].received = tie(
        d_attended, up_scatters[0].received, up_scatters[1].received
    )
    up_scatters[1].second()
    up_scatters[0].third()
    left = attend_back(query, pair_own, pair_other, d_attended, log_rows, halves[0])
    d_query, d_attended, out_scatter.received, down_shards[0] = tie(
        left[0], d_attended, out_scatter.received, down_shards[0]
    )
    out_scatter.second()
    right = attend_back(query, pair_own, pair_other, d_attended, log_rows, halves[1])
    *right, up_scatters[1].received, down_shards[1] = tie(
        *right, up_scatters[1].received, down_shards[1]
    )
    up_scatters[1].third()
    d_query = join_heads(d_query, right[0], width)
    d_own = join_heads(left[1], right[1], width)
    d_other = permute(join_heads(left[2], right[2], width), core_rule)
    d_own = (d_own + d_other.astype(jnp.float32)).astype(jnp.bfloat16)
    d_projected = jnp.concatenate([d_query, d_own[0], d_own[1]], axis=-1)

    down_total = lax.psum(jnp.concatenate(down_shards), "rep")
    d_hidden_one, qkv_halves = product_back(hidden_one, d_projected, full_qkv)
    qkv_scatter = Scatter(qkv_halves)
    column_sums = jnp.sum(d_projected.astype(jnp.float32), axis=0)
    d_hidden_one, *arrived = tie(
        d_hidden_one,
        qkv_scatter.received,
        up_scatters[0].received,
        up_scatters[1].received,
        out_scatter.received,
    )
    for scatter, received in zip((qkv_scatter, *up_scatters, out_scatter), arrived):
        scatter.received = received
    qkv_scatter.second()
    up_sum = ReplicaSum(
        jnp.concatenate([scatter.result() for scatter in up_scatters], axis=1), replicas
    )
    out_scatter.third()
    d_shift_one = jnp.sum(d_hidden_one, axis=0)
    d_scale_one = jnp.sum(d_hidden_one * normed_one, axis=0)
    latent_grad = d_middle + norm_back(d_hidden_one * (1.0 + scale_one), normed_one, inverse_one)
    bias_grads = (
        jnp.concatenate([column_sums[:width], column_sums[2 * width :]]),
        out_bias_grad,
        up_bias_grad,
        down_bias_grad,
    )
    sums = [d_shift_one, d_scale_one, d_gate_one, d_shift_two, d_scale_two, d_gate_two]
    ada_width = 6 * width
    small_sums = jnp.concatenate(sums + list(bias_grads))
    qkv_scatter.received, out_scatter.received = tie(
        qkv_scatter.received, out_scatter.received
    )
    qkv_scatter.third()
    qkv_shard, *up_sum.received = tie(qkv_scatter.result(), *up_sum.received)
    qkv_shard, latent_grad, block_out, small_sums = tie(
        qkv_shard, latent_grad.astype(jnp.bfloat16), block_out, small_sums
    )
    late_sum = ReplicaSum(
        jnp.concatenate([out_scatter.result(), qkv_shard], axis=1), replicas
    )
    latent_grad = swap_halves(latent_grad[None]).astype(jnp.float32)
    block_out = swap_halves(block_out[None])
    sums_all = gather_group(small_sums)
    up_sum.second()
    down_total, *late_sum.received = tie(down_total, *late_sum.received)
    late_sum.second()
    *up_sum.received, late_sum.received[0] = tie(*up_sum.received, late_sum.received[0])
    up_total = up_sum.result()
    up_total = join_units(jnp.split(up_total, 2, axis=1))
    late_total = late_sum.result()
    out_total, qkv_total = late_total[:, :width], late_total[:, width:]

    d_group = sums_all[:, :ada_width].reshape(2, 2, 2, ada_width).sum(1).reshape(4, ada_width)
    bias_mine = []
    start = ada_width
    for grad in bias_grads:
        total = jnp.sum(sums_all[:, start : start + grad.shape[0]], axis=0)
        piece = grad.shape[0] // SHARDS
        bias_mine.append(lax.dynamic_slice_in_dim(total, place * piece, piece))
        start += grad.shape[0]
    d_silu = lax.dot_general(
        d_group,
        ada_weight.astype(jnp.float32),
        (((1,), (1,)), ((), ())),
        precision=exact_mode,
    )
    cond_mine = lax.dynamic_slice_in_dim(cond_group, place * rows, rows, 1)
    cond_part = jax.vjp(jax.nn.silu, cond_mine)[1](d_silu)[0]
    cond_all = gather_group(cond_part)
    cond_grad = lax.dynamic_index_in_dim(cond_all, fsdp_index, 1, keepdims=False)
    cond_grad = cond_grad.reshape(1, width)

    packed = jnp.concatenate(
        [d_group.reshape(-1), silu_mine.astype(jnp.float32).reshape(-1)] + bias_mine
    )
    packed_all = gather_replicas(packed, replicas)
    d_all = packed_all[:, : 4 * ada_width].reshape(-1, ada_width)
    silu_all = packed_all[:, 4 * ada_width : 4 * ada_width + 4 * rows].reshape(-1, rows)
    ada_total = lax.dot_general(
        silu_all, d_all, (((0,), (0,)), ((), ())), precision=exact_mode
    )
    ada_bias_total = jnp.sum(
        lax.dynamic_slice_in_dim(d_all, place * ada_bias.shape[0], ada_bias.shape[0], 1), axis=0
    )
    bias_totals = jnp.sum(packed_all[:, 4 * ada_width + 4 * rows :], axis=0)
    cuts = [0]
    for piece in bias_mine:
        cuts.append(cuts[-1] + piece.shape[0])
    qv_total, out_bias_total, up_bias_total, down_bias_total = (
        bias_totals[low:high] for low, high in zip(cuts[:-1], cuts[1:])
    )
    return (
        block_out,
        latent_grad,
        cond_grad,
        ada_total,
        ada_bias_total,
        qkv_total.astype(jnp.float32),
        qv_total,
        out_total.astype(jnp.float32),
        out_bias_total,
        up_total.astype(jnp.float32),
        up_bias_total,
        down_total.astype(jnp.float32),
        down_bias_total,
    )


def solution(mesh):
    tokens = P(("rep", "fsdp"), "sp", None)
    rows = P(("rep", "fsdp"), None)
    matrix = P(GROUP, None)
    vector = P(GROUP)
    weights = (matrix, vector) * 5
    return jax.shard_map(
        per_device,
        mesh=mesh,
        in_specs=(tokens, rows, P(("rep", "fsdp"))) + weights + (tokens,),
        out_specs=(tokens, tokens, rows) + weights,
        check_vma=False,
    )
```

```python
import functools

import jax
import jax.numpy as jnp
from jax import lax
from jax.experimental import pallas as pl
from jax.experimental.pallas import tpu as pltpu
from jax.sharding import PartitionSpec as P

HEAD = 72
GROUP = ("fsdp", "sp")
SHARDS = 8

exact_mode = lax.Precision.HIGHEST
epsilon = 1e-06


def normalize(values):
    average = jnp.mean(values, -1, keepdims=True)
    centered = values - average
    inverse = lax.rsqrt(jnp.mean(centered * centered, -1, keepdims=True) + epsilon)
    return (centered * inverse, inverse)


def norm_back(upstream, normed, inverse):
    return (
        upstream
        - jnp.mean(upstream, -1, keepdims=True)
        - normed * jnp.mean(upstream * normed, -1, keepdims=True)
    ) * inverse


def matmul(left, right):
    return jnp.dot(left, right, preferred_element_type=jnp.float32)


def place_of():
    return lax.axis_index("fsdp") * 2 + lax.axis_index("sp")


def pairs_by(rule):
    return [(place, rule(place)) for place in range(SHARDS)]


def swap_rule(place):
    return (place & 4) | ((place & 1) << 1) | ((place >> 1) & 1)


def core_rule(place):
    return place ^ 2


def first_rule(place):
    return place ^ (1 if place & 2 else 4)


def second_rule(place):
    return place ^ (4 if place & 2 else 1)


def permute(values, rule):
    return lax.ppermute(values, GROUP, pairs_by(rule))


def swap_halves(values):
    place = place_of()
    pairs = [pair for pair in pairs_by(swap_rule) if pair[0] != pair[1]]
    received = lax.ppermute(values, GROUP, pairs)
    stays = ((place >> 1) & 1) == (place & 1)
    return jnp.where(stays, values, received)


def gather_group(values):
    place = place_of()
    stacked = values[None]
    for bit in (1, 2, 4):
        received = permute(stacked, lambda at: at ^ bit)
        stacked = jnp.where(
            (place & bit) == 0,
            jnp.concatenate([stacked, received]),
            jnp.concatenate([received, stacked]),
        )
    return stacked


def gather_replicas(values, replicas):
    stacked = [values]
    for shift in range(1, replicas):
        pairs = [(at, (at + shift) % replicas) for at in range(replicas)]
        stacked.append(lax.ppermute(values, "rep", pairs))
    return jnp.stack(stacked)


def assemble_kernel(widths, order_ref, *refs):
    pieces, wholes = refs[:SHARDS], refs[SHARDS : SHARDS + len(widths)]
    buffer, load_sems, store_sems = refs[SHARDS + len(widths) :]
    rows = buffer.shape[1]
    loads = [
        pltpu.make_async_copy(piece, buffer.at[at], load_sems.at[at])
        for at, piece in enumerate(pieces)
    ]
    for load in loads:
        load.start()
    stores = []
    for at, load in enumerate(loads):
        load.wait()
        target = pl.ds(pl.multiple_of(order_ref[at] * rows, 16), rows)
        start = 0
        for which, width in enumerate(widths):
            store = pltpu.make_async_copy(
                buffer.at[at, :, pl.ds(start, width)],
                wholes[which].at[target],
                store_sems.at[which, at],
            )
            store.start()
            stores.append(store)
            start += width
    for store in stores:
        store.wait()


def assemble(pieces, order, widths):
    rows, columns = pieces[0].shape
    size = SHARDS * rows * columns * 2
    return pl.pallas_call(
        functools.partial(assemble_kernel, widths),
        out_shape=[
            jax.ShapeDtypeStruct((SHARDS * rows, width), pieces[0].dtype) for width in widths
        ],
        in_specs=[pl.BlockSpec(memory_space=pltpu.SMEM)]
        + [pl.BlockSpec(memory_space=pl.ANY)] * SHARDS,
        out_specs=[pl.BlockSpec(memory_space=pl.ANY)] * len(widths),
        scratch_shapes=[
            pltpu.VMEM((SHARDS, rows, columns), pieces[0].dtype),
            pltpu.SemaphoreType.DMA((SHARDS,)),
            pltpu.SemaphoreType.DMA((len(widths), SHARDS)),
        ],
        compiler_params=pltpu.CompilerParams(vmem_limit_bytes=size + (4 << 20)),
        cost_estimate=SHORT,
    )(order, *pieces)


def gather_pieces(shard):
    place = place_of()
    near = jnp.where((place & 2) == 0, 4, 1)
    far = 5 - near
    other = place ^ 2
    first = permute(shard, first_rule)
    second = permute(shard, second_rule)
    both = permute(first, second_rule)
    held = [shard, first, second, both]
    pieces = held + [permute(piece, core_rule) for piece in held]
    order = [place, place ^ near, place ^ far, place ^ 5]
    order += [other, other ^ far, other ^ near, other ^ 5]
    return pieces, jnp.stack(order).astype(jnp.int32)


def tie(*values):
    return lax.optimization_barrier(values)


class Scatter:
    def __init__(self, halves):
        self.place = place_of()
        self.core = (self.place >> 1) & 1
        self.kept, sent = halves
        self.low = sent.dtype
        self.received = permute(sent, core_rule)

    def second(self):
        kept = self.kept.astype(jnp.float32) + self.received.astype(jnp.float32)
        kept = kept.astype(self.low)
        mine = ((self.place >> 2) << 1) | (self.place & 1)
        near = jnp.where(self.core == 0, 2, 1)

        def pair(which):
            parts = [which, which ^ 3 ^ near]
            return jnp.concatenate([lax.dynamic_slice_in_dim(kept, at, 1, 0) for at in parts])

        self.kept = pair(mine)
        self.received = permute(pair(mine ^ near), first_rule)

    def third(self):
        kept = self.kept.astype(jnp.float32) + self.received.astype(jnp.float32)
        self.kept = kept[0]
        self.received = permute(kept[1].astype(self.low), second_rule)

    def result(self):
        return self.kept + self.received.astype(jnp.float32)


class ReplicaSum:
    def __init__(self, partial, replicas):
        self.replicas = replicas
        self.own = lax.axis_index("rep")
        self.shape = partial.shape
        self.span = partial.shape[1] // replicas
        low = partial.astype(jnp.bfloat16)
        self.kept = self.piece(partial, self.own)
        self.received = [
            self.send(self.piece(low, self.own + shift), shift) for shift in range(1, replicas)
        ]

    def piece(self, values, which):
        return lax.dynamic_slice_in_dim(values, which % self.replicas * self.span, self.span, 1)

    def send(self, values, shift):
        pairs = [(at, (at + shift) % self.replicas) for at in range(self.replicas)]
        return lax.ppermute(values, "rep", pairs)

    def second(self):
        total = self.kept
        for received in self.received:
            total = total + received.astype(jnp.float32)
        low = total.astype(jnp.bfloat16)
        self.received = [low] + [self.send(low, shift) for shift in range(1, self.replicas)]

    def result(self):
        whole = jnp.zeros(self.shape, jnp.float32)
        for shift, received in enumerate(self.received):
            start = (self.own - shift) % self.replicas * self.span
            whole = lax.dynamic_update_slice_in_dim(whole, received.astype(jnp.float32), start, 1)
        return whole


WINDOW = 256
GELU_RATE = 0.7978845608028654
GELU_CUBE = 0.044715
SHORT = pl.CostEstimate(flops=1 << 20, bytes_accessed=1 << 20, transcendentals=0)


def head_lanes(heads, width):
    low = heads[0] * HEAD // 128 * 128
    high = -(-(heads[-1] + 1) * HEAD // 128) * 128
    return min(low, width - WINDOW), high


def head_window(first_head, width, base):
    first = (first_head + pl.program_id(0)) * HEAD
    start = jnp.minimum(first // 128 * 128, width - WINDOW)
    start = pl.multiple_of(start, 128)
    lane = lax.broadcasted_iota(jnp.int32, (1, WINDOW), 1) + start
    inside = (lane >= first) & (lane < first + HEAD)
    mask = jnp.where(inside, 1.0, 0.0).astype(jnp.bfloat16)
    lanes = [pl.ds(pl.multiple_of(start + at, 128), WINDOW) for at in (0, width, -base)]
    return (*lanes, mask)


def dot_last(left, right):
    return lax.dot_general(
        left, right, (((1,), (1,)), ((), ())), preferred_element_type=jnp.float32
    )


def dot_first(left, right):
    return lax.dot_general(
        left, right, (((0,), (0,)), ((), ())), preferred_element_type=jnp.float32
    )


def attend_kernel(first_head, base, query_ref, own_ref, other_ref, out_ref, log_ref, total_ref):
    length, width = query_ref.shape
    head = pl.program_id(0)
    key_lanes, value_lanes, out_lanes, mask = head_window(first_head, width, base)
    score_scale = float(HEAD) ** (-0.5)

    @pl.when(head == 0)
    def _():
        total_ref[...] = jnp.zeros_like(total_ref)
        log_ref[...] = jnp.zeros_like(log_ref)

    keys = jnp.concatenate([own_ref[:, key_lanes], other_ref[:, key_lanes]]) * mask
    values = jnp.concatenate([own_ref[:, value_lanes], other_ref[:, value_lanes]]) * mask
    rows = min(256, length)
    for at in range(0, length, rows):
        block = pl.ds(at, rows)
        scores = dot_last(query_ref[block, key_lanes], keys)
        row_max = jnp.max(scores, -1, keepdims=True)
        weights = jnp.exp((scores - row_max) * score_scale)
        row_total = jnp.sum(weights, -1, keepdims=True)
        probs = (weights * (1.0 / row_total)).astype(jnp.bfloat16)
        total_ref[block, out_lanes] += jnp.dot(
            probs, values, preferred_element_type=jnp.float32
        )
        log_total = row_max * score_scale + jnp.log(row_total)
        lane = lax.broadcasted_iota(jnp.int32, (rows, 128), 1)
        log_ref[block, :] = jnp.where(lane == first_head + head, log_total, log_ref[block, :])

    @pl.when(head == pl.num_programs(0) - 1)
    def _():
        out_ref[...] = total_ref[...].astype(out_ref.dtype)


def attend(query, own, other, heads):
    length, width = query.shape
    low, high = head_lanes(heads, width)
    return pl.pallas_call(
        functools.partial(attend_kernel, heads[0], low),
        grid=(len(heads),),
        out_shape=(
            jax.ShapeDtypeStruct((length, high - low), jnp.bfloat16),
            jax.ShapeDtypeStruct((length, 128), jnp.float32),
        ),
        in_specs=[
            pl.BlockSpec((length, width), lambda head: (0, 0)),
            pl.BlockSpec(own.shape, lambda head: (0, 0)),
            pl.BlockSpec(other.shape, lambda head: (0, 0)),
        ],
        out_specs=(
            pl.BlockSpec((length, high - low), lambda head: (0, 0)),
            pl.BlockSpec((length, 128), lambda head: (0, 0)),
        ),
        scratch_shapes=[pltpu.VMEM((length, high - low), jnp.float32)],
        compiler_params=pltpu.CompilerParams(vmem_limit_bytes=48 << 20),
        cost_estimate=SHORT,
    )(query, own, other)


def attend_back_kernel(
    first_head, base, query_ref, own_ref, other_ref, upstream_ref, log_ref, d_query_ref, d_own_ref, d_other_ref,
    query_total, key_total, value_total,
):
    length, width = query_ref.shape
    head = pl.program_id(0)
    key_lanes, value_lanes, out_lanes, mask = head_window(first_head, width, base)
    score_scale = float(HEAD) ** (-0.5)

    @pl.when(head == 0)
    def _():
        query_total[...] = jnp.zeros_like(query_total)
        key_total[...] = jnp.zeros_like(key_total)
        value_total[...] = jnp.zeros_like(value_total)

    keys = jnp.concatenate([own_ref[:, key_lanes], other_ref[:, key_lanes]]) * mask
    values = jnp.concatenate([own_ref[:, value_lanes], other_ref[:, value_lanes]]) * mask
    rows = min(256, length)
    for at in range(0, length, rows):
        block = pl.ds(at, rows)
        query = query_ref[block, key_lanes] * mask
        upstream = upstream_ref[block, key_lanes] * mask
        scores = dot_last(keys, query)
        probs = jnp.exp(scores * score_scale - log_ref[0, :, block])
        d_probs = dot_last(values, upstream)
        weighted = probs * d_probs
        row_sum = jnp.sum(weighted, 0, keepdims=True)
        d_scores = (weighted - probs * row_sum).astype(jnp.bfloat16)
        value_total[:, out_lanes] += jnp.dot(
            probs.astype(jnp.bfloat16), upstream, preferred_element_type=jnp.float32
        )
        key_total[:, out_lanes] += score_scale * jnp.dot(
            d_scores, query, preferred_element_type=jnp.float32
        )
        query_total[block, out_lanes] += dot_first(d_scores, keys)

    @pl.when(head == pl.num_programs(0) - 1)
    def _():
        d_query_ref[...] = (query_total[...] * score_scale).astype(d_query_ref.dtype)
        for at, total in enumerate((key_total, value_total)):
            d_own_ref[at] = total[: own_ref.shape[0]]
            d_other_ref[at] = total[own_ref.shape[0] :].astype(d_other_ref.dtype)


def attend_back(query, own, other, upstream, log_totals, heads):
    length, width = query.shape
    low, high = head_lanes(heads, width)
    span = high - low
    whole = lambda head: (0, 0)
    halves = pl.BlockSpec((2, own.shape[0], span), lambda head: (0, 0, 0))
    return pl.pallas_call(
        functools.partial(attend_back_kernel, heads[0], low),
        grid=(len(heads),),
        out_shape=(
            jax.ShapeDtypeStruct((length, span), jnp.bfloat16),
            jax.ShapeDtypeStruct((2, own.shape[0], span), jnp.float32),
            jax.ShapeDtypeStruct((2, other.shape[0], span), jnp.bfloat16),
        ),
        in_specs=[
            pl.BlockSpec((length, width), whole),
            pl.BlockSpec(own.shape, whole),
            pl.BlockSpec(other.shape, whole),
            pl.BlockSpec((length, width), whole),
            pl.BlockSpec((1, 1, length), lambda head: (heads[0] + head, 0, 0)),
        ],
        out_specs=(pl.BlockSpec((length, span), whole), halves, halves),
        scratch_shapes=[
            pltpu.VMEM((length, span), jnp.float32),
            pltpu.VMEM((own.shape[0] + other.shape[0], span), jnp.float32),
            pltpu.VMEM((own.shape[0] + other.shape[0], span), jnp.float32),
        ],
        compiler_params=pltpu.CompilerParams(vmem_limit_bytes=56 << 20),
        cost_estimate=SHORT,
    )(query, own, other, upstream, log_totals)


def join_heads(left, right, width):
    shared = left.shape[-1] + right.shape[-1] - width
    if shared == 0:
        return jnp.concatenate([left, right], axis=-1)
    edge = left.shape[-1] - shared
    middle = left[..., edge:] + right[..., :shared]
    return jnp.concatenate([left[..., :edge], middle, right[..., shared:]], axis=-1)


def store_halves(grad, kept_ref, sent_ref):
    core = lax.axis_index("fsdp") % 2
    rows = grad.shape[0] // SHARDS
    low = grad.astype(kept_ref.dtype)
    for owner in (0, 1):
        blocks = [at for at in range(SHARDS) if (at >> 1) & 1 == owner]

        @pl.when(core == owner)
        def _():
            for slot, at in enumerate(blocks):
                kept_ref[slot] = low[at * rows : (at + 1) * rows]

        @pl.when(core != owner)
        def _():
            for slot, at in enumerate(blocks):
                sent_ref[slot] = low[at * rows : (at + 1) * rows]


def product_back_kernel(
    left_ref, upstream_ref, weight_ref, d_left_ref, kept_ref, sent_ref, turned_ref
):
    @pl.when(pl.program_id(0) == 0)
    def _():
        turned_ref[...] = left_ref[...].T
        d_left_ref[...] = jnp.zeros_like(d_left_ref)

    upstream = upstream_ref[...]
    grad = jnp.dot(turned_ref[...], upstream, preferred_element_type=jnp.float32)
    store_halves(grad, kept_ref, sent_ref)
    d_left_ref[...] += dot_last(upstream, weight_ref[...])


def product_back(left, upstream, weight):
    length, width = left.shape
    columns = weight.shape[1]
    block = 384
    fixed = pl.BlockSpec((length, width), lambda at: (0, 0))
    half = pl.BlockSpec((SHARDS // 2, width // SHARDS, block), lambda at: (0, 0, at))
    half_shape = jax.ShapeDtypeStruct((SHARDS // 2, width // SHARDS, columns), jnp.bfloat16)
    d_left, kept, sent = pl.pallas_call(
        product_back_kernel,
        grid=(columns // block,),
        out_shape=(
            jax.ShapeDtypeStruct((length, width), jnp.float32),
            half_shape,
            half_shape,
        ),
        in_specs=[
            fixed,
            pl.BlockSpec((length, block), lambda at: (0, at)),
            pl.BlockSpec((width, block), lambda at: (0, at)),
        ],
        out_specs=(fixed, half, half),
        scratch_shapes=[pltpu.VMEM((width, length), jnp.bfloat16)],
        compiler_params=pltpu.CompilerParams(vmem_limit_bytes=32 << 20),
        cost_estimate=SHORT,
    )(left, upstream, weight)
    return d_left, (kept, sent)


def mlp_kernel(
    hidden_ref, upstream_ref, up_ref, bias_ref, down_ref,
    branch_ref, d_hidden_ref, up_kept_ref, up_sent_ref, down_grad_ref, bias_grad_ref,
    turned_ref,
):
    @pl.when(pl.program_id(0) == 0)
    def _():
        turned_ref[...] = hidden_ref[...].T
        branch_ref[...] = jnp.zeros_like(branch_ref)
        d_hidden_ref[...] = jnp.zeros_like(d_hidden_ref)

    hidden = hidden_ref[...]
    upstream = upstream_ref[...]
    preact = (
        jnp.dot(hidden, up_ref[...], preferred_element_type=jnp.float32) + bias_ref[...]
    )
    square = preact * preact
    bent = jnp.tanh(GELU_RATE * preact * (1.0 + GELU_CUBE * square))
    half = 0.5 * (1.0 + bent)
    slope = half + (0.5 * GELU_RATE) * preact * (1.0 - bent * bent) * (
        1.0 + (3.0 * GELU_CUBE) * square
    )
    activated = (preact * half).astype(jnp.bfloat16)
    branch_ref[...] += jnp.dot(activated, down_ref[...], preferred_element_type=jnp.float32)
    d_preact = dot_last(upstream, down_ref[...]) * slope
    d_preact = d_preact.astype(jnp.bfloat16)
    bias_grad_ref[...] = jnp.sum(d_preact.astype(jnp.float32), 0, keepdims=True)
    down_grad_ref[...] = dot_first(activated, upstream).astype(jnp.bfloat16)
    d_hidden_ref[...] += dot_last(d_preact, up_ref[...])
    up_grad = jnp.dot(turned_ref[...], d_preact, preferred_element_type=jnp.float32)
    store_halves(up_grad, up_kept_ref, up_sent_ref)


def mlp(hidden, upstream, up, bias, down):
    length, width = hidden.shape
    units = up.shape[1]
    block = 512
    fixed = pl.BlockSpec((length, width), lambda at: (0, 0))
    columns = pl.BlockSpec((width, block), lambda at: (0, at))
    lanes = pl.BlockSpec((1, block), lambda at: (0, at))
    rows = pl.BlockSpec((block, width), lambda at: (at, 0))
    half = pl.BlockSpec((SHARDS // 2, width // SHARDS, block), lambda at: (0, 0, at))
    half_shape = jax.ShapeDtypeStruct((SHARDS // 2, width // SHARDS, units), jnp.bfloat16)
    return pl.pallas_call(
        mlp_kernel,
        grid=(units // block,),
        out_shape=(
            jax.ShapeDtypeStruct((length, width), jnp.float32),
            jax.ShapeDtypeStruct((length, width), jnp.float32),
            half_shape,
            half_shape,
            jax.ShapeDtypeStruct(down.shape, jnp.bfloat16),
            jax.ShapeDtypeStruct((1, units), jnp.float32),
        ),
        in_specs=[fixed, fixed, columns, lanes, rows],
        out_specs=(fixed, fixed, half, half, rows, lanes),
        scratch_shapes=[pltpu.VMEM((width, length), jnp.bfloat16)],
        compiler_params=pltpu.CompilerParams(vmem_limit_bytes=56 << 20),
        cost_estimate=SHORT,
    )(hidden, upstream, up, bias, down)


def per_device(
    latent_in,
    condition,
    valid_slots,
    ada_weight,
    ada_bias,
    qkv_weight,
    qv_bias,
    out_weight,
    out_bias,
    up_weight,
    up_bias,
    down_weight,
    down_bias,
    cotangent,
):
    number, length, width = latent_in.shape
    place = place_of()
    fsdp_index = lax.axis_index("fsdp")
    held = (place >> 2) * 2 + (place & 1)
    rows = width // SHARDS
    replicas = lax.axis_size("rep")

    small = jnp.concatenate(
        [
            condition[0],
            qv_bias,
            out_bias,
            up_bias,
            down_bias,
            jnp.broadcast_to(valid_slots.astype(jnp.bfloat16), (128,)),
        ]
    )
    small_all = gather_group(small)
    latent_low = swap_halves(latent_in)
    pieces, order = gather_pieces(jnp.concatenate([qkv_weight, out_weight], axis=1))
    full_up = lax.all_gather(up_weight, GROUP, axis=0, tiled=True)
    cotangent_low = swap_halves(cotangent)
    full_qkv, full_out = assemble(pieces, order, (3 * width, width))
    full_down = lax.all_gather(down_weight, GROUP, axis=0, tiled=True)

    bounds = [0, width]
    for bias in (qv_bias, out_bias, up_bias, down_bias):
        bounds.append(bounds[-1] + bias.shape[0])
    cond_group = small_all[::2, :width].astype(jnp.float32)
    full_qv_bias, full_out_bias, full_up_bias, full_down_bias = (
        small_all[:, low:high].reshape(-1).astype(jnp.float32)
        for low, high in zip(bounds[1:-1], bounds[2:])
    )
    valid_group = small_all[::2, bounds[-1]].astype(jnp.float32)
    slot_mask = lax.dynamic_slice_in_dim(valid_group, held, 1)[:, None, None]

    silu_group = jax.nn.silu(cond_group).astype(jnp.bfloat16)
    silu_mine = lax.dynamic_slice_in_dim(silu_group, place * rows, rows, 1)
    ada_bias_row = lax.dynamic_update_slice_in_dim(
        jnp.zeros((ada_weight.shape[1],), jnp.float32),
        ada_bias.astype(jnp.float32),
        place * ada_bias.shape[0],
        0,
    )
    modulation = matmul(silu_mine, ada_weight) + ada_bias_row
    for bit, count in ((4, 2), (1, 1)):
        upper = (place & bit) != 0
        sent = jnp.where(upper, modulation[:count], modulation[count:])
        kept = jnp.where(upper, modulation[count:], modulation[:count])
        modulation = kept + permute(sent, lambda at: at ^ bit)
    modulation = modulation + permute(modulation, core_rule)
    shift_one, scale_one, gate_one, shift_two, scale_two, gate_two = jnp.split(
        modulation, 6, axis=-1
    )

    latent = latent_low[0].astype(jnp.float32)
    normed_one, inverse_one = normalize(latent)
    hidden_one = (normed_one * (1.0 + scale_one) + shift_one).astype(jnp.bfloat16)
    bias_full = jnp.concatenate(
        [full_qv_bias[:width], jnp.zeros((width,), jnp.float32), full_qv_bias[width:]]
    )
    projected = (matmul(hidden_one, full_qkv) + bias_full).astype(jnp.bfloat16)
    query = projected[:, :width]
    pair_own = projected[:, width:]
    pair_other = permute(pair_own, core_rule)
    heads = range(width // HEAD)
    halves = heads[: len(heads) // 2], heads[len(heads) // 2 :]
    attended_low, log_totals = attend(query, pair_own, pair_other, heads)
    log_rows = log_totals[:, : len(heads)].T[:, None, :]
    branch_one = matmul(attended_low, full_out) + full_out_bias
    middle = latent + gate_one * branch_one

    normed_two, inverse_two = normalize(middle)
    hidden_two = (normed_two * (1.0 + scale_two) + shift_two).astype(jnp.bfloat16)
    mask_row = slot_mask[0]
    d_out = cotangent_low[0].astype(jnp.float32) * mask_row
    d_branch_two = (gate_two * d_out).astype(jnp.bfloat16)
    branch_two, d_hidden_two, up_kept, up_sent, down_grad, up_bias_grad = mlp(
        hidden_two, d_branch_two, full_up, full_up_bias[None], full_down
    )
    up_scatter = Scatter((up_kept, up_sent))
    down_shard = lax.psum_scatter(down_grad, GROUP, scatter_dimension=0, tiled=True)
    branch_two = branch_two + full_down_bias
    block_out = (mask_row * (middle + gate_two * branch_two)).astype(jnp.bfloat16)
    d_gate_two = jnp.sum(d_out * branch_two, axis=0)
    down_bias_grad = jnp.sum(d_branch_two.astype(jnp.float32), axis=0)
    up_bias_grad = up_bias_grad[0]
    d_shift_two = jnp.sum(d_hidden_two, axis=0)
    d_scale_two = jnp.sum(d_hidden_two * normed_two, axis=0)
    d_middle = d_out + norm_back(d_hidden_two * (1.0 + scale_two), normed_two, inverse_two)
    d_gate_one = jnp.sum(d_middle * branch_one, axis=0)
    d_branch_one = (gate_one * d_middle).astype(jnp.bfloat16)

    d_attended, out_halves = product_back(attended_low, d_branch_one, full_out)
    d_attended = d_attended.astype(jnp.bfloat16)
    out_scatter = Scatter(out_halves)
    out_bias_grad = jnp.sum(d_branch_one.astype(jnp.float32), axis=0)
    d_attended, up_scatter.received = tie(d_attended, up_scatter.received)
    up_scatter.second()
    left = attend_back(query, pair_own, pair_other, d_attended, log_rows, halves[0])
    d_query, d_attended, out_scatter.received = tie(left[0], d_attended, out_scatter.received)
    out_scatter.second()
    right = attend_back(query, pair_own, pair_other, d_attended, log_rows, halves[1])
    *right, up_scatter.received = tie(*right, up_scatter.received)
    up_scatter.third()
    d_query = join_heads(d_query, right[0], width)
    d_own = join_heads(left[1], right[1], width)
    d_other = permute(join_heads(left[2], right[2], width), core_rule)
    d_own = (d_own + d_other.astype(jnp.float32)).astype(jnp.bfloat16)
    d_projected = jnp.concatenate([d_query, d_own[0], d_own[1]], axis=-1)

    d_projected, down_shard, up_scatter.received = tie(
        d_projected, down_shard, up_scatter.received
    )
    down_total = lax.psum(down_shard, "rep")
    up_sum = ReplicaSum(up_scatter.result(), replicas)
    d_hidden_one, qkv_halves = product_back(hidden_one, d_projected, full_qkv)
    qkv_scatter = Scatter(qkv_halves)
    column_sums = jnp.sum(d_projected.astype(jnp.float32), axis=0)
    d_hidden_one, qkv_scatter.received, out_scatter.received = tie(
        d_hidden_one, qkv_scatter.received, out_scatter.received
    )
    qkv_scatter.second()
    out_scatter.third()
    d_shift_one = jnp.sum(d_hidden_one, axis=0)
    d_scale_one = jnp.sum(d_hidden_one * normed_one, axis=0)
    latent_grad = d_middle + norm_back(d_hidden_one * (1.0 + scale_one), normed_one, inverse_one)
    bias_grads = (
        jnp.concatenate([column_sums[:width], column_sums[2 * width :]]),
        out_bias_grad,
        up_bias_grad,
        down_bias_grad,
    )
    sums = [d_shift_one, d_scale_one, d_gate_one, d_shift_two, d_scale_two, d_gate_two]
    ada_width = 6 * width
    small_sums = jnp.concatenate(sums + list(bias_grads))
    qkv_scatter.received, out_scatter.received, down_total, *up_sum.received = tie(
        qkv_scatter.received, out_scatter.received, down_total, *up_sum.received
    )
    qkv_scatter.third()
    qkv_shard = qkv_scatter.result()
    qkv_shard, latent_grad, block_out, small_sums, *up_sum.received = tie(
        qkv_shard, latent_grad.astype(jnp.bfloat16), block_out, small_sums, *up_sum.received
    )
    late_sum = ReplicaSum(
        jnp.concatenate([out_scatter.result(), qkv_shard], axis=1), replicas
    )
    latent_grad = swap_halves(latent_grad[None]).astype(jnp.float32)
    block_out = swap_halves(block_out[None])
    sums_all = gather_group(small_sums)
    up_sum.second()
    *late_sum.received, sums_all = tie(*late_sum.received, sums_all)
    late_sum.second()
    late_sum.received[0], *up_sum.received = tie(late_sum.received[0], *up_sum.received)
    up_total = up_sum.result()
    late_total = late_sum.result()
    out_total, qkv_total = late_total[:, :width], late_total[:, width:]

    d_group = sums_all[:, :ada_width].reshape(2, 2, 2, ada_width).sum(1).reshape(4, ada_width)
    bias_mine = []
    start = ada_width
    for grad in bias_grads:
        total = jnp.sum(sums_all[:, start : start + grad.shape[0]], axis=0)
        piece = grad.shape[0] // SHARDS
        bias_mine.append(lax.dynamic_slice_in_dim(total, place * piece, piece))
        start += grad.shape[0]
    d_silu = lax.dot_general(
        d_group,
        ada_weight.astype(jnp.float32),
        (((1,), (1,)), ((), ())),
        precision=exact_mode,
    )
    cond_mine = lax.dynamic_slice_in_dim(cond_group, place * rows, rows, 1)
    cond_part = jax.vjp(jax.nn.silu, cond_mine)[1](d_silu)[0]
    cond_all = gather_group(cond_part)
    cond_grad = lax.dynamic_index_in_dim(cond_all, fsdp_index, 1, keepdims=False)
    cond_grad = cond_grad.reshape(1, width)

    packed = jnp.concatenate(
        [d_group.reshape(-1), silu_mine.astype(jnp.float32).reshape(-1)] + bias_mine
    )
    packed_all = gather_replicas(packed, replicas)
    d_all = packed_all[:, : 4 * ada_width].reshape(-1, ada_width)
    silu_all = packed_all[:, 4 * ada_width : 4 * ada_width + 4 * rows].reshape(-1, rows)
    ada_total = lax.dot_general(
        silu_all, d_all, (((0,), (0,)), ((), ())), precision=exact_mode
    )
    ada_bias_total = jnp.sum(
        lax.dynamic_slice_in_dim(d_all, place * ada_bias.shape[0], ada_bias.shape[0], 1), axis=0
    )
    bias_totals = jnp.sum(packed_all[:, 4 * ada_width + 4 * rows :], axis=0)
    cuts = [0]
    for piece in bias_mine:
        cuts.append(cuts[-1] + piece.shape[0])
    qv_total, out_bias_total, up_bias_total, down_bias_total = (
        bias_totals[low:high] for low, high in zip(cuts[:-1], cuts[1:])
    )
    return (
        block_out,
        latent_grad,
        cond_grad,
        ada_total,
        ada_bias_total,
        qkv_total.astype(jnp.float32),
        qv_total,
        out_total.astype(jnp.float32),
        out_bias_total,
        up_total.astype(jnp.float32),
        up_bias_total,
        down_total.astype(jnp.float32),
        down_bias_total,
    )


def solution(mesh):
    tokens = P(("rep", "fsdp"), "sp", None)
    rows = P(("rep", "fsdp"), None)
    matrix = P(GROUP, None)
    vector = P(GROUP)
    weights = (matrix, vector) * 5
    return jax.shard_map(
        per_device,
        mesh=mesh,
        in_specs=(tokens, rows, P(("rep", "fsdp"))) + weights + (tokens,),
        out_specs=(tokens, tokens, rows) + weights,
        check_vma=False,
    )
```

```python
import functools

import jax
import jax.numpy as jnp
from jax import lax
from jax.experimental import pallas as pl
from jax.experimental.pallas import tpu as pltpu
from jax.sharding import PartitionSpec as P

HEAD = 72
GROUP = ("fsdp", "sp")
SHARDS = 8

exact_mode = lax.Precision.HIGHEST
epsilon = 1e-06


def normalize(values):
    average = jnp.mean(values, -1, keepdims=True)
    centered = values - average
    inverse = lax.rsqrt(jnp.mean(centered * centered, -1, keepdims=True) + epsilon)
    return (centered * inverse, inverse)


def norm_back(upstream, normed, inverse):
    return (
        upstream
        - jnp.mean(upstream, -1, keepdims=True)
        - normed * jnp.mean(upstream * normed, -1, keepdims=True)
    ) * inverse


def matmul(left, right):
    return jnp.dot(left, right, preferred_element_type=jnp.float32)


def place_of():
    return lax.axis_index("fsdp") * 2 + lax.axis_index("sp")


def pairs_by(rule):
    return [(place, rule(place)) for place in range(SHARDS)]


def swap_rule(place):
    return (place & 4) | ((place & 1) << 1) | ((place >> 1) & 1)


def core_rule(place):
    return place ^ 2


def first_rule(place):
    return place ^ (1 if place & 2 else 4)


def second_rule(place):
    return place ^ (4 if place & 2 else 1)


def permute(values, rule):
    return lax.ppermute(values, GROUP, pairs_by(rule))


def swap_halves(values):
    place = place_of()
    pairs = [pair for pair in pairs_by(swap_rule) if pair[0] != pair[1]]
    received = lax.ppermute(values, GROUP, pairs)
    stays = ((place >> 1) & 1) == (place & 1)
    return jnp.where(stays, values, received)


def gather_group(values):
    place = place_of()
    stacked = values[None]
    for bit in (1, 2, 4):
        received = permute(stacked, lambda at: at ^ bit)
        stacked = jnp.where(
            (place & bit) == 0,
            jnp.concatenate([stacked, received]),
            jnp.concatenate([received, stacked]),
        )
    return stacked


def gather_replicas(values, replicas):
    stacked = [values]
    for shift in range(1, replicas):
        pairs = [(at, (at + shift) % replicas) for at in range(replicas)]
        stacked.append(lax.ppermute(values, "rep", pairs))
    return jnp.stack(stacked)


def assemble_kernel(widths, order_ref, *refs):
    pieces, wholes = refs[:SHARDS], refs[SHARDS : SHARDS + len(widths)]
    buffer, load_sems, store_sems = refs[SHARDS + len(widths) :]
    rows = buffer.shape[1]
    loads = [
        pltpu.make_async_copy(piece, buffer.at[at], load_sems.at[at])
        for at, piece in enumerate(pieces)
    ]
    for load in loads:
        load.start()
    stores = []
    for at, load in enumerate(loads):
        load.wait()
        target = pl.ds(pl.multiple_of(order_ref[at] * rows, 16), rows)
        start = 0
        for which, width in enumerate(widths):
            store = pltpu.make_async_copy(
                buffer.at[at, :, pl.ds(start, width)],
                wholes[which].at[target],
                store_sems.at[which, at],
            )
            store.start()
            stores.append(store)
            start += width
    for store in stores:
        store.wait()


def assemble(pieces, order, widths):
    rows, columns = pieces[0].shape
    size = SHARDS * rows * columns * 2
    return pl.pallas_call(
        functools.partial(assemble_kernel, widths),
        out_shape=[
            jax.ShapeDtypeStruct((SHARDS * rows, width), pieces[0].dtype) for width in widths
        ],
        in_specs=[pl.BlockSpec(memory_space=pltpu.SMEM)]
        + [pl.BlockSpec(memory_space=pl.ANY)] * SHARDS,
        out_specs=[pl.BlockSpec(memory_space=pl.ANY)] * len(widths),
        scratch_shapes=[
            pltpu.VMEM((SHARDS, rows, columns), pieces[0].dtype),
            pltpu.SemaphoreType.DMA((SHARDS,)),
            pltpu.SemaphoreType.DMA((len(widths), SHARDS)),
        ],
        compiler_params=pltpu.CompilerParams(vmem_limit_bytes=size + (4 << 20)),
        cost_estimate=SHORT,
    )(order, *pieces)


def gather_pieces(shard):
    place = place_of()
    near = jnp.where((place & 2) == 0, 4, 1)
    far = 5 - near
    other = place ^ 2
    first = permute(shard, first_rule)
    second = permute(shard, second_rule)
    both = permute(first, second_rule)
    held = [shard, first, second, both]
    pieces = held + [permute(piece, core_rule) for piece in held]
    order = [place, place ^ near, place ^ far, place ^ 5]
    order += [other, other ^ far, other ^ near, other ^ 5]
    return pieces, jnp.stack(order).astype(jnp.int32)


def tie(*values):
    return lax.optimization_barrier(values)


class Scatter:
    def __init__(self, halves):
        self.place = place_of()
        self.core = (self.place >> 1) & 1
        self.kept, sent = halves
        self.low = sent.dtype
        self.received = permute(sent, core_rule)

    def second(self):
        kept = self.kept.astype(jnp.float32) + self.received.astype(jnp.float32)
        kept = kept.astype(self.low)
        mine = ((self.place >> 2) << 1) | (self.place & 1)
        near = jnp.where(self.core == 0, 2, 1)

        def pair(which):
            parts = [which, which ^ 3 ^ near]
            return jnp.concatenate([lax.dynamic_slice_in_dim(kept, at, 1, 0) for at in parts])

        self.kept = pair(mine)
        self.received = permute(pair(mine ^ near), first_rule)

    def third(self):
        kept = self.kept.astype(jnp.float32) + self.received.astype(jnp.float32)
        self.kept = kept[0]
        self.received = permute(kept[1].astype(self.low), second_rule)

    def result(self):
        return self.kept + self.received.astype(jnp.float32)


class ReplicaSum:
    def __init__(self, partial, replicas):
        self.replicas = replicas
        self.own = lax.axis_index("rep")
        self.shape = partial.shape
        self.span = partial.shape[1] // replicas
        low = partial.astype(jnp.bfloat16)
        self.kept = self.piece(partial, self.own)
        self.received = [
            self.send(self.piece(low, self.own + shift), shift) for shift in range(1, replicas)
        ]

    def piece(self, values, which):
        return lax.dynamic_slice_in_dim(values, which % self.replicas * self.span, self.span, 1)

    def send(self, values, shift):
        pairs = [(at, (at + shift) % self.replicas) for at in range(self.replicas)]
        return lax.ppermute(values, "rep", pairs)

    def second(self):
        total = self.kept
        for received in self.received:
            total = total + received.astype(jnp.float32)
        low = total.astype(jnp.bfloat16)
        self.received = [low] + [self.send(low, shift) for shift in range(1, self.replicas)]

    def result(self):
        whole = jnp.zeros(self.shape, jnp.float32)
        for shift, received in enumerate(self.received):
            start = (self.own - shift) % self.replicas * self.span
            whole = lax.dynamic_update_slice_in_dim(whole, received.astype(jnp.float32), start, 1)
        return whole


WINDOW = 256
GELU_RATE = 0.7978845608028654
GELU_CUBE = 0.044715
SHORT = pl.CostEstimate(flops=1 << 20, bytes_accessed=1 << 20, transcendentals=0)


def head_lanes(heads, width):
    low = heads[0] * HEAD // 128 * 128
    high = -(-(heads[-1] + 1) * HEAD // 128) * 128
    return min(low, width - WINDOW), high


def head_window(first_head, width, base):
    first = (first_head + pl.program_id(0)) * HEAD
    start = jnp.minimum(first // 128 * 128, width - WINDOW)
    start = pl.multiple_of(start, 128)
    lane = lax.broadcasted_iota(jnp.int32, (1, WINDOW), 1) + start
    inside = (lane >= first) & (lane < first + HEAD)
    mask = jnp.where(inside, 1.0, 0.0).astype(jnp.bfloat16)
    lanes = [pl.ds(pl.multiple_of(start + at, 128), WINDOW) for at in (0, width, -base)]
    return (*lanes, mask)


def dot_last(left, right):
    return lax.dot_general(
        left, right, (((1,), (1,)), ((), ())), preferred_element_type=jnp.float32
    )


def dot_first(left, right):
    return lax.dot_general(
        left, right, (((0,), (0,)), ((), ())), preferred_element_type=jnp.float32
    )


def attend_kernel(first_head, base, query_ref, own_ref, other_ref, out_ref, log_ref, total_ref):
    length, width = query_ref.shape
    head = pl.program_id(0)
    key_lanes, value_lanes, out_lanes, mask = head_window(first_head, width, base)
    score_scale = float(HEAD) ** (-0.5)

    @pl.when(head == 0)
    def _():
        total_ref[...] = jnp.zeros_like(total_ref)
        log_ref[...] = jnp.zeros_like(log_ref)

    keys = jnp.concatenate([own_ref[:, key_lanes], other_ref[:, key_lanes]]) * mask
    values = jnp.concatenate([own_ref[:, value_lanes], other_ref[:, value_lanes]]) * mask
    rows = min(256, length)
    for at in range(0, length, rows):
        block = pl.ds(at, rows)
        scores = dot_last(query_ref[block, key_lanes], keys)
        row_max = jnp.max(scores, -1, keepdims=True)
        weights = jnp.exp((scores - row_max) * score_scale)
        row_total = jnp.sum(weights, -1, keepdims=True)
        probs = (weights * (1.0 / row_total)).astype(jnp.bfloat16)
        total_ref[block, out_lanes] += jnp.dot(
            probs, values, preferred_element_type=jnp.float32
        )
        log_total = row_max * score_scale + jnp.log(row_total)
        lane = lax.broadcasted_iota(jnp.int32, (rows, 128), 1)
        log_ref[block, :] = jnp.where(lane == first_head + head, log_total, log_ref[block, :])

    @pl.when(head == pl.num_programs(0) - 1)
    def _():
        out_ref[...] = total_ref[...].astype(out_ref.dtype)


def attend(query, own, other, heads):
    length, width = query.shape
    low, high = head_lanes(heads, width)
    return pl.pallas_call(
        functools.partial(attend_kernel, heads[0], low),
        grid=(len(heads),),
        out_shape=(
            jax.ShapeDtypeStruct((length, high - low), jnp.bfloat16),
            jax.ShapeDtypeStruct((length, 128), jnp.float32),
        ),
        in_specs=[
            pl.BlockSpec((length, width), lambda head: (0, 0)),
            pl.BlockSpec(own.shape, lambda head: (0, 0)),
            pl.BlockSpec(other.shape, lambda head: (0, 0)),
        ],
        out_specs=(
            pl.BlockSpec((length, high - low), lambda head: (0, 0)),
            pl.BlockSpec((length, 128), lambda head: (0, 0)),
        ),
        scratch_shapes=[pltpu.VMEM((length, high - low), jnp.float32)],
        compiler_params=pltpu.CompilerParams(vmem_limit_bytes=48 << 20),
        cost_estimate=SHORT,
    )(query, own, other)


def attend_back_kernel(
    first_head, base, query_ref, own_ref, other_ref, upstream_ref, log_ref, d_query_ref, d_own_ref, d_other_ref,
    query_total, key_total, value_total,
):
    length, width = query_ref.shape
    head = pl.program_id(0)
    key_lanes, value_lanes, out_lanes, mask = head_window(first_head, width, base)
    score_scale = float(HEAD) ** (-0.5)

    @pl.when(head == 0)
    def _():
        query_total[...] = jnp.zeros_like(query_total)
        key_total[...] = jnp.zeros_like(key_total)
        value_total[...] = jnp.zeros_like(value_total)

    keys = jnp.concatenate([own_ref[:, key_lanes], other_ref[:, key_lanes]]) * mask
    values = jnp.concatenate([own_ref[:, value_lanes], other_ref[:, value_lanes]]) * mask
    rows = min(256, length)
    for at in range(0, length, rows):
        block = pl.ds(at, rows)
        query = query_ref[block, key_lanes] * mask
        upstream = upstream_ref[block, key_lanes] * mask
        scores = dot_last(keys, query)
        probs = jnp.exp(scores * score_scale - log_ref[0, :, block])
        d_probs = dot_last(values, upstream)
        weighted = probs * d_probs
        row_sum = jnp.sum(weighted, 0, keepdims=True)
        d_scores = (weighted - probs * row_sum).astype(jnp.bfloat16)
        value_total[:, out_lanes] += jnp.dot(
            probs.astype(jnp.bfloat16), upstream, preferred_element_type=jnp.float32
        )
        key_total[:, out_lanes] += score_scale * jnp.dot(
            d_scores, query, preferred_element_type=jnp.float32
        )
        query_total[block, out_lanes] += dot_first(d_scores, keys)

    @pl.when(head == pl.num_programs(0) - 1)
    def _():
        d_query_ref[...] = (query_total[...] * score_scale).astype(d_query_ref.dtype)
        for at, total in enumerate((key_total, value_total)):
            d_own_ref[at] = total[: own_ref.shape[0]]
            d_other_ref[at] = total[own_ref.shape[0] :].astype(d_other_ref.dtype)


def attend_back(query, own, other, upstream, log_totals, heads):
    length, width = query.shape
    low, high = head_lanes(heads, width)
    span = high - low
    whole = lambda head: (0, 0)
    halves = pl.BlockSpec((2, own.shape[0], span), lambda head: (0, 0, 0))
    return pl.pallas_call(
        functools.partial(attend_back_kernel, heads[0], low),
        grid=(len(heads),),
        out_shape=(
            jax.ShapeDtypeStruct((length, span), jnp.bfloat16),
            jax.ShapeDtypeStruct((2, own.shape[0], span), jnp.float32),
            jax.ShapeDtypeStruct((2, other.shape[0], span), jnp.bfloat16),
        ),
        in_specs=[
            pl.BlockSpec((length, width), whole),
            pl.BlockSpec(own.shape, whole),
            pl.BlockSpec(other.shape, whole),
            pl.BlockSpec((length, width), whole),
            pl.BlockSpec((1, 1, length), lambda head: (heads[0] + head, 0, 0)),
        ],
        out_specs=(pl.BlockSpec((length, span), whole), halves, halves),
        scratch_shapes=[
            pltpu.VMEM((length, span), jnp.float32),
            pltpu.VMEM((own.shape[0] + other.shape[0], span), jnp.float32),
            pltpu.VMEM((own.shape[0] + other.shape[0], span), jnp.float32),
        ],
        compiler_params=pltpu.CompilerParams(vmem_limit_bytes=56 << 20),
        cost_estimate=SHORT,
    )(query, own, other, upstream, log_totals)


def join_heads(left, right, width):
    shared = left.shape[-1] + right.shape[-1] - width
    if shared == 0:
        return jnp.concatenate([left, right], axis=-1)
    edge = left.shape[-1] - shared
    middle = left[..., edge:] + right[..., :shared]
    return jnp.concatenate([left[..., :edge], middle, right[..., shared:]], axis=-1)


def store_halves(grad, kept_ref, sent_ref):
    core = lax.axis_index("fsdp") % 2
    rows = grad.shape[0] // SHARDS
    low = grad.astype(kept_ref.dtype)
    for owner in (0, 1):
        blocks = [at for at in range(SHARDS) if (at >> 1) & 1 == owner]

        @pl.when(core == owner)
        def _():
            for slot, at in enumerate(blocks):
                kept_ref[slot] = low[at * rows : (at + 1) * rows]

        @pl.when(core != owner)
        def _():
            for slot, at in enumerate(blocks):
                sent_ref[slot] = low[at * rows : (at + 1) * rows]


def product_back_kernel(
    left_ref, upstream_ref, weight_ref, d_left_ref, kept_ref, sent_ref, turned_ref
):
    @pl.when(pl.program_id(0) == 0)
    def _():
        turned_ref[...] = left_ref[...].T
        d_left_ref[...] = jnp.zeros_like(d_left_ref)

    upstream = upstream_ref[...]
    grad = jnp.dot(turned_ref[...], upstream, preferred_element_type=jnp.float32)
    store_halves(grad, kept_ref, sent_ref)
    d_left_ref[...] += dot_last(upstream, weight_ref[...])


def product_back(left, upstream, weight):
    length, width = left.shape
    columns = weight.shape[1]
    block = width
    fixed = pl.BlockSpec((length, width), lambda at: (0, 0))
    half = pl.BlockSpec((SHARDS // 2, width // SHARDS, block), lambda at: (0, 0, at))
    half_shape = jax.ShapeDtypeStruct((SHARDS // 2, width // SHARDS, columns), jnp.bfloat16)
    d_left, kept, sent = pl.pallas_call(
        product_back_kernel,
        grid=(columns // block,),
        out_shape=(
            jax.ShapeDtypeStruct((length, width), jnp.float32),
            half_shape,
            half_shape,
        ),
        in_specs=[
            fixed,
            pl.BlockSpec((length, block), lambda at: (0, at)),
            pl.BlockSpec((width, block), lambda at: (0, at)),
        ],
        out_specs=(fixed, half, half),
        scratch_shapes=[pltpu.VMEM((width, length), jnp.bfloat16)],
        compiler_params=pltpu.CompilerParams(vmem_limit_bytes=52 << 20),
        cost_estimate=SHORT,
    )(left, upstream, weight)
    return d_left, (kept, sent)


def mlp_kernel(
    hidden_ref, upstream_ref, up_ref, bias_ref, down_ref,
    branch_ref, d_hidden_ref, up_kept_ref, up_sent_ref, down_grad_ref, bias_grad_ref,
    turned_ref,
):
    @pl.when(pl.program_id(0) == 0)
    def _():
        turned_ref[...] = hidden_ref[...].T
        branch_ref[...] = jnp.zeros_like(branch_ref)
        d_hidden_ref[...] = jnp.zeros_like(d_hidden_ref)

    hidden = hidden_ref[...]
    upstream = upstream_ref[...]
    preact = (
        jnp.dot(hidden, up_ref[...], preferred_element_type=jnp.float32) + bias_ref[...]
    )
    square = preact * preact
    bent = jnp.tanh(GELU_RATE * preact * (1.0 + GELU_CUBE * square))
    half = 0.5 * (1.0 + bent)
    slope = half + (0.5 * GELU_RATE) * preact * (1.0 - bent * bent) * (
        1.0 + (3.0 * GELU_CUBE) * square
    )
    activated = (preact * half).astype(jnp.bfloat16)
    branch_ref[...] += jnp.dot(activated, down_ref[...], preferred_element_type=jnp.float32)
    d_preact = dot_last(upstream, down_ref[...]) * slope
    d_preact = d_preact.astype(jnp.bfloat16)
    bias_grad_ref[...] = jnp.sum(d_preact.astype(jnp.float32), 0, keepdims=True)
    down_grad_ref[...] = dot_first(activated, upstream).astype(jnp.bfloat16)
    d_hidden_ref[...] += dot_last(d_preact, up_ref[...])
    up_grad = jnp.dot(turned_ref[...], d_preact, preferred_element_type=jnp.float32)
    store_halves(up_grad, up_kept_ref, up_sent_ref)


def mlp(hidden, upstream, up, bias, down):
    length, width = hidden.shape
    units = up.shape[1]
    block = 512
    fixed = pl.BlockSpec((length, width), lambda at: (0, 0))
    columns = pl.BlockSpec((width, block), lambda at: (0, at))
    lanes = pl.BlockSpec((1, block), lambda at: (0, at))
    rows = pl.BlockSpec((block, width), lambda at: (at, 0))
    half = pl.BlockSpec((SHARDS // 2, width // SHARDS, block), lambda at: (0, 0, at))
    half_shape = jax.ShapeDtypeStruct((SHARDS // 2, width // SHARDS, units), jnp.bfloat16)
    return pl.pallas_call(
        mlp_kernel,
        grid=(units // block,),
        out_shape=(
            jax.ShapeDtypeStruct((length, width), jnp.float32),
            jax.ShapeDtypeStruct((length, width), jnp.float32),
            half_shape,
            half_shape,
            jax.ShapeDtypeStruct(down.shape, jnp.bfloat16),
            jax.ShapeDtypeStruct((1, units), jnp.float32),
        ),
        in_specs=[fixed, fixed, columns, lanes, rows],
        out_specs=(fixed, fixed, half, half, rows, lanes),
        scratch_shapes=[pltpu.VMEM((width, length), jnp.bfloat16)],
        compiler_params=pltpu.CompilerParams(vmem_limit_bytes=56 << 20),
        cost_estimate=SHORT,
    )(hidden, upstream, up, bias, down)


def per_device(
    latent_in,
    condition,
    valid_slots,
    ada_weight,
    ada_bias,
    qkv_weight,
    qv_bias,
    out_weight,
    out_bias,
    up_weight,
    up_bias,
    down_weight,
    down_bias,
    cotangent,
):
    number, length, width = latent_in.shape
    place = place_of()
    fsdp_index = lax.axis_index("fsdp")
    held = (place >> 2) * 2 + (place & 1)
    rows = width // SHARDS
    replicas = lax.axis_size("rep")

    small = jnp.concatenate(
        [
            condition[0],
            qv_bias,
            out_bias,
            up_bias,
            down_bias,
            jnp.broadcast_to(valid_slots.astype(jnp.bfloat16), (128,)),
        ]
    )
    small_all = gather_group(small)
    latent_low = swap_halves(latent_in)
    pieces, order = gather_pieces(jnp.concatenate([qkv_weight, out_weight], axis=1))
    full_up = lax.all_gather(up_weight, GROUP, axis=0, tiled=True)
    cotangent_low = swap_halves(cotangent)
    full_qkv, full_out = assemble(pieces, order, (3 * width, width))
    full_down = lax.all_gather(down_weight, GROUP, axis=0, tiled=True)

    bounds = [0, width]
    for bias in (qv_bias, out_bias, up_bias, down_bias):
        bounds.append(bounds[-1] + bias.shape[0])
    cond_group = small_all[::2, :width].astype(jnp.float32)
    full_qv_bias, full_out_bias, full_up_bias, full_down_bias = (
        small_all[:, low:high].reshape(-1).astype(jnp.float32)
        for low, high in zip(bounds[1:-1], bounds[2:])
    )
    valid_group = small_all[::2, bounds[-1]].astype(jnp.float32)
    slot_mask = lax.dynamic_slice_in_dim(valid_group, held, 1)[:, None, None]

    silu_group = jax.nn.silu(cond_group).astype(jnp.bfloat16)
    silu_mine = lax.dynamic_slice_in_dim(silu_group, place * rows, rows, 1)
    ada_bias_row = lax.dynamic_update_slice_in_dim(
        jnp.zeros((ada_weight.shape[1],), jnp.float32),
        ada_bias.astype(jnp.float32),
        place * ada_bias.shape[0],
        0,
    )
    modulation = matmul(silu_mine, ada_weight) + ada_bias_row
    for bit, count in ((4, 2), (1, 1)):
        upper = (place & bit) != 0
        sent = jnp.where(upper, modulation[:count], modulation[count:])
        kept = jnp.where(upper, modulation[count:], modulation[:count])
        modulation = kept + permute(sent, lambda at: at ^ bit)
    modulation = modulation + permute(modulation, core_rule)
    shift_one, scale_one, gate_one, shift_two, scale_two, gate_two = jnp.split(
        modulation, 6, axis=-1
    )

    latent = latent_low[0].astype(jnp.float32)
    normed_one, inverse_one = normalize(latent)
    hidden_one = (normed_one * (1.0 + scale_one) + shift_one).astype(jnp.bfloat16)
    bias_full = jnp.concatenate(
        [full_qv_bias[:width], jnp.zeros((width,), jnp.float32), full_qv_bias[width:]]
    )
    projected = (matmul(hidden_one, full_qkv) + bias_full).astype(jnp.bfloat16)
    query = projected[:, :width]
    pair_own = projected[:, width:]
    pair_other = permute(pair_own, core_rule)
    heads = range(width // HEAD)
    halves = heads[: len(heads) // 2], heads[len(heads) // 2 :]
    attended_low, log_totals = attend(query, pair_own, pair_other, heads)
    log_rows = log_totals[:, : len(heads)].T[:, None, :]
    branch_one = matmul(attended_low, full_out) + full_out_bias
    middle = latent + gate_one * branch_one

    normed_two, inverse_two = normalize(middle)
    hidden_two = (normed_two * (1.0 + scale_two) + shift_two).astype(jnp.bfloat16)
    mask_row = slot_mask[0]
    d_out = cotangent_low[0].astype(jnp.float32) * mask_row
    d_branch_two = (gate_two * d_out).astype(jnp.bfloat16)
    branch_two, d_hidden_two, up_kept, up_sent, down_grad, up_bias_grad = mlp(
        hidden_two, d_branch_two, full_up, full_up_bias[None], full_down
    )
    up_scatter = Scatter((up_kept, up_sent))
    down_shard = lax.psum_scatter(down_grad, GROUP, scatter_dimension=0, tiled=True)
    branch_two = branch_two + full_down_bias
    block_out = (mask_row * (middle + gate_two * branch_two)).astype(jnp.bfloat16)
    d_gate_two = jnp.sum(d_out * branch_two, axis=0)
    down_bias_grad = jnp.sum(d_branch_two.astype(jnp.float32), axis=0)
    up_bias_grad = up_bias_grad[0]
    d_shift_two = jnp.sum(d_hidden_two, axis=0)
    d_scale_two = jnp.sum(d_hidden_two * normed_two, axis=0)
    d_middle = d_out + norm_back(d_hidden_two * (1.0 + scale_two), normed_two, inverse_two)
    d_gate_one = jnp.sum(d_middle * branch_one, axis=0)
    d_branch_one = (gate_one * d_middle).astype(jnp.bfloat16)

    d_attended, out_halves = product_back(attended_low, d_branch_one, full_out)
    d_attended = d_attended.astype(jnp.bfloat16)
    out_scatter = Scatter(out_halves)
    out_bias_grad = jnp.sum(d_branch_one.astype(jnp.float32), axis=0)
    d_attended, up_scatter.received = tie(d_attended, up_scatter.received)
    up_scatter.second()
    left = attend_back(query, pair_own, pair_other, d_attended, log_rows, halves[0])
    d_query, d_attended, out_scatter.received = tie(left[0], d_attended, out_scatter.received)
    out_scatter.second()
    right = attend_back(query, pair_own, pair_other, d_attended, log_rows, halves[1])
    *right, up_scatter.received = tie(*right, up_scatter.received)
    up_scatter.third()
    d_query = join_heads(d_query, right[0], width)
    d_own = join_heads(left[1], right[1], width)
    d_other = permute(join_heads(left[2], right[2], width), core_rule)
    d_own = (d_own + d_other.astype(jnp.float32)).astype(jnp.bfloat16)
    d_projected = jnp.concatenate([d_query, d_own[0], d_own[1]], axis=-1)

    d_projected, down_shard = tie(d_projected, down_shard)
    d_hidden_one, qkv_halves = product_back(hidden_one, d_projected, full_qkv)
    qkv_scatter = Scatter(qkv_halves)
    column_sums = jnp.sum(d_projected.astype(jnp.float32), axis=0)
    d_hidden_one, *arrived = tie(
        d_hidden_one,
        qkv_scatter.received,
        up_scatter.received,
        out_scatter.received,
    )
    qkv_scatter.received, up_scatter.received, out_scatter.received = arrived
    qkv_scatter.second()
    down_total = lax.psum(down_shard, "rep")
    up_sum = ReplicaSum(up_scatter.result(), replicas)
    out_scatter.third()
    d_shift_one = jnp.sum(d_hidden_one, axis=0)
    d_scale_one = jnp.sum(d_hidden_one * normed_one, axis=0)
    latent_grad = d_middle + norm_back(d_hidden_one * (1.0 + scale_one), normed_one, inverse_one)
    bias_grads = (
        jnp.concatenate([column_sums[:width], column_sums[2 * width :]]),
        out_bias_grad,
        up_bias_grad,
        down_bias_grad,
    )
    sums = [d_shift_one, d_scale_one, d_gate_one, d_shift_two, d_scale_two, d_gate_two]
    ada_width = 6 * width
    small_sums = jnp.concatenate(sums + list(bias_grads))
    qkv_scatter.received, out_scatter.received = tie(
        qkv_scatter.received, out_scatter.received
    )
    qkv_scatter.third()
    qkv_shard = qkv_scatter.result()
    qkv_shard, latent_grad, block_out, small_sums, *up_sum.received = tie(
        qkv_shard, latent_grad.astype(jnp.bfloat16), block_out, small_sums, *up_sum.received
    )
    late_sum = ReplicaSum(
        jnp.concatenate([out_scatter.result(), qkv_shard], axis=1), replicas
    )
    latent_grad = swap_halves(latent_grad[None]).astype(jnp.float32)
    block_out = swap_halves(block_out[None])
    sums_all = gather_group(small_sums)
    up_sum.second()
    down_total, sums_all, *late_sum.received = tie(down_total, sums_all, *late_sum.received)
    late_sum.second()

    d_group = sums_all[:, :ada_width].reshape(2, 2, 2, ada_width).sum(1).reshape(4, ada_width)
    bias_mine = []
    start = ada_width
    for grad in bias_grads:
        total = jnp.sum(sums_all[:, start : start + grad.shape[0]], axis=0)
        piece = grad.shape[0] // SHARDS
        bias_mine.append(lax.dynamic_slice_in_dim(total, place * piece, piece))
        start += grad.shape[0]
    d_silu = lax.dot_general(
        d_group,
        ada_weight.astype(jnp.float32),
        (((1,), (1,)), ((), ())),
        precision=exact_mode,
    )
    cond_mine = lax.dynamic_slice_in_dim(cond_group, place * rows, rows, 1)
    cond_part = jax.vjp(jax.nn.silu, cond_mine)[1](d_silu)[0]
    cond_all = gather_group(cond_part)
    cond_grad = lax.dynamic_index_in_dim(cond_all, fsdp_index, 1, keepdims=False)
    cond_grad = cond_grad.reshape(1, width)

    packed = jnp.concatenate(
        [d_group.reshape(-1), silu_mine.astype(jnp.float32).reshape(-1)] + bias_mine
    )
    packed_all = gather_replicas(packed, replicas)
    packed_all, *late_sum.received = tie(packed_all, *late_sum.received)
    late_sum.received[0], *up_sum.received = tie(late_sum.received[0], *up_sum.received)
    up_total = up_sum.result()
    late_total = late_sum.result()
    out_total, qkv_total = late_total[:, :width], late_total[:, width:]

    d_all = packed_all[:, : 4 * ada_width].reshape(-1, ada_width)
    silu_all = packed_all[:, 4 * ada_width : 4 * ada_width + 4 * rows].reshape(-1, rows)
    ada_total = lax.dot_general(
        silu_all, d_all, (((0,), (0,)), ((), ())), precision=exact_mode
    )
    ada_bias_total = jnp.sum(
        lax.dynamic_slice_in_dim(d_all, place * ada_bias.shape[0], ada_bias.shape[0], 1), axis=0
    )
    bias_totals = jnp.sum(packed_all[:, 4 * ada_width + 4 * rows :], axis=0)
    cuts = [0]
    for piece in bias_mine:
        cuts.append(cuts[-1] + piece.shape[0])
    qv_total, out_bias_total, up_bias_total, down_bias_total = (
        bias_totals[low:high] for low, high in zip(cuts[:-1], cuts[1:])
    )
    return (
        block_out,
        latent_grad,
        cond_grad,
        ada_total,
        ada_bias_total,
        qkv_total.astype(jnp.float32),
        qv_total,
        out_total.astype(jnp.float32),
        out_bias_total,
        up_total.astype(jnp.float32),
        up_bias_total,
        down_total.astype(jnp.float32),
        down_bias_total,
    )


def solution(mesh):
    tokens = P(("rep", "fsdp"), "sp", None)
    rows = P(("rep", "fsdp"), None)
    matrix = P(GROUP, None)
    vector = P(GROUP)
    weights = (matrix, vector) * 5
    return jax.shard_map(
        per_device,
        mesh=mesh,
        in_specs=(tokens, rows, P(("rep", "fsdp"))) + weights + (tokens,),
        out_specs=(tokens, tokens, rows) + weights,
        check_vma=False,
    )
```

```python
import functools

import jax
import jax.numpy as jnp
from jax import lax
from jax.experimental import pallas as pl
from jax.experimental.pallas import tpu as pltpu
from jax.sharding import PartitionSpec as P

HEAD = 72
GROUP = ("fsdp", "sp")
SHARDS = 8

exact_mode = lax.Precision.HIGHEST
epsilon = 1e-06


def normalize(values):
    average = jnp.mean(values, -1, keepdims=True)
    centered = values - average
    inverse = lax.rsqrt(jnp.mean(centered * centered, -1, keepdims=True) + epsilon)
    return (centered * inverse, inverse)


def norm_back(upstream, normed, inverse):
    return (
        upstream
        - jnp.mean(upstream, -1, keepdims=True)
        - normed * jnp.mean(upstream * normed, -1, keepdims=True)
    ) * inverse


def matmul(left, right):
    return jnp.dot(left, right, preferred_element_type=jnp.float32)


def place_of():
    return lax.axis_index("fsdp") * 2 + lax.axis_index("sp")


def pairs_by(rule):
    return [(place, rule(place)) for place in range(SHARDS)]


def swap_rule(place):
    return (place & 4) | ((place & 1) << 1) | ((place >> 1) & 1)


def core_rule(place):
    return place ^ 2


def first_rule(place):
    return place ^ (1 if place & 2 else 4)


def second_rule(place):
    return place ^ (4 if place & 2 else 1)


def permute(values, rule):
    return lax.ppermute(values, GROUP, pairs_by(rule))


def swap_halves(values):
    place = place_of()
    pairs = [pair for pair in pairs_by(swap_rule) if pair[0] != pair[1]]
    received = lax.ppermute(values, GROUP, pairs)
    stays = ((place >> 1) & 1) == (place & 1)
    return jnp.where(stays, values, received)


def gather_group(values):
    place = place_of()
    stacked = values[None]
    for bit in (1, 2, 4):
        received = permute(stacked, lambda at: at ^ bit)
        stacked = jnp.where(
            (place & bit) == 0,
            jnp.concatenate([stacked, received]),
            jnp.concatenate([received, stacked]),
        )
    return stacked


def gather_replicas(values, replicas):
    stacked = [values]
    for shift in range(1, replicas):
        pairs = [(at, (at + shift) % replicas) for at in range(replicas)]
        stacked.append(lax.ppermute(values, "rep", pairs))
    return jnp.stack(stacked)


def assemble_kernel(widths, order_ref, *refs):
    pieces, wholes = refs[:SHARDS], refs[SHARDS : SHARDS + len(widths)]
    buffer, load_sems, store_sems = refs[SHARDS + len(widths) :]
    rows = buffer.shape[1]
    loads = [
        pltpu.make_async_copy(piece, buffer.at[at], load_sems.at[at])
        for at, piece in enumerate(pieces)
    ]
    for load in loads:
        load.start()
    stores = []
    for at, load in enumerate(loads):
        load.wait()
        target = pl.ds(pl.multiple_of(order_ref[at] * rows, 16), rows)
        start = 0
        for which, width in enumerate(widths):
            store = pltpu.make_async_copy(
                buffer.at[at, :, pl.ds(start, width)],
                wholes[which].at[target],
                store_sems.at[which, at],
            )
            store.start()
            stores.append(store)
            start += width
    for store in stores:
        store.wait()


def assemble(pieces, order, widths):
    rows, columns = pieces[0].shape
    size = SHARDS * rows * columns * 2
    return pl.pallas_call(
        functools.partial(assemble_kernel, widths),
        out_shape=[
            jax.ShapeDtypeStruct((SHARDS * rows, width), pieces[0].dtype) for width in widths
        ],
        in_specs=[pl.BlockSpec(memory_space=pltpu.SMEM)]
        + [pl.BlockSpec(memory_space=pl.ANY)] * SHARDS,
        out_specs=[pl.BlockSpec(memory_space=pl.ANY)] * len(widths),
        scratch_shapes=[
            pltpu.VMEM((SHARDS, rows, columns), pieces[0].dtype),
            pltpu.SemaphoreType.DMA((SHARDS,)),
            pltpu.SemaphoreType.DMA((len(widths), SHARDS)),
        ],
        compiler_params=pltpu.CompilerParams(vmem_limit_bytes=size + (4 << 20)),
        cost_estimate=SHORT,
    )(order, *pieces)


def gather_pieces(shard):
    place = place_of()
    near = jnp.where((place & 2) == 0, 4, 1)
    far = 5 - near
    other = place ^ 2
    first = permute(shard, first_rule)
    second = permute(shard, second_rule)
    both = permute(first, second_rule)
    held = [shard, first, second, both]
    pieces = held + [permute(piece, core_rule) for piece in held]
    order = [place, place ^ near, place ^ far, place ^ 5]
    order += [other, other ^ far, other ^ near, other ^ 5]
    return pieces, jnp.stack(order).astype(jnp.int32)


def tie(*values):
    return lax.optimization_barrier(values)


class Scatter:
    def __init__(self, halves):
        self.place = place_of()
        self.core = (self.place >> 1) & 1
        self.kept, sent = halves
        self.low = sent.dtype
        self.received = permute(sent, core_rule)

    def second(self):
        kept = self.kept.astype(jnp.float32) + self.received.astype(jnp.float32)
        kept = kept.astype(self.low)
        mine = ((self.place >> 2) << 1) | (self.place & 1)
        near = jnp.where(self.core == 0, 2, 1)

        def pair(which):
            parts = [which, which ^ 3 ^ near]
            return jnp.concatenate([lax.dynamic_slice_in_dim(kept, at, 1, 0) for at in parts])

        self.kept = pair(mine)
        self.received = permute(pair(mine ^ near), first_rule)

    def add_third(self):
        kept = self.kept.astype(jnp.float32) + self.received.astype(jnp.float32)
        self.kept, self.sent = kept[0], kept[1].astype(self.low)

    def send_third(self):
        self.received = permute(self.sent, second_rule)

    def third(self):
        self.add_third()
        self.send_third()

    def result(self):
        return self.kept + self.received.astype(jnp.float32)


class ReplicaSum:
    def __init__(self, partial, replicas):
        self.replicas = replicas
        self.own = lax.axis_index("rep")
        self.shape = partial.shape
        self.span = partial.shape[1] // replicas
        low = partial.astype(jnp.bfloat16)
        self.kept = self.piece(partial, self.own)
        self.received = [
            self.send(self.piece(low, self.own + shift), shift) for shift in range(1, replicas)
        ]

    def piece(self, values, which):
        return lax.dynamic_slice_in_dim(values, which % self.replicas * self.span, self.span, 1)

    def send(self, values, shift):
        pairs = [(at, (at + shift) % self.replicas) for at in range(self.replicas)]
        return lax.ppermute(values, "rep", pairs)

    def second(self):
        total = self.kept
        for received in self.received:
            total = total + received.astype(jnp.float32)
        low = total.astype(jnp.bfloat16)
        self.received = [low] + [self.send(low, shift) for shift in range(1, self.replicas)]

    def result(self):
        whole = jnp.zeros(self.shape, jnp.float32)
        for shift, received in enumerate(self.received):
            start = (self.own - shift) % self.replicas * self.span
            whole = lax.dynamic_update_slice_in_dim(whole, received.astype(jnp.float32), start, 1)
        return whole


WINDOW = 256
GELU_RATE = 0.7978845608028654
GELU_CUBE = 0.044715
SHORT = pl.CostEstimate(flops=1 << 20, bytes_accessed=1 << 20, transcendentals=0)


def head_lanes(heads, width):
    low = heads[0] * HEAD // 128 * 128
    high = -(-(heads[-1] + 1) * HEAD // 128) * 128
    return min(low, width - WINDOW), high


def head_window(first_head, width, base):
    first = (first_head + pl.program_id(0)) * HEAD
    start = jnp.minimum(first // 128 * 128, width - WINDOW)
    start = pl.multiple_of(start, 128)
    lane = lax.broadcasted_iota(jnp.int32, (1, WINDOW), 1) + start
    inside = (lane >= first) & (lane < first + HEAD)
    mask = jnp.where(inside, 1.0, 0.0).astype(jnp.bfloat16)
    lanes = [pl.ds(pl.multiple_of(start + at, 128), WINDOW) for at in (0, width, -base)]
    return (*lanes, mask)


def dot_last(left, right):
    return lax.dot_general(
        left, right, (((1,), (1,)), ((), ())), preferred_element_type=jnp.float32
    )


def dot_first(left, right):
    return lax.dot_general(
        left, right, (((0,), (0,)), ((), ())), preferred_element_type=jnp.float32
    )


def attend_kernel(first_head, base, query_ref, own_ref, other_ref, out_ref, log_ref, total_ref):
    length, width = query_ref.shape
    head = pl.program_id(0)
    key_lanes, value_lanes, out_lanes, mask = head_window(first_head, width, base)
    score_scale = float(HEAD) ** (-0.5)

    @pl.when(head == 0)
    def _():
        total_ref[...] = jnp.zeros_like(total_ref)
        log_ref[...] = jnp.zeros_like(log_ref)

    keys = jnp.concatenate([own_ref[:, key_lanes], other_ref[:, key_lanes]]) * mask
    values = jnp.concatenate([own_ref[:, value_lanes], other_ref[:, value_lanes]]) * mask
    rows = min(256, length)
    for at in range(0, length, rows):
        block = pl.ds(at, rows)
        scores = dot_last(query_ref[block, key_lanes], keys)
        row_max = jnp.max(scores, -1, keepdims=True)
        weights = jnp.exp((scores - row_max) * score_scale)
        row_total = jnp.sum(weights, -1, keepdims=True)
        probs = (weights * (1.0 / row_total)).astype(jnp.bfloat16)
        total_ref[block, out_lanes] += jnp.dot(
            probs, values, preferred_element_type=jnp.float32
        )
        log_total = row_max * score_scale + jnp.log(row_total)
        lane = lax.broadcasted_iota(jnp.int32, (rows, 128), 1)
        log_ref[block, :] = jnp.where(lane == first_head + head, log_total, log_ref[block, :])

    @pl.when(head == pl.num_programs(0) - 1)
    def _():
        out_ref[...] = total_ref[...].astype(out_ref.dtype)


def attend(query, own, other, heads):
    length, width = query.shape
    low, high = head_lanes(heads, width)
    return pl.pallas_call(
        functools.partial(attend_kernel, heads[0], low),
        grid=(len(heads),),
        out_shape=(
            jax.ShapeDtypeStruct((length, high - low), jnp.bfloat16),
            jax.ShapeDtypeStruct((length, 128), jnp.float32),
        ),
        in_specs=[
            pl.BlockSpec((length, width), lambda head: (0, 0)),
            pl.BlockSpec(own.shape, lambda head: (0, 0)),
            pl.BlockSpec(other.shape, lambda head: (0, 0)),
        ],
        out_specs=(
            pl.BlockSpec((length, high - low), lambda head: (0, 0)),
            pl.BlockSpec((length, 128), lambda head: (0, 0)),
        ),
        scratch_shapes=[pltpu.VMEM((length, high - low), jnp.float32)],
        compiler_params=pltpu.CompilerParams(vmem_limit_bytes=48 << 20),
        cost_estimate=SHORT,
    )(query, own, other)


def attend_back_kernel(
    first_head, base, query_ref, own_ref, other_ref, upstream_ref, log_ref, d_query_ref, d_own_ref, d_other_ref,
    query_total, key_total, value_total,
):
    length, width = query_ref.shape
    head = pl.program_id(0)
    key_lanes, value_lanes, out_lanes, mask = head_window(first_head, width, base)
    score_scale = float(HEAD) ** (-0.5)

    @pl.when(head == 0)
    def _():
        query_total[...] = jnp.zeros_like(query_total)
        key_total[...] = jnp.zeros_like(key_total)
        value_total[...] = jnp.zeros_like(value_total)

    keys = jnp.concatenate([own_ref[:, key_lanes], other_ref[:, key_lanes]]) * mask
    values = jnp.concatenate([own_ref[:, value_lanes], other_ref[:, value_lanes]]) * mask
    rows = min(256, length)
    for at in range(0, length, rows):
        block = pl.ds(at, rows)
        query = query_ref[block, key_lanes] * mask
        upstream = upstream_ref[block, key_lanes] * mask
        scores = dot_last(keys, query)
        probs = jnp.exp(scores * score_scale - log_ref[0, :, block])
        d_probs = dot_last(values, upstream)
        weighted = probs * d_probs
        row_sum = jnp.sum(weighted, 0, keepdims=True)
        d_scores = (weighted - probs * row_sum).astype(jnp.bfloat16)
        value_total[:, out_lanes] += jnp.dot(
            probs.astype(jnp.bfloat16), upstream, preferred_element_type=jnp.float32
        )
        key_total[:, out_lanes] += score_scale * jnp.dot(
            d_scores, query, preferred_element_type=jnp.float32
        )
        query_total[block, out_lanes] += dot_first(d_scores, keys)

    @pl.when(head == pl.num_programs(0) - 1)
    def _():
        d_query_ref[...] = (query_total[...] * score_scale).astype(d_query_ref.dtype)
        for at, total in enumerate((key_total, value_total)):
            d_own_ref[at] = total[: own_ref.shape[0]]
            d_other_ref[at] = total[own_ref.shape[0] :].astype(d_other_ref.dtype)


def attend_back(query, own, other, upstream, log_totals, heads):
    length, width = query.shape
    low, high = head_lanes(heads, width)
    span = high - low
    whole = lambda head: (0, 0)
    halves = pl.BlockSpec((2, own.shape[0], span), lambda head: (0, 0, 0))
    return pl.pallas_call(
        functools.partial(attend_back_kernel, heads[0], low),
        grid=(len(heads),),
        out_shape=(
            jax.ShapeDtypeStruct((length, span), jnp.bfloat16),
            jax.ShapeDtypeStruct((2, own.shape[0], span), jnp.float32),
            jax.ShapeDtypeStruct((2, other.shape[0], span), jnp.bfloat16),
        ),
        in_specs=[
            pl.BlockSpec((length, width), whole),
            pl.BlockSpec(own.shape, whole),
            pl.BlockSpec(other.shape, whole),
            pl.BlockSpec((length, width), whole),
            pl.BlockSpec((1, 1, length), lambda head: (heads[0] + head, 0, 0)),
        ],
        out_specs=(pl.BlockSpec((length, span), whole), halves, halves),
        scratch_shapes=[
            pltpu.VMEM((length, span), jnp.float32),
            pltpu.VMEM((own.shape[0] + other.shape[0], span), jnp.float32),
            pltpu.VMEM((own.shape[0] + other.shape[0], span), jnp.float32),
        ],
        compiler_params=pltpu.CompilerParams(vmem_limit_bytes=56 << 20),
        cost_estimate=SHORT,
    )(query, own, other, upstream, log_totals)


def join_heads(left, right, width):
    shared = left.shape[-1] + right.shape[-1] - width
    if shared == 0:
        return jnp.concatenate([left, right], axis=-1)
    edge = left.shape[-1] - shared
    middle = left[..., edge:] + right[..., :shared]
    return jnp.concatenate([left[..., :edge], middle, right[..., shared:]], axis=-1)


def store_halves(grad, kept_ref, sent_ref):
    core = lax.axis_index("fsdp") % 2
    rows = grad.shape[0] // SHARDS
    low = grad.astype(kept_ref.dtype)
    for owner in (0, 1):
        blocks = [at for at in range(SHARDS) if (at >> 1) & 1 == owner]

        @pl.when(core == owner)
        def _():
            for slot, at in enumerate(blocks):
                kept_ref[slot] = low[at * rows : (at + 1) * rows]

        @pl.when(core != owner)
        def _():
            for slot, at in enumerate(blocks):
                sent_ref[slot] = low[at * rows : (at + 1) * rows]


def product_back_kernel(
    left_ref, upstream_ref, weight_ref, d_left_ref, kept_ref, sent_ref, turned_ref
):
    @pl.when(pl.program_id(0) == 0)
    def _():
        turned_ref[...] = left_ref[...].T
        d_left_ref[...] = jnp.zeros_like(d_left_ref)

    upstream = upstream_ref[...]
    grad = jnp.dot(turned_ref[...], upstream, preferred_element_type=jnp.float32)
    store_halves(grad, kept_ref, sent_ref)
    d_left_ref[...] += dot_last(upstream, weight_ref[...])


def product_back(left, upstream, weight):
    length, width = left.shape
    columns = weight.shape[1]
    block = width
    fixed = pl.BlockSpec((length, width), lambda at: (0, 0))
    half = pl.BlockSpec((SHARDS // 2, width // SHARDS, block), lambda at: (0, 0, at))
    half_shape = jax.ShapeDtypeStruct((SHARDS // 2, width // SHARDS, columns), jnp.bfloat16)
    d_left, kept, sent = pl.pallas_call(
        product_back_kernel,
        grid=(columns // block,),
        out_shape=(
            jax.ShapeDtypeStruct((length, width), jnp.float32),
            half_shape,
            half_shape,
        ),
        in_specs=[
            fixed,
            pl.BlockSpec((length, block), lambda at: (0, at)),
            pl.BlockSpec((width, block), lambda at: (0, at)),
        ],
        out_specs=(fixed, half, half),
        scratch_shapes=[pltpu.VMEM((width, length), jnp.bfloat16)],
        compiler_params=pltpu.CompilerParams(vmem_limit_bytes=52 << 20),
        cost_estimate=SHORT,
    )(left, upstream, weight)
    return d_left, (kept, sent)


def mlp_kernel(
    hidden_ref, upstream_ref, up_ref, bias_ref, down_ref,
    branch_ref, d_hidden_ref, up_kept_ref, up_sent_ref, down_grad_ref, bias_grad_ref,
    turned_ref,
):
    @pl.when(pl.program_id(0) == 0)
    def _():
        turned_ref[...] = hidden_ref[...].T
        branch_ref[...] = jnp.zeros_like(branch_ref)
        d_hidden_ref[...] = jnp.zeros_like(d_hidden_ref)

    hidden = hidden_ref[...]
    upstream = upstream_ref[...]
    preact = (
        jnp.dot(hidden, up_ref[...], preferred_element_type=jnp.float32) + bias_ref[...]
    )
    square = preact * preact
    bent = jnp.tanh(GELU_RATE * preact * (1.0 + GELU_CUBE * square))
    half = 0.5 * (1.0 + bent)
    slope = half + (0.5 * GELU_RATE) * preact * (1.0 - bent * bent) * (
        1.0 + (3.0 * GELU_CUBE) * square
    )
    activated = (preact * half).astype(jnp.bfloat16)
    branch_ref[...] += jnp.dot(activated, down_ref[...], preferred_element_type=jnp.float32)
    d_preact = dot_last(upstream, down_ref[...]) * slope
    d_preact = d_preact.astype(jnp.bfloat16)
    bias_grad_ref[...] = jnp.sum(d_preact.astype(jnp.float32), 0, keepdims=True)
    down_grad_ref[...] = dot_first(activated, upstream).astype(jnp.bfloat16)
    d_hidden_ref[...] += dot_last(d_preact, up_ref[...])
    up_grad = jnp.dot(turned_ref[...], d_preact, preferred_element_type=jnp.float32)
    store_halves(up_grad, up_kept_ref, up_sent_ref)


def mlp(hidden, upstream, up, bias, down):
    length, width = hidden.shape
    units = up.shape[1]
    block = 512
    fixed = pl.BlockSpec((length, width), lambda at: (0, 0))
    columns = pl.BlockSpec((width, block), lambda at: (0, at))
    lanes = pl.BlockSpec((1, block), lambda at: (0, at))
    rows = pl.BlockSpec((block, width), lambda at: (at, 0))
    half = pl.BlockSpec((SHARDS // 2, width // SHARDS, block), lambda at: (0, 0, at))
    half_shape = jax.ShapeDtypeStruct((SHARDS // 2, width // SHARDS, units), jnp.bfloat16)
    return pl.pallas_call(
        mlp_kernel,
        grid=(units // block,),
        out_shape=(
            jax.ShapeDtypeStruct((length, width), jnp.float32),
            jax.ShapeDtypeStruct((length, width), jnp.float32),
            half_shape,
            half_shape,
            jax.ShapeDtypeStruct(down.shape, jnp.bfloat16),
            jax.ShapeDtypeStruct((1, units), jnp.float32),
        ),
        in_specs=[fixed, fixed, columns, lanes, rows],
        out_specs=(fixed, fixed, half, half, rows, lanes),
        scratch_shapes=[pltpu.VMEM((width, length), jnp.bfloat16)],
        compiler_params=pltpu.CompilerParams(vmem_limit_bytes=56 << 20),
        cost_estimate=SHORT,
    )(hidden, upstream, up, bias, down)


def per_device(
    latent_in,
    condition,
    valid_slots,
    ada_weight,
    ada_bias,
    qkv_weight,
    qv_bias,
    out_weight,
    out_bias,
    up_weight,
    up_bias,
    down_weight,
    down_bias,
    cotangent,
):
    number, length, width = latent_in.shape
    place = place_of()
    fsdp_index = lax.axis_index("fsdp")
    held = (place >> 2) * 2 + (place & 1)
    rows = width // SHARDS
    replicas = lax.axis_size("rep")

    small = jnp.concatenate(
        [
            condition[0],
            qv_bias,
            out_bias,
            up_bias,
            down_bias,
            jnp.broadcast_to(valid_slots.astype(jnp.bfloat16), (128,)),
        ]
    )
    small_all = gather_group(small)
    latent_low = swap_halves(latent_in)
    pieces, order = gather_pieces(jnp.concatenate([qkv_weight, out_weight], axis=1))
    full_up = lax.all_gather(up_weight, GROUP, axis=0, tiled=True)
    cotangent_low = swap_halves(cotangent)
    full_qkv, full_out = assemble(pieces, order, (3 * width, width))
    full_down = lax.all_gather(down_weight, GROUP, axis=0, tiled=True)

    bounds = [0, width]
    for bias in (qv_bias, out_bias, up_bias, down_bias):
        bounds.append(bounds[-1] + bias.shape[0])
    cond_group = small_all[::2, :width].astype(jnp.float32)
    full_qv_bias, full_out_bias, full_up_bias, full_down_bias = (
        small_all[:, low:high].reshape(-1).astype(jnp.float32)
        for low, high in zip(bounds[1:-1], bounds[2:])
    )
    valid_group = small_all[::2, bounds[-1]].astype(jnp.float32)
    slot_mask = lax.dynamic_slice_in_dim(valid_group, held, 1)[:, None, None]

    silu_group = jax.nn.silu(cond_group).astype(jnp.bfloat16)
    silu_mine = lax.dynamic_slice_in_dim(silu_group, place * rows, rows, 1)
    ada_bias_row = lax.dynamic_update_slice_in_dim(
        jnp.zeros((ada_weight.shape[1],), jnp.float32),
        ada_bias.astype(jnp.float32),
        place * ada_bias.shape[0],
        0,
    )
    modulation = matmul(silu_mine, ada_weight) + ada_bias_row
    for bit, count in ((4, 2), (1, 1)):
        upper = (place & bit) != 0
        sent = jnp.where(upper, modulation[:count], modulation[count:])
        kept = jnp.where(upper, modulation[count:], modulation[:count])
        modulation = kept + permute(sent, lambda at: at ^ bit)
    modulation = modulation + permute(modulation, core_rule)
    shift_one, scale_one, gate_one, shift_two, scale_two, gate_two = jnp.split(
        modulation, 6, axis=-1
    )

    latent = latent_low[0].astype(jnp.float32)
    normed_one, inverse_one = normalize(latent)
    hidden_one = (normed_one * (1.0 + scale_one) + shift_one).astype(jnp.bfloat16)
    bias_full = jnp.concatenate(
        [full_qv_bias[:width], jnp.zeros((width,), jnp.float32), full_qv_bias[width:]]
    )
    projected = (matmul(hidden_one, full_qkv) + bias_full).astype(jnp.bfloat16)
    query = projected[:, :width]
    pair_own = projected[:, width:]
    pair_other = permute(pair_own, core_rule)
    heads = range(width // HEAD)
    halves = heads[: len(heads) // 2], heads[len(heads) // 2 :]
    attended_low, log_totals = attend(query, pair_own, pair_other, heads)
    log_rows = log_totals[:, : len(heads)].T[:, None, :]
    branch_one = matmul(attended_low, full_out) + full_out_bias
    middle = latent + gate_one * branch_one

    normed_two, inverse_two = normalize(middle)
    hidden_two = (normed_two * (1.0 + scale_two) + shift_two).astype(jnp.bfloat16)
    mask_row = slot_mask[0]
    d_out = cotangent_low[0].astype(jnp.float32) * mask_row
    d_branch_two = (gate_two * d_out).astype(jnp.bfloat16)
    branch_two, d_hidden_two, up_kept, up_sent, down_grad, up_bias_grad = mlp(
        hidden_two, d_branch_two, full_up, full_up_bias[None], full_down
    )
    up_scatter = Scatter((up_kept, up_sent))
    down_shard = lax.psum_scatter(down_grad, GROUP, scatter_dimension=0, tiled=True)
    branch_two = branch_two + full_down_bias
    block_out = (mask_row * (middle + gate_two * branch_two)).astype(jnp.bfloat16)
    d_gate_two = jnp.sum(d_out * branch_two, axis=0)
    down_bias_grad = jnp.sum(d_branch_two.astype(jnp.float32), axis=0)
    up_bias_grad = up_bias_grad[0]
    d_shift_two = jnp.sum(d_hidden_two, axis=0)
    d_scale_two = jnp.sum(d_hidden_two * normed_two, axis=0)
    d_middle = d_out + norm_back(d_hidden_two * (1.0 + scale_two), normed_two, inverse_two)
    d_gate_one = jnp.sum(d_middle * branch_one, axis=0)
    d_branch_one = (gate_one * d_middle).astype(jnp.bfloat16)

    d_attended, out_halves = product_back(attended_low, d_branch_one, full_out)
    d_attended = d_attended.astype(jnp.bfloat16)
    out_scatter = Scatter(out_halves)
    out_bias_grad = jnp.sum(d_branch_one.astype(jnp.float32), axis=0)
    d_attended, up_scatter.received = tie(d_attended, up_scatter.received)
    up_scatter.second()
    left = attend_back(query, pair_own, pair_other, d_attended, log_rows, halves[0])
    d_query, d_attended, out_scatter.received = tie(left[0], d_attended, out_scatter.received)
    out_scatter.second()
    right = attend_back(query, pair_own, pair_other, d_attended, log_rows, halves[1])
    *right, up_scatter.received, out_scatter.received = tie(
        *right, up_scatter.received, out_scatter.received
    )
    up_scatter.add_third()
    out_scatter.add_third()
    d_query = join_heads(d_query, right[0], width)
    d_own = join_heads(left[1], right[1], width)
    d_other = permute(join_heads(left[2], right[2], width), core_rule)
    d_own = (d_own + d_other.astype(jnp.float32)).astype(jnp.bfloat16)
    d_projected = jnp.concatenate([d_query, d_own[0], d_own[1]], axis=-1)

    d_projected, down_shard, up_scatter.sent, out_scatter.sent = tie(
        d_projected, down_shard, up_scatter.sent, out_scatter.sent
    )
    up_scatter.send_third()
    out_scatter.send_third()
    down_total = lax.psum(down_shard, "rep")
    d_hidden_one, qkv_halves = product_back(hidden_one, d_projected, full_qkv)
    qkv_scatter = Scatter(qkv_halves)
    d_hidden_one, d_projected, *arrived = tie(
        d_hidden_one,
        d_projected,
        qkv_scatter.received,
        up_scatter.received,
    )
    qkv_scatter.received, up_scatter.received = arrived
    qkv_scatter.second()
    up_sum = ReplicaSum(up_scatter.result(), replicas)
    column_sums = jnp.sum(d_projected.astype(jnp.float32), axis=0)
    d_shift_one = jnp.sum(d_hidden_one, axis=0)
    d_scale_one = jnp.sum(d_hidden_one * normed_one, axis=0)
    latent_grad = d_middle + norm_back(d_hidden_one * (1.0 + scale_one), normed_one, inverse_one)
    bias_grads = (
        jnp.concatenate([column_sums[:width], column_sums[2 * width :]]),
        out_bias_grad,
        up_bias_grad,
        down_bias_grad,
    )
    sums = [d_shift_one, d_scale_one, d_gate_one, d_shift_two, d_scale_two, d_gate_two]
    ada_width = 6 * width
    small_sums = jnp.concatenate(sums + list(bias_grads))
    qkv_scatter.received, out_scatter.received = tie(
        qkv_scatter.received, out_scatter.received
    )
    qkv_scatter.third()
    qkv_shard = qkv_scatter.result()
    qkv_shard, latent_grad, block_out, small_sums, *up_sum.received = tie(
        qkv_shard, latent_grad.astype(jnp.bfloat16), block_out, small_sums, *up_sum.received
    )
    late_sum = ReplicaSum(
        jnp.concatenate([out_scatter.result(), qkv_shard], axis=1), replicas
    )
    latent_grad = swap_halves(latent_grad[None])
    block_out = swap_halves(block_out[None])
    sums_all = gather_group(small_sums)
    up_sum.second()
    down_total, sums_all, latent_grad, block_out, *late_sum.received = tie(
        down_total, sums_all, latent_grad, block_out, *late_sum.received
    )
    late_sum.second()

    d_group = sums_all[:, :ada_width].reshape(2, 2, 2, ada_width).sum(1).reshape(4, ada_width)
    bias_mine = []
    start = ada_width
    for grad in bias_grads:
        total = jnp.sum(sums_all[:, start : start + grad.shape[0]], axis=0)
        piece = grad.shape[0] // SHARDS
        bias_mine.append(lax.dynamic_slice_in_dim(total, place * piece, piece))
        start += grad.shape[0]
    d_silu = lax.dot_general(
        d_group,
        ada_weight.astype(jnp.float32),
        (((1,), (1,)), ((), ())),
        precision=exact_mode,
    )
    cond_mine = lax.dynamic_slice_in_dim(cond_group, place * rows, rows, 1)
    cond_part = jax.vjp(jax.nn.silu, cond_mine)[1](d_silu)[0]
    cond_all = gather_group(cond_part)
    cond_grad = lax.dynamic_index_in_dim(cond_all, fsdp_index, 1, keepdims=False)
    cond_grad = cond_grad.reshape(1, width)

    packed = jnp.concatenate(
        [d_group.reshape(-1), silu_mine.astype(jnp.float32).reshape(-1)] + bias_mine
    )
    packed_all = gather_replicas(packed, replicas)
    packed_all, *late_sum.received = tie(packed_all, *late_sum.received)
    late_sum.received[0], *up_sum.received = tie(late_sum.received[0], *up_sum.received)
    up_total = up_sum.result()
    late_total = late_sum.result()
    out_total, qkv_total = late_total[:, :width], late_total[:, width:]

    d_all = packed_all[:, : 4 * ada_width].reshape(-1, ada_width)
    silu_all = packed_all[:, 4 * ada_width : 4 * ada_width + 4 * rows].reshape(-1, rows)
    ada_total = lax.dot_general(
        silu_all, d_all, (((0,), (0,)), ((), ())), precision=exact_mode
    )
    ada_bias_total = jnp.sum(
        lax.dynamic_slice_in_dim(d_all, place * ada_bias.shape[0], ada_bias.shape[0], 1), axis=0
    )
    bias_totals = jnp.sum(packed_all[:, 4 * ada_width + 4 * rows :], axis=0)
    cuts = [0]
    for piece in bias_mine:
        cuts.append(cuts[-1] + piece.shape[0])
    qv_total, out_bias_total, up_bias_total, down_bias_total = (
        bias_totals[low:high] for low, high in zip(cuts[:-1], cuts[1:])
    )
    return (
        block_out,
        latent_grad.astype(jnp.float32),
        cond_grad,
        ada_total,
        ada_bias_total,
        qkv_total.astype(jnp.float32),
        qv_total,
        out_total.astype(jnp.float32),
        out_bias_total,
        up_total.astype(jnp.float32),
        up_bias_total,
        down_total.astype(jnp.float32),
        down_bias_total,
    )


def solution(mesh):
    tokens = P(("rep", "fsdp"), "sp", None)
    rows = P(("rep", "fsdp"), None)
    matrix = P(GROUP, None)
    vector = P(GROUP)
    weights = (matrix, vector) * 5
    return jax.shard_map(
        per_device,
        mesh=mesh,
        in_specs=(tokens, rows, P(("rep", "fsdp"))) + weights + (tokens,),
        out_specs=(tokens, tokens, rows) + weights,
        check_vma=False,
    )
```

```python
import functools

import jax
import jax.numpy as jnp
from jax import lax
from jax.experimental import pallas as pl
from jax.experimental.pallas import tpu as pltpu
from jax.sharding import PartitionSpec as P

HEAD = 72
GROUP = ("fsdp", "sp")
SHARDS = 8

exact_mode = lax.Precision.HIGHEST
epsilon = 1e-06


def normalize(values):
    average = jnp.mean(values, -1, keepdims=True)
    centered = values - average
    inverse = lax.rsqrt(jnp.mean(centered * centered, -1, keepdims=True) + epsilon)
    return (centered * inverse, inverse)


def norm_back(upstream, normed, inverse):
    return (
        upstream
        - jnp.mean(upstream, -1, keepdims=True)
        - normed * jnp.mean(upstream * normed, -1, keepdims=True)
    ) * inverse


def matmul(left, right):
    return jnp.dot(left, right, preferred_element_type=jnp.float32)


def place_of():
    return lax.axis_index("fsdp") * 2 + lax.axis_index("sp")


def pairs_by(rule):
    return [(place, rule(place)) for place in range(SHARDS)]


def swap_rule(place):
    return (place & 4) | ((place & 1) << 1) | ((place >> 1) & 1)


def core_rule(place):
    return place ^ 2


def first_rule(place):
    return place ^ (1 if place & 2 else 4)


def second_rule(place):
    return place ^ (4 if place & 2 else 1)


def permute(values, rule):
    return lax.ppermute(values, GROUP, pairs_by(rule))


def swap_halves(values):
    place = place_of()
    pairs = [pair for pair in pairs_by(swap_rule) if pair[0] != pair[1]]
    received = lax.ppermute(values, GROUP, pairs)
    stays = ((place >> 1) & 1) == (place & 1)
    return jnp.where(stays, values, received)


def gather_group(values):
    place = place_of()
    stacked = values[None]
    for bit in (1, 2, 4):
        received = permute(stacked, lambda at: at ^ bit)
        stacked = jnp.where(
            (place & bit) == 0,
            jnp.concatenate([stacked, received]),
            jnp.concatenate([received, stacked]),
        )
    return stacked


def gather_replicas(values, replicas):
    stacked = [values]
    for shift in range(1, replicas):
        pairs = [(at, (at + shift) % replicas) for at in range(replicas)]
        stacked.append(lax.ppermute(values, "rep", pairs))
    return jnp.stack(stacked)


def assemble_kernel(widths, order_ref, *refs):
    pieces, wholes = refs[:SHARDS], refs[SHARDS : SHARDS + len(widths)]
    buffer, load_sems, store_sems = refs[SHARDS + len(widths) :]
    rows = buffer.shape[1]
    loads = [
        pltpu.make_async_copy(piece, buffer.at[at], load_sems.at[at])
        for at, piece in enumerate(pieces)
    ]
    for load in loads:
        load.start()
    stores = []
    for at, load in enumerate(loads):
        load.wait()
        target = pl.ds(pl.multiple_of(order_ref[at] * rows, 16), rows)
        start = 0
        for which, width in enumerate(widths):
            store = pltpu.make_async_copy(
                buffer.at[at, :, pl.ds(start, width)],
                wholes[which].at[target],
                store_sems.at[which, at],
            )
            store.start()
            stores.append(store)
            start += width
    for store in stores:
        store.wait()


def assemble(pieces, order, widths):
    rows, columns = pieces[0].shape
    size = SHARDS * rows * columns * 2
    return pl.pallas_call(
        functools.partial(assemble_kernel, widths),
        out_shape=[
            jax.ShapeDtypeStruct((SHARDS * rows, width), pieces[0].dtype) for width in widths
        ],
        in_specs=[pl.BlockSpec(memory_space=pltpu.SMEM)]
        + [pl.BlockSpec(memory_space=pl.ANY)] * SHARDS,
        out_specs=[pl.BlockSpec(memory_space=pl.ANY)] * len(widths),
        scratch_shapes=[
            pltpu.VMEM((SHARDS, rows, columns), pieces[0].dtype),
            pltpu.SemaphoreType.DMA((SHARDS,)),
            pltpu.SemaphoreType.DMA((len(widths), SHARDS)),
        ],
        compiler_params=pltpu.CompilerParams(vmem_limit_bytes=size + (4 << 20)),
        cost_estimate=SHORT,
    )(order, *pieces)


def gather_pieces(shard):
    place = place_of()
    near = jnp.where((place & 2) == 0, 4, 1)
    far = 5 - near
    other = place ^ 2
    first = permute(shard, first_rule)
    second = permute(shard, second_rule)
    both = permute(first, second_rule)
    held = [shard, first, second, both]
    pieces = held + [permute(piece, core_rule) for piece in held]
    order = [place, place ^ near, place ^ far, place ^ 5]
    order += [other, other ^ far, other ^ near, other ^ 5]
    return pieces, jnp.stack(order).astype(jnp.int32)


def tie(*values):
    return lax.optimization_barrier(values)


class Scatter:
    def __init__(self, halves):
        self.place = place_of()
        self.core = (self.place >> 1) & 1
        self.kept, sent = halves
        self.low = sent.dtype
        self.received = permute(sent, core_rule)

    def second(self):
        kept = self.kept.astype(jnp.float32) + self.received.astype(jnp.float32)
        kept = kept.astype(self.low)
        mine = ((self.place >> 2) << 1) | (self.place & 1)
        near = jnp.where(self.core == 0, 2, 1)

        def pair(which):
            parts = [which, which ^ 3 ^ near]
            return jnp.concatenate([lax.dynamic_slice_in_dim(kept, at, 1, 0) for at in parts])

        self.kept = pair(mine)
        self.received = permute(pair(mine ^ near), first_rule)

    def add_third(self):
        kept = self.kept.astype(jnp.float32) + self.received.astype(jnp.float32)
        self.kept, self.sent = kept[0], kept[1].astype(self.low)

    def send_third(self):
        self.received = permute(self.sent, second_rule)

    def third(self):
        self.add_third()
        self.send_third()

    def result(self):
        return self.kept + self.received.astype(jnp.float32)


class ReplicaSum:
    def __init__(self, partial, replicas):
        self.replicas = replicas
        self.own = lax.axis_index("rep")
        self.shape = partial.shape
        self.span = partial.shape[1] // replicas
        low = partial.astype(jnp.bfloat16)
        self.kept = self.piece(partial, self.own)
        self.received = [
            self.send(self.piece(low, self.own + shift), shift) for shift in range(1, replicas)
        ]

    def piece(self, values, which):
        return lax.dynamic_slice_in_dim(values, which % self.replicas * self.span, self.span, 1)

    def send(self, values, shift):
        pairs = [(at, (at + shift) % self.replicas) for at in range(self.replicas)]
        return lax.ppermute(values, "rep", pairs)

    def second(self):
        total = self.kept
        for received in self.received:
            total = total + received.astype(jnp.float32)
        low = total.astype(jnp.bfloat16)
        self.received = [low] + [self.send(low, shift) for shift in range(1, self.replicas)]

    def result(self):
        whole = jnp.zeros(self.shape, jnp.float32)
        for shift, received in enumerate(self.received):
            start = (self.own - shift) % self.replicas * self.span
            whole = lax.dynamic_update_slice_in_dim(whole, received.astype(jnp.float32), start, 1)
        return whole


WINDOW = 256
GELU_RATE = 0.7978845608028654
GELU_CUBE = 0.044715
SHORT = pl.CostEstimate(flops=1 << 20, bytes_accessed=1 << 20, transcendentals=0)


def head_lanes(heads, width):
    low = heads[0] * HEAD // 128 * 128
    high = -(-(heads[-1] + 1) * HEAD // 128) * 128
    return min(low, width - WINDOW), high


def head_window(first_head, width, base):
    first = (first_head + pl.program_id(0)) * HEAD
    start = jnp.minimum(first // 128 * 128, width - WINDOW)
    start = pl.multiple_of(start, 128)
    lane = lax.broadcasted_iota(jnp.int32, (1, WINDOW), 1) + start
    inside = (lane >= first) & (lane < first + HEAD)
    mask = jnp.where(inside, 1.0, 0.0).astype(jnp.bfloat16)
    lanes = [pl.ds(pl.multiple_of(start + at, 128), WINDOW) for at in (0, width, -base)]
    return (*lanes, mask)


def dot_last(left, right):
    return lax.dot_general(
        left, right, (((1,), (1,)), ((), ())), preferred_element_type=jnp.float32
    )


def dot_first(left, right):
    return lax.dot_general(
        left, right, (((0,), (0,)), ((), ())), preferred_element_type=jnp.float32
    )


def attend_kernel(first_head, base, query_ref, own_ref, other_ref, out_ref, log_ref, total_ref):
    length, width = query_ref.shape
    head = pl.program_id(0)
    key_lanes, value_lanes, out_lanes, mask = head_window(first_head, width, base)
    score_scale = float(HEAD) ** (-0.5)

    @pl.when(head == 0)
    def _():
        total_ref[...] = jnp.zeros_like(total_ref)
        log_ref[...] = jnp.zeros_like(log_ref)

    keys = jnp.concatenate([own_ref[:, key_lanes], other_ref[:, key_lanes]]) * mask
    values = jnp.concatenate([own_ref[:, value_lanes], other_ref[:, value_lanes]]) * mask
    rows = min(256, length)
    for at in range(0, length, rows):
        block = pl.ds(at, rows)
        scores = dot_last(query_ref[block, key_lanes], keys)
        row_max = jnp.max(scores, -1, keepdims=True)
        weights = jnp.exp((scores - row_max) * score_scale)
        row_total = jnp.sum(weights, -1, keepdims=True)
        probs = (weights * (1.0 / row_total)).astype(jnp.bfloat16)
        total_ref[block, out_lanes] += jnp.dot(
            probs, values, preferred_element_type=jnp.float32
        )
        log_total = row_max * score_scale + jnp.log(row_total)
        lane = lax.broadcasted_iota(jnp.int32, (rows, 128), 1)
        log_ref[block, :] = jnp.where(lane == first_head + head, log_total, log_ref[block, :])

    @pl.when(head == pl.num_programs(0) - 1)
    def _():
        out_ref[...] = total_ref[...].astype(out_ref.dtype)


def attend(query, own, other, heads):
    length, width = query.shape
    low, high = head_lanes(heads, width)
    return pl.pallas_call(
        functools.partial(attend_kernel, heads[0], low),
        grid=(len(heads),),
        out_shape=(
            jax.ShapeDtypeStruct((length, high - low), jnp.bfloat16),
            jax.ShapeDtypeStruct((length, 128), jnp.float32),
        ),
        in_specs=[
            pl.BlockSpec((length, width), lambda head: (0, 0)),
            pl.BlockSpec(own.shape, lambda head: (0, 0)),
            pl.BlockSpec(other.shape, lambda head: (0, 0)),
        ],
        out_specs=(
            pl.BlockSpec((length, high - low), lambda head: (0, 0)),
            pl.BlockSpec((length, 128), lambda head: (0, 0)),
        ),
        scratch_shapes=[pltpu.VMEM((length, high - low), jnp.float32)],
        compiler_params=pltpu.CompilerParams(vmem_limit_bytes=48 << 20),
        cost_estimate=SHORT,
    )(query, own, other)


def attend_back_kernel(
    first_head, base, query_ref, own_ref, other_ref, upstream_ref, log_ref, d_query_ref, d_own_ref, d_other_ref,
    query_total, key_total, value_total,
):
    length, width = query_ref.shape
    head = pl.program_id(0)
    key_lanes, value_lanes, out_lanes, mask = head_window(first_head, width, base)
    score_scale = float(HEAD) ** (-0.5)

    @pl.when(head == 0)
    def _():
        query_total[...] = jnp.zeros_like(query_total)
        key_total[...] = jnp.zeros_like(key_total)
        value_total[...] = jnp.zeros_like(value_total)

    keys = jnp.concatenate([own_ref[:, key_lanes], other_ref[:, key_lanes]]) * mask
    values = jnp.concatenate([own_ref[:, value_lanes], other_ref[:, value_lanes]]) * mask
    rows = min(256, length)
    for at in range(0, length, rows):
        block = pl.ds(at, rows)
        query = query_ref[block, key_lanes] * mask
        upstream = upstream_ref[block, key_lanes] * mask
        scores = dot_last(keys, query)
        probs = jnp.exp(scores * score_scale - log_ref[0, :, block])
        d_probs = dot_last(values, upstream)
        weighted = probs * d_probs
        row_sum = jnp.sum(weighted, 0, keepdims=True)
        d_scores = (weighted - probs * row_sum).astype(jnp.bfloat16)
        value_total[:, out_lanes] += jnp.dot(
            probs.astype(jnp.bfloat16), upstream, preferred_element_type=jnp.float32
        )
        key_total[:, out_lanes] += score_scale * jnp.dot(
            d_scores, query, preferred_element_type=jnp.float32
        )
        query_total[block, out_lanes] += dot_first(d_scores, keys)

    @pl.when(head == pl.num_programs(0) - 1)
    def _():
        d_query_ref[...] = (query_total[...] * score_scale).astype(d_query_ref.dtype)
        for at, total in enumerate((key_total, value_total)):
            d_own_ref[at] = total[: own_ref.shape[0]]
            d_other_ref[at] = total[own_ref.shape[0] :].astype(d_other_ref.dtype)


def attend_back(query, own, other, upstream, log_totals, heads):
    length, width = query.shape
    low, high = head_lanes(heads, width)
    span = high - low
    whole = lambda head: (0, 0)
    halves = pl.BlockSpec((2, own.shape[0], span), lambda head: (0, 0, 0))
    return pl.pallas_call(
        functools.partial(attend_back_kernel, heads[0], low),
        grid=(len(heads),),
        out_shape=(
            jax.ShapeDtypeStruct((length, span), jnp.bfloat16),
            jax.ShapeDtypeStruct((2, own.shape[0], span), jnp.float32),
            jax.ShapeDtypeStruct((2, other.shape[0], span), jnp.bfloat16),
        ),
        in_specs=[
            pl.BlockSpec((length, width), whole),
            pl.BlockSpec(own.shape, whole),
            pl.BlockSpec(other.shape, whole),
            pl.BlockSpec((length, width), whole),
            pl.BlockSpec((1, 1, length), lambda head: (heads[0] + head, 0, 0)),
        ],
        out_specs=(pl.BlockSpec((length, span), whole), halves, halves),
        scratch_shapes=[
            pltpu.VMEM((length, span), jnp.float32),
            pltpu.VMEM((own.shape[0] + other.shape[0], span), jnp.float32),
            pltpu.VMEM((own.shape[0] + other.shape[0], span), jnp.float32),
        ],
        compiler_params=pltpu.CompilerParams(vmem_limit_bytes=56 << 20),
        cost_estimate=SHORT,
    )(query, own, other, upstream, log_totals)


def join_heads(left, right, width):
    shared = left.shape[-1] + right.shape[-1] - width
    if shared == 0:
        return jnp.concatenate([left, right], axis=-1)
    edge = left.shape[-1] - shared
    middle = left[..., edge:] + right[..., :shared]
    return jnp.concatenate([left[..., :edge], middle, right[..., shared:]], axis=-1)


def store_halves(grad, kept_ref, sent_ref):
    core = lax.axis_index("fsdp") % 2
    rows = grad.shape[0] // SHARDS
    low = grad.astype(kept_ref.dtype)
    for owner in (0, 1):
        blocks = [at for at in range(SHARDS) if (at >> 1) & 1 == owner]

        @pl.when(core == owner)
        def _():
            for slot, at in enumerate(blocks):
                kept_ref[slot] = low[at * rows : (at + 1) * rows]

        @pl.when(core != owner)
        def _():
            for slot, at in enumerate(blocks):
                sent_ref[slot] = low[at * rows : (at + 1) * rows]


def product_back_kernel(
    left_ref, upstream_ref, weight_ref, d_left_ref, kept_ref, sent_ref, turned_ref
):
    @pl.when(pl.program_id(0) == 0)
    def _():
        turned_ref[...] = left_ref[...].T
        d_left_ref[...] = jnp.zeros_like(d_left_ref)

    upstream = upstream_ref[...]
    grad = jnp.dot(turned_ref[...], upstream, preferred_element_type=jnp.float32)
    store_halves(grad, kept_ref, sent_ref)
    d_left_ref[...] += dot_last(upstream, weight_ref[...])


def product_back(left, upstream, weight):
    length, width = left.shape
    columns = weight.shape[1]
    block = width
    fixed = pl.BlockSpec((length, width), lambda at: (0, 0))
    half = pl.BlockSpec((SHARDS // 2, width // SHARDS, block), lambda at: (0, 0, at))
    half_shape = jax.ShapeDtypeStruct((SHARDS // 2, width // SHARDS, columns), jnp.bfloat16)
    d_left, kept, sent = pl.pallas_call(
        product_back_kernel,
        grid=(columns // block,),
        out_shape=(
            jax.ShapeDtypeStruct((length, width), jnp.float32),
            half_shape,
            half_shape,
        ),
        in_specs=[
            fixed,
            pl.BlockSpec((length, block), lambda at: (0, at)),
            pl.BlockSpec((width, block), lambda at: (0, at)),
        ],
        out_specs=(fixed, half, half),
        scratch_shapes=[pltpu.VMEM((width, length), jnp.bfloat16)],
        compiler_params=pltpu.CompilerParams(vmem_limit_bytes=52 << 20),
        cost_estimate=SHORT,
    )(left, upstream, weight)
    return d_left, (kept, sent)


def mlp_kernel(
    hidden_ref, upstream_ref, up_ref, bias_ref, down_ref,
    branch_ref, d_hidden_ref, up_kept_ref, up_sent_ref, down_grad_ref, bias_grad_ref,
    turned_ref,
):
    @pl.when(pl.program_id(0) == 0)
    def _():
        turned_ref[...] = hidden_ref[...].T
        branch_ref[...] = jnp.zeros_like(branch_ref)
        d_hidden_ref[...] = jnp.zeros_like(d_hidden_ref)

    hidden = hidden_ref[...]
    upstream = upstream_ref[...]
    preact = (
        jnp.dot(hidden, up_ref[...], preferred_element_type=jnp.float32) + bias_ref[...]
    )
    square = preact * preact
    bent = jnp.tanh(GELU_RATE * preact * (1.0 + GELU_CUBE * square))
    half = 0.5 * (1.0 + bent)
    slope = half + (0.5 * GELU_RATE) * preact * (1.0 - bent * bent) * (
        1.0 + (3.0 * GELU_CUBE) * square
    )
    activated = (preact * half).astype(jnp.bfloat16)
    branch_ref[...] += jnp.dot(activated, down_ref[...], preferred_element_type=jnp.float32)
    d_preact = dot_last(upstream, down_ref[...]) * slope
    d_preact = d_preact.astype(jnp.bfloat16)
    bias_grad_ref[...] = jnp.sum(d_preact.astype(jnp.float32), 0, keepdims=True)
    down_grad_ref[...] = dot_first(activated, upstream).astype(jnp.bfloat16)
    d_hidden_ref[...] += dot_last(d_preact, up_ref[...])
    up_grad = jnp.dot(turned_ref[...], d_preact, preferred_element_type=jnp.float32)
    store_halves(up_grad, up_kept_ref, up_sent_ref)


def mlp(hidden, upstream, up, bias, down):
    length, width = hidden.shape
    units = up.shape[1]
    block = 512
    fixed = pl.BlockSpec((length, width), lambda at: (0, 0))
    columns = pl.BlockSpec((width, block), lambda at: (0, at))
    lanes = pl.BlockSpec((1, block), lambda at: (0, at))
    rows = pl.BlockSpec((block, width), lambda at: (at, 0))
    half = pl.BlockSpec((SHARDS // 2, width // SHARDS, block), lambda at: (0, 0, at))
    half_shape = jax.ShapeDtypeStruct((SHARDS // 2, width // SHARDS, units), jnp.bfloat16)
    return pl.pallas_call(
        mlp_kernel,
        grid=(units // block,),
        out_shape=(
            jax.ShapeDtypeStruct((length, width), jnp.float32),
            jax.ShapeDtypeStruct((length, width), jnp.float32),
            half_shape,
            half_shape,
            jax.ShapeDtypeStruct(down.shape, jnp.bfloat16),
            jax.ShapeDtypeStruct((1, units), jnp.float32),
        ),
        in_specs=[fixed, fixed, columns, lanes, rows],
        out_specs=(fixed, fixed, half, half, rows, lanes),
        scratch_shapes=[pltpu.VMEM((width, length), jnp.bfloat16)],
        compiler_params=pltpu.CompilerParams(vmem_limit_bytes=56 << 20),
        cost_estimate=SHORT,
    )(hidden, upstream, up, bias, down)


def per_device(
    latent_in,
    condition,
    valid_slots,
    ada_weight,
    ada_bias,
    qkv_weight,
    qv_bias,
    out_weight,
    out_bias,
    up_weight,
    up_bias,
    down_weight,
    down_bias,
    cotangent,
):
    number, length, width = latent_in.shape
    place = place_of()
    fsdp_index = lax.axis_index("fsdp")
    held = (place >> 2) * 2 + (place & 1)
    rows = width // SHARDS
    replicas = lax.axis_size("rep")

    small = jnp.concatenate(
        [
            condition[0],
            qv_bias,
            out_bias,
            up_bias,
            down_bias,
            jnp.broadcast_to(valid_slots.astype(jnp.bfloat16), (128,)),
        ]
    )
    small_all = gather_group(small)
    latent_low = swap_halves(latent_in)
    pieces, order = gather_pieces(jnp.concatenate([qkv_weight, out_weight], axis=1))
    full_up = lax.all_gather(up_weight, GROUP, axis=0, tiled=True)
    cotangent_low = swap_halves(cotangent)
    full_qkv, full_out = assemble(pieces, order, (3 * width, width))
    full_down = lax.all_gather(down_weight, GROUP, axis=0, tiled=True)

    bounds = [0, width]
    for bias in (qv_bias, out_bias, up_bias, down_bias):
        bounds.append(bounds[-1] + bias.shape[0])
    cond_group = small_all[::2, :width].astype(jnp.float32)
    full_qv_bias, full_out_bias, full_up_bias, full_down_bias = (
        small_all[:, low:high].reshape(-1).astype(jnp.float32)
        for low, high in zip(bounds[1:-1], bounds[2:])
    )
    valid_group = small_all[::2, bounds[-1]].astype(jnp.float32)
    slot_mask = lax.dynamic_slice_in_dim(valid_group, held, 1)[:, None, None]

    silu_group = jax.nn.silu(cond_group).astype(jnp.bfloat16)
    silu_mine = lax.dynamic_slice_in_dim(silu_group, place * rows, rows, 1)
    ada_bias_row = lax.dynamic_update_slice_in_dim(
        jnp.zeros((ada_weight.shape[1],), jnp.float32),
        ada_bias.astype(jnp.float32),
        place * ada_bias.shape[0],
        0,
    )
    modulation = matmul(silu_mine, ada_weight) + ada_bias_row
    for bit, count in ((4, 2), (1, 1)):
        upper = (place & bit) != 0
        sent = jnp.where(upper, modulation[:count], modulation[count:])
        kept = jnp.where(upper, modulation[count:], modulation[:count])
        modulation = kept + permute(sent, lambda at: at ^ bit)
    modulation = modulation + permute(modulation, core_rule)
    shift_one, scale_one, gate_one, shift_two, scale_two, gate_two = jnp.split(
        modulation, 6, axis=-1
    )

    latent = latent_low[0].astype(jnp.float32)
    normed_one, inverse_one = normalize(latent)
    hidden_one = (normed_one * (1.0 + scale_one) + shift_one).astype(jnp.bfloat16)
    bias_full = jnp.concatenate(
        [full_qv_bias[:width], jnp.zeros((width,), jnp.float32), full_qv_bias[width:]]
    )
    projected = (matmul(hidden_one, full_qkv) + bias_full).astype(jnp.bfloat16)
    query = projected[:, :width]
    pair_own = projected[:, width:]
    pair_other = permute(pair_own, core_rule)
    heads = range(width // HEAD)
    halves = heads[: len(heads) // 2], heads[len(heads) // 2 :]
    attended_low, log_totals = attend(query, pair_own, pair_other, heads)
    log_rows = log_totals[:, : len(heads)].T[:, None, :]
    branch_one = matmul(attended_low, full_out) + full_out_bias
    middle = latent + gate_one * branch_one

    normed_two, inverse_two = normalize(middle)
    hidden_two = (normed_two * (1.0 + scale_two) + shift_two).astype(jnp.bfloat16)
    mask_row = slot_mask[0]
    d_out = cotangent_low[0].astype(jnp.float32) * mask_row
    d_branch_two = (gate_two * d_out).astype(jnp.bfloat16)
    branch_two, d_hidden_two, up_kept, up_sent, down_grad, up_bias_grad = mlp(
        hidden_two, d_branch_two, full_up, full_up_bias[None], full_down
    )
    up_scatter = Scatter((up_kept, up_sent))
    down_shard = lax.psum_scatter(down_grad, GROUP, scatter_dimension=0, tiled=True)
    branch_two = branch_two + full_down_bias
    block_out = (mask_row * (middle + gate_two * branch_two)).astype(jnp.bfloat16)
    d_gate_two = jnp.sum(d_out * branch_two, axis=0)
    down_bias_grad = jnp.sum(d_branch_two.astype(jnp.float32), axis=0)
    up_bias_grad = up_bias_grad[0]
    d_shift_two = jnp.sum(d_hidden_two, axis=0)
    d_scale_two = jnp.sum(d_hidden_two * normed_two, axis=0)
    d_middle = d_out + norm_back(d_hidden_two * (1.0 + scale_two), normed_two, inverse_two)
    d_gate_one = jnp.sum(d_middle * branch_one, axis=0)
    d_branch_one = (gate_one * d_middle).astype(jnp.bfloat16)

    d_attended, out_halves = product_back(attended_low, d_branch_one, full_out)
    d_attended = d_attended.astype(jnp.bfloat16)
    out_scatter = Scatter(out_halves)
    out_bias_grad = jnp.sum(d_branch_one.astype(jnp.float32), axis=0)
    d_attended, up_scatter.received = tie(d_attended, up_scatter.received)
    up_scatter.second()
    left = attend_back(query, pair_own, pair_other, d_attended, log_rows, halves[0])
    d_query, d_attended, out_scatter.received = tie(left[0], d_attended, out_scatter.received)
    out_scatter.second()
    right = attend_back(query, pair_own, pair_other, d_attended, log_rows, halves[1])
    d_other = permute(join_heads(left[2], right[2], width), core_rule)
    d_right, up_scatter.received, out_scatter.received = tie(
        right[1], up_scatter.received, out_scatter.received
    )
    up_scatter.add_third()
    out_scatter.add_third()
    d_query = join_heads(d_query, right[0], width)
    d_own = join_heads(left[1], d_right, width)
    d_own = (d_own + d_other.astype(jnp.float32)).astype(jnp.bfloat16)
    d_projected = jnp.concatenate([d_query, d_own[0], d_own[1]], axis=-1)

    d_projected, down_shard, up_scatter.sent, out_scatter.sent = tie(
        d_projected, down_shard, up_scatter.sent, out_scatter.sent
    )
    up_scatter.send_third()
    out_scatter.send_third()
    down_total = lax.psum(down_shard, "rep")
    d_hidden_one, qkv_halves = product_back(hidden_one, d_projected, full_qkv)
    qkv_scatter = Scatter(qkv_halves)
    d_hidden_one, d_projected, *arrived = tie(
        d_hidden_one,
        d_projected,
        qkv_scatter.received,
        up_scatter.received,
    )
    qkv_scatter.received, up_scatter.received = arrived
    qkv_scatter.second()
    up_sum = ReplicaSum(up_scatter.result(), replicas)
    column_sums = jnp.sum(d_projected.astype(jnp.float32), axis=0)
    d_shift_one = jnp.sum(d_hidden_one, axis=0)
    d_scale_one = jnp.sum(d_hidden_one * normed_one, axis=0)
    latent_grad = d_middle + norm_back(d_hidden_one * (1.0 + scale_one), normed_one, inverse_one)
    bias_grads = (
        jnp.concatenate([column_sums[:width], column_sums[2 * width :]]),
        out_bias_grad,
        up_bias_grad,
        down_bias_grad,
    )
    sums = [d_shift_one, d_scale_one, d_gate_one, d_shift_two, d_scale_two, d_gate_two]
    ada_width = 6 * width
    small_sums = jnp.concatenate(sums + list(bias_grads))
    qkv_scatter.received, out_scatter.received = tie(
        qkv_scatter.received, out_scatter.received
    )
    qkv_scatter.third()
    qkv_shard = qkv_scatter.result()
    qkv_shard, latent_grad, block_out, small_sums, *up_sum.received = tie(
        qkv_shard, latent_grad.astype(jnp.bfloat16), block_out, small_sums, *up_sum.received
    )
    late_sum = ReplicaSum(
        jnp.concatenate([out_scatter.result(), qkv_shard], axis=1), replicas
    )
    latent_grad = swap_halves(latent_grad[None])
    block_out = swap_halves(block_out[None])
    sums_all = gather_group(small_sums)
    up_sum.second()
    down_total, sums_all, latent_grad, block_out, *late_sum.received = tie(
        down_total, sums_all, latent_grad, block_out, *late_sum.received
    )
    late_sum.second()

    d_group = sums_all[:, :ada_width].reshape(2, 2, 2, ada_width).sum(1).reshape(4, ada_width)
    bias_mine = []
    start = ada_width
    for grad in bias_grads:
        total = jnp.sum(sums_all[:, start : start + grad.shape[0]], axis=0)
        piece = grad.shape[0] // SHARDS
        bias_mine.append(lax.dynamic_slice_in_dim(total, place * piece, piece))
        start += grad.shape[0]
    d_silu = lax.dot_general(
        d_group,
        ada_weight.astype(jnp.float32),
        (((1,), (1,)), ((), ())),
        precision=exact_mode,
    )
    cond_mine = lax.dynamic_slice_in_dim(cond_group, place * rows, rows, 1)
    cond_part = jax.vjp(jax.nn.silu, cond_mine)[1](d_silu)[0]
    cond_all = gather_group(cond_part)
    cond_grad = lax.dynamic_index_in_dim(cond_all, fsdp_index, 1, keepdims=False)
    cond_grad = cond_grad.reshape(1, width)

    packed = jnp.concatenate(
        [d_group.reshape(-1), silu_mine.astype(jnp.float32).reshape(-1)] + bias_mine
    )
    packed_all = gather_replicas(packed, replicas)
    packed_all, *late_sum.received = tie(packed_all, *late_sum.received)
    late_sum.received[0], *up_sum.received = tie(late_sum.received[0], *up_sum.received)
    up_total = up_sum.result()
    late_total = late_sum.result()
    out_total, qkv_total = late_total[:, :width], late_total[:, width:]

    d_all = packed_all[:, : 4 * ada_width].reshape(-1, ada_width)
    silu_all = packed_all[:, 4 * ada_width : 4 * ada_width + 4 * rows].reshape(-1, rows)
    ada_total = lax.dot_general(
        silu_all, d_all, (((0,), (0,)), ((), ())), precision=exact_mode
    )
    ada_bias_total = jnp.sum(
        lax.dynamic_slice_in_dim(d_all, place * ada_bias.shape[0], ada_bias.shape[0], 1), axis=0
    )
    bias_totals = jnp.sum(packed_all[:, 4 * ada_width + 4 * rows :], axis=0)
    cuts = [0]
    for piece in bias_mine:
        cuts.append(cuts[-1] + piece.shape[0])
    qv_total, out_bias_total, up_bias_total, down_bias_total = (
        bias_totals[low:high] for low, high in zip(cuts[:-1], cuts[1:])
    )
    return (
        block_out,
        latent_grad.astype(jnp.float32),
        cond_grad,
        ada_total,
        ada_bias_total,
        qkv_total.astype(jnp.float32),
        qv_total,
        out_total.astype(jnp.float32),
        out_bias_total,
        up_total.astype(jnp.float32),
        up_bias_total,
        down_total.astype(jnp.float32),
        down_bias_total,
    )


def solution(mesh):
    tokens = P(("rep", "fsdp"), "sp", None)
    rows = P(("rep", "fsdp"), None)
    matrix = P(GROUP, None)
    vector = P(GROUP)
    weights = (matrix, vector) * 5
    return jax.shard_map(
        per_device,
        mesh=mesh,
        in_specs=(tokens, rows, P(("rep", "fsdp"))) + weights + (tokens,),
        out_specs=(tokens, tokens, rows) + weights,
        check_vma=False,
    )
```

```python
import functools

import jax
import jax.numpy as jnp
from jax import lax
from jax.experimental import pallas as pl
from jax.experimental.pallas import tpu as pltpu
from jax.sharding import PartitionSpec as P

HEAD = 72
GROUP = ("fsdp", "sp")
SHARDS = 8

exact_mode = lax.Precision.HIGHEST
epsilon = 1e-06


def normalize(values):
    average = jnp.mean(values, -1, keepdims=True)
    centered = values - average
    inverse = lax.rsqrt(jnp.mean(centered * centered, -1, keepdims=True) + epsilon)
    return (centered * inverse, inverse)


def norm_back(upstream, normed, inverse):
    return (
        upstream
        - jnp.mean(upstream, -1, keepdims=True)
        - normed * jnp.mean(upstream * normed, -1, keepdims=True)
    ) * inverse


def matmul(left, right):
    return jnp.dot(left, right, preferred_element_type=jnp.float32)


def place_of():
    return lax.axis_index("fsdp") * 2 + lax.axis_index("sp")


def pairs_by(rule):
    return [(place, rule(place)) for place in range(SHARDS)]


def swap_rule(place):
    return (place & 4) | ((place & 1) << 1) | ((place >> 1) & 1)


def core_rule(place):
    return place ^ 2


def first_rule(place):
    return place ^ (1 if place & 2 else 4)


def second_rule(place):
    return place ^ (4 if place & 2 else 1)


def permute(values, rule):
    return lax.ppermute(values, GROUP, pairs_by(rule))


def swap_halves(values):
    place = place_of()
    pairs = [pair for pair in pairs_by(swap_rule) if pair[0] != pair[1]]
    received = lax.ppermute(values, GROUP, pairs)
    stays = ((place >> 1) & 1) == (place & 1)
    return jnp.where(stays, values, received)


def gather_group(values):
    place = place_of()
    stacked = values[None]
    for bit in (1, 2, 4):
        received = permute(stacked, lambda at: at ^ bit)
        stacked = jnp.where(
            (place & bit) == 0,
            jnp.concatenate([stacked, received]),
            jnp.concatenate([received, stacked]),
        )
    return stacked


def gather_replicas(values, replicas):
    stacked = [values]
    for shift in range(1, replicas):
        pairs = [(at, (at + shift) % replicas) for at in range(replicas)]
        stacked.append(lax.ppermute(values, "rep", pairs))
    return jnp.stack(stacked)


def assemble_kernel(widths, order_ref, *refs):
    pieces, wholes = refs[:SHARDS], refs[SHARDS : SHARDS + len(widths)]
    buffer, load_sems, store_sems = refs[SHARDS + len(widths) :]
    rows = buffer.shape[1]
    loads = [
        pltpu.make_async_copy(piece, buffer.at[at], load_sems.at[at])
        for at, piece in enumerate(pieces)
    ]
    for load in loads:
        load.start()
    stores = []
    for at, load in enumerate(loads):
        load.wait()
        target = pl.ds(pl.multiple_of(order_ref[at] * rows, 16), rows)
        start = 0
        for which, width in enumerate(widths):
            store = pltpu.make_async_copy(
                buffer.at[at, :, pl.ds(start, width)],
                wholes[which].at[target],
                store_sems.at[which, at],
            )
            store.start()
            stores.append(store)
            start += width
    for store in stores:
        store.wait()


def assemble(pieces, order, widths):
    rows, columns = pieces[0].shape
    size = SHARDS * rows * columns * 2
    return pl.pallas_call(
        functools.partial(assemble_kernel, widths),
        out_shape=[
            jax.ShapeDtypeStruct((SHARDS * rows, width), pieces[0].dtype) for width in widths
        ],
        in_specs=[pl.BlockSpec(memory_space=pltpu.SMEM)]
        + [pl.BlockSpec(memory_space=pl.ANY)] * SHARDS,
        out_specs=[pl.BlockSpec(memory_space=pl.ANY)] * len(widths),
        scratch_shapes=[
            pltpu.VMEM((SHARDS, rows, columns), pieces[0].dtype),
            pltpu.SemaphoreType.DMA((SHARDS,)),
            pltpu.SemaphoreType.DMA((len(widths), SHARDS)),
        ],
        compiler_params=pltpu.CompilerParams(vmem_limit_bytes=size + (4 << 20)),
        cost_estimate=SHORT,
    )(order, *pieces)


def gather_pieces(shard):
    place = place_of()
    near = jnp.where((place & 2) == 0, 4, 1)
    far = 5 - near
    other = place ^ 2
    first = permute(shard, first_rule)
    second = permute(shard, second_rule)
    both = permute(first, second_rule)
    held = [shard, first, second, both]
    pieces = held + [permute(piece, core_rule) for piece in held]
    order = [place, place ^ near, place ^ far, place ^ 5]
    order += [other, other ^ far, other ^ near, other ^ 5]
    return pieces, jnp.stack(order).astype(jnp.int32)


def tie(*values):
    return lax.optimization_barrier(values)


class Scatter:
    def __init__(self, halves):
        self.place = place_of()
        self.core = (self.place >> 1) & 1
        self.kept, sent = halves
        self.low = sent.dtype
        self.received = permute(sent, core_rule)

    def second(self):
        kept = self.kept.astype(jnp.float32) + self.received.astype(jnp.float32)
        kept = kept.astype(self.low)
        mine = ((self.place >> 2) << 1) | (self.place & 1)
        near = jnp.where(self.core == 0, 2, 1)

        def pair(which):
            parts = [which, which ^ 3 ^ near]
            return jnp.concatenate([lax.dynamic_slice_in_dim(kept, at, 1, 0) for at in parts])

        self.kept = pair(mine)
        self.received = permute(pair(mine ^ near), first_rule)

    def add_third(self):
        kept = self.kept.astype(jnp.float32) + self.received.astype(jnp.float32)
        self.kept, self.sent = kept[0], kept[1].astype(self.low)

    def send_third(self):
        self.received = permute(self.sent, second_rule)

    def third(self):
        self.add_third()
        self.send_third()

    def result(self):
        return self.kept + self.received.astype(jnp.float32)


class ReplicaSum:
    def __init__(self, partial, replicas):
        self.replicas = replicas
        self.own = lax.axis_index("rep")
        self.shape = partial.shape
        self.span = partial.shape[1] // replicas
        low = partial.astype(jnp.bfloat16)
        self.kept = self.piece(partial, self.own)
        self.received = [
            self.send(self.piece(low, self.own + shift), shift) for shift in range(1, replicas)
        ]

    def piece(self, values, which):
        return lax.dynamic_slice_in_dim(values, which % self.replicas * self.span, self.span, 1)

    def send(self, values, shift):
        pairs = [(at, (at + shift) % self.replicas) for at in range(self.replicas)]
        return lax.ppermute(values, "rep", pairs)

    def second(self):
        total = self.kept
        for received in self.received:
            total = total + received.astype(jnp.float32)
        low = total.astype(jnp.bfloat16)
        self.received = [low] + [self.send(low, shift) for shift in range(1, self.replicas)]

    def result(self):
        whole = jnp.zeros(self.shape, jnp.float32)
        for shift, received in enumerate(self.received):
            start = (self.own - shift) % self.replicas * self.span
            whole = lax.dynamic_update_slice_in_dim(whole, received.astype(jnp.float32), start, 1)
        return whole


WINDOW = 256
GELU_RATE = 0.7978845608028654
GELU_CUBE = 0.044715
SHORT = pl.CostEstimate(flops=1 << 20, bytes_accessed=1 << 20, transcendentals=0)


def head_lanes(heads, width):
    low = heads[0] * HEAD // 128 * 128
    high = -(-(heads[-1] + 1) * HEAD // 128) * 128
    return min(low, width - WINDOW), high


def head_window(first_head, width, base):
    first = (first_head + pl.program_id(0)) * HEAD
    start = jnp.minimum(first // 128 * 128, width - WINDOW)
    start = pl.multiple_of(start, 128)
    lane = lax.broadcasted_iota(jnp.int32, (1, WINDOW), 1) + start
    inside = (lane >= first) & (lane < first + HEAD)
    mask = jnp.where(inside, 1.0, 0.0).astype(jnp.bfloat16)
    lanes = [pl.ds(pl.multiple_of(start + at, 128), WINDOW) for at in (0, width, -base)]
    return (*lanes, mask)


def dot_last(left, right):
    return lax.dot_general(
        left, right, (((1,), (1,)), ((), ())), preferred_element_type=jnp.float32
    )


def dot_first(left, right):
    return lax.dot_general(
        left, right, (((0,), (0,)), ((), ())), preferred_element_type=jnp.float32
    )


def attend_kernel(first_head, base, query_ref, own_ref, other_ref, out_ref, log_ref, total_ref):
    length, width = query_ref.shape
    head = pl.program_id(0)
    key_lanes, value_lanes, out_lanes, mask = head_window(first_head, width, base)
    score_scale = float(HEAD) ** (-0.5)

    @pl.when(head == 0)
    def _():
        total_ref[...] = jnp.zeros_like(total_ref)
        log_ref[...] = jnp.zeros_like(log_ref)

    keys = jnp.concatenate([own_ref[:, key_lanes], other_ref[:, key_lanes]]) * mask
    values = jnp.concatenate([own_ref[:, value_lanes], other_ref[:, value_lanes]]) * mask
    rows = min(256, length)
    for at in range(0, length, rows):
        block = pl.ds(at, rows)
        scores = dot_last(query_ref[block, key_lanes], keys)
        row_max = jnp.max(scores, -1, keepdims=True)
        weights = jnp.exp((scores - row_max) * score_scale)
        row_total = jnp.sum(weights, -1, keepdims=True)
        probs = (weights * (1.0 / row_total)).astype(jnp.bfloat16)
        total_ref[block, out_lanes] += jnp.dot(
            probs, values, preferred_element_type=jnp.float32
        )
        log_total = row_max * score_scale + jnp.log(row_total)
        lane = lax.broadcasted_iota(jnp.int32, (rows, 128), 1)
        log_ref[block, :] = jnp.where(lane == first_head + head, log_total, log_ref[block, :])

    @pl.when(head == pl.num_programs(0) - 1)
    def _():
        out_ref[...] = total_ref[...].astype(out_ref.dtype)


def attend(query, own, other, heads):
    length, width = query.shape
    low, high = head_lanes(heads, width)
    return pl.pallas_call(
        functools.partial(attend_kernel, heads[0], low),
        grid=(len(heads),),
        out_shape=(
            jax.ShapeDtypeStruct((length, high - low), jnp.bfloat16),
            jax.ShapeDtypeStruct((length, 128), jnp.float32),
        ),
        in_specs=[
            pl.BlockSpec((length, width), lambda head: (0, 0)),
            pl.BlockSpec(own.shape, lambda head: (0, 0)),
            pl.BlockSpec(other.shape, lambda head: (0, 0)),
        ],
        out_specs=(
            pl.BlockSpec((length, high - low), lambda head: (0, 0)),
            pl.BlockSpec((length, 128), lambda head: (0, 0)),
        ),
        scratch_shapes=[pltpu.VMEM((length, high - low), jnp.float32)],
        compiler_params=pltpu.CompilerParams(vmem_limit_bytes=48 << 20),
        cost_estimate=SHORT,
    )(query, own, other)


def attend_back_kernel(
    first_head, base, query_ref, own_ref, other_ref, upstream_ref, log_ref, d_query_ref, d_own_ref, d_other_ref,
    query_total, key_total, value_total,
):
    length, width = query_ref.shape
    head = pl.program_id(0)
    key_lanes, value_lanes, out_lanes, mask = head_window(first_head, width, base)
    score_scale = float(HEAD) ** (-0.5)

    @pl.when(head == 0)
    def _():
        query_total[...] = jnp.zeros_like(query_total)
        key_total[...] = jnp.zeros_like(key_total)
        value_total[...] = jnp.zeros_like(value_total)

    keys = jnp.concatenate([own_ref[:, key_lanes], other_ref[:, key_lanes]]) * mask
    values = jnp.concatenate([own_ref[:, value_lanes], other_ref[:, value_lanes]]) * mask
    rows = min(256, length)
    for at in range(0, length, rows):
        block = pl.ds(at, rows)
        query = query_ref[block, key_lanes] * mask
        upstream = upstream_ref[block, key_lanes] * mask
        scores = dot_last(keys, query)
        probs = jnp.exp(scores * score_scale - log_ref[0, :, block])
        d_probs = dot_last(values, upstream)
        weighted = probs * d_probs
        row_sum = jnp.sum(weighted, 0, keepdims=True)
        d_scores = (weighted - probs * row_sum).astype(jnp.bfloat16)
        value_total[:, out_lanes] += jnp.dot(
            probs.astype(jnp.bfloat16), upstream, preferred_element_type=jnp.float32
        )
        key_total[:, out_lanes] += score_scale * jnp.dot(
            d_scores, query, preferred_element_type=jnp.float32
        )
        query_total[block, out_lanes] += dot_first(d_scores, keys)

    @pl.when(head == pl.num_programs(0) - 1)
    def _():
        d_query_ref[...] = (query_total[...] * score_scale).astype(d_query_ref.dtype)
        for at, total in enumerate((key_total, value_total)):
            d_own_ref[at] = total[: own_ref.shape[0]]
            d_other_ref[at] = total[own_ref.shape[0] :].astype(d_other_ref.dtype)


def attend_back(query, own, other, upstream, log_totals, heads):
    length, width = query.shape
    low, high = head_lanes(heads, width)
    span = high - low
    whole = lambda head: (0, 0)
    halves = pl.BlockSpec((2, own.shape[0], span), lambda head: (0, 0, 0))
    return pl.pallas_call(
        functools.partial(attend_back_kernel, heads[0], low),
        grid=(len(heads),),
        out_shape=(
            jax.ShapeDtypeStruct((length, span), jnp.bfloat16),
            jax.ShapeDtypeStruct((2, own.shape[0], span), jnp.float32),
            jax.ShapeDtypeStruct((2, other.shape[0], span), jnp.bfloat16),
        ),
        in_specs=[
            pl.BlockSpec((length, width), whole),
            pl.BlockSpec(own.shape, whole),
            pl.BlockSpec(other.shape, whole),
            pl.BlockSpec((length, width), whole),
            pl.BlockSpec((1, 1, length), lambda head: (heads[0] + head, 0, 0)),
        ],
        out_specs=(pl.BlockSpec((length, span), whole), halves, halves),
        scratch_shapes=[
            pltpu.VMEM((length, span), jnp.float32),
            pltpu.VMEM((own.shape[0] + other.shape[0], span), jnp.float32),
            pltpu.VMEM((own.shape[0] + other.shape[0], span), jnp.float32),
        ],
        compiler_params=pltpu.CompilerParams(vmem_limit_bytes=56 << 20),
        cost_estimate=SHORT,
    )(query, own, other, upstream, log_totals)


def join_heads(left, right, width):
    shared = left.shape[-1] + right.shape[-1] - width
    if shared == 0:
        return jnp.concatenate([left, right], axis=-1)
    edge = left.shape[-1] - shared
    middle = left[..., edge:] + right[..., :shared]
    return jnp.concatenate([left[..., :edge], middle, right[..., shared:]], axis=-1)


def store_halves(grad, kept_ref, sent_ref):
    core = lax.axis_index("fsdp") % 2
    rows = grad.shape[0] // SHARDS
    low = grad.astype(kept_ref.dtype)
    for owner in (0, 1):
        blocks = [at for at in range(SHARDS) if (at >> 1) & 1 == owner]

        @pl.when(core == owner)
        def _():
            for slot, at in enumerate(blocks):
                kept_ref[slot] = low[at * rows : (at + 1) * rows]

        @pl.when(core != owner)
        def _():
            for slot, at in enumerate(blocks):
                sent_ref[slot] = low[at * rows : (at + 1) * rows]


def product_back_kernel(
    left_ref, upstream_ref, weight_ref, d_left_ref, kept_ref, sent_ref, turned_ref
):
    @pl.when(pl.program_id(0) == 0)
    def _():
        turned_ref[...] = left_ref[...].T
        d_left_ref[...] = jnp.zeros_like(d_left_ref)

    upstream = upstream_ref[...]
    grad = jnp.dot(turned_ref[...], upstream, preferred_element_type=jnp.float32)
    store_halves(grad, kept_ref, sent_ref)
    d_left_ref[...] += dot_last(upstream, weight_ref[...])


def product_back(left, upstream, weight):
    length, width = left.shape
    columns = weight.shape[1]
    block = width
    fixed = pl.BlockSpec((length, width), lambda at: (0, 0))
    half = pl.BlockSpec((SHARDS // 2, width // SHARDS, block), lambda at: (0, 0, at))
    half_shape = jax.ShapeDtypeStruct((SHARDS // 2, width // SHARDS, columns), jnp.bfloat16)
    d_left, kept, sent = pl.pallas_call(
        product_back_kernel,
        grid=(columns // block,),
        out_shape=(
            jax.ShapeDtypeStruct((length, width), jnp.float32),
            half_shape,
            half_shape,
        ),
        in_specs=[
            fixed,
            pl.BlockSpec((length, block), lambda at: (0, at)),
            pl.BlockSpec((width, block), lambda at: (0, at)),
        ],
        out_specs=(fixed, half, half),
        scratch_shapes=[pltpu.VMEM((width, length), jnp.bfloat16)],
        compiler_params=pltpu.CompilerParams(vmem_limit_bytes=52 << 20),
        cost_estimate=SHORT,
    )(left, upstream, weight)
    return d_left, (kept, sent)


def mlp_kernel(
    hidden_ref, upstream_ref, up_ref, bias_ref, down_ref,
    branch_ref, d_hidden_ref, up_kept_ref, up_sent_ref, down_grad_ref, bias_grad_ref,
    turned_ref,
):
    @pl.when(pl.program_id(0) == 0)
    def _():
        turned_ref[...] = hidden_ref[...].T
        branch_ref[...] = jnp.zeros_like(branch_ref)
        d_hidden_ref[...] = jnp.zeros_like(d_hidden_ref)

    hidden = hidden_ref[...]
    upstream = upstream_ref[...]
    preact = (
        jnp.dot(hidden, up_ref[...], preferred_element_type=jnp.float32) + bias_ref[...]
    )
    square = preact * preact
    bent = jnp.tanh(GELU_RATE * preact * (1.0 + GELU_CUBE * square))
    half = 0.5 * (1.0 + bent)
    slope = half + (0.5 * GELU_RATE) * preact * (1.0 - bent * bent) * (
        1.0 + (3.0 * GELU_CUBE) * square
    )
    activated = (preact * half).astype(jnp.bfloat16)
    branch_ref[...] += jnp.dot(activated, down_ref[...], preferred_element_type=jnp.float32)
    d_preact = dot_last(upstream, down_ref[...]) * slope
    d_preact = d_preact.astype(jnp.bfloat16)
    bias_grad_ref[...] = jnp.sum(d_preact.astype(jnp.float32), 0, keepdims=True)
    down_grad_ref[...] = dot_first(activated, upstream).astype(jnp.bfloat16)
    d_hidden_ref[...] += dot_last(d_preact, up_ref[...])
    up_grad = jnp.dot(turned_ref[...], d_preact, preferred_element_type=jnp.float32)
    store_halves(up_grad, up_kept_ref, up_sent_ref)


def mlp(hidden, upstream, up, bias, down):
    length, width = hidden.shape
    units = up.shape[1]
    block = 512
    fixed = pl.BlockSpec((length, width), lambda at: (0, 0))
    columns = pl.BlockSpec((width, block), lambda at: (0, at))
    lanes = pl.BlockSpec((1, block), lambda at: (0, at))
    rows = pl.BlockSpec((block, width), lambda at: (at, 0))
    half = pl.BlockSpec((SHARDS // 2, width // SHARDS, block), lambda at: (0, 0, at))
    half_shape = jax.ShapeDtypeStruct((SHARDS // 2, width // SHARDS, units), jnp.bfloat16)
    return pl.pallas_call(
        mlp_kernel,
        grid=(units // block,),
        out_shape=(
            jax.ShapeDtypeStruct((length, width), jnp.float32),
            jax.ShapeDtypeStruct((length, width), jnp.float32),
            half_shape,
            half_shape,
            jax.ShapeDtypeStruct(down.shape, jnp.bfloat16),
            jax.ShapeDtypeStruct((1, units), jnp.float32),
        ),
        in_specs=[fixed, fixed, columns, lanes, rows],
        out_specs=(fixed, fixed, half, half, rows, lanes),
        scratch_shapes=[pltpu.VMEM((width, length), jnp.bfloat16)],
        compiler_params=pltpu.CompilerParams(vmem_limit_bytes=56 << 20),
        cost_estimate=SHORT,
    )(hidden, upstream, up, bias, down)


def per_device(
    latent_in,
    condition,
    valid_slots,
    ada_weight,
    ada_bias,
    qkv_weight,
    qv_bias,
    out_weight,
    out_bias,
    up_weight,
    up_bias,
    down_weight,
    down_bias,
    cotangent,
):
    number, length, width = latent_in.shape
    place = place_of()
    fsdp_index = lax.axis_index("fsdp")
    held = (place >> 2) * 2 + (place & 1)
    rows = width // SHARDS
    replicas = lax.axis_size("rep")

    small = jnp.concatenate(
        [
            condition[0],
            qv_bias,
            out_bias,
            up_bias,
            down_bias,
            jnp.broadcast_to(valid_slots.astype(jnp.bfloat16), (128,)),
        ]
    )
    small_all = gather_group(small)
    latent_low = swap_halves(latent_in)
    pieces, order = gather_pieces(jnp.concatenate([qkv_weight, out_weight], axis=1))
    full_up = lax.all_gather(up_weight, GROUP, axis=0, tiled=True)
    cotangent_low = swap_halves(cotangent)
    full_qkv, full_out = assemble(pieces, order, (3 * width, width))
    full_down = lax.all_gather(down_weight, GROUP, axis=0, tiled=True)

    bounds = [0, width]
    for bias in (qv_bias, out_bias, up_bias, down_bias):
        bounds.append(bounds[-1] + bias.shape[0])
    cond_group = small_all[::2, :width].astype(jnp.float32)
    full_qv_bias, full_out_bias, full_up_bias, full_down_bias = (
        small_all[:, low:high].reshape(-1).astype(jnp.float32)
        for low, high in zip(bounds[1:-1], bounds[2:])
    )
    valid_group = small_all[::2, bounds[-1]].astype(jnp.float32)
    slot_mask = lax.dynamic_slice_in_dim(valid_group, held, 1)[:, None, None]

    silu_group = jax.nn.silu(cond_group).astype(jnp.bfloat16)
    silu_mine = lax.dynamic_slice_in_dim(silu_group, place * rows, rows, 1)
    ada_bias_row = lax.dynamic_update_slice_in_dim(
        jnp.zeros((ada_weight.shape[1],), jnp.float32),
        ada_bias.astype(jnp.float32),
        place * ada_bias.shape[0],
        0,
    )
    modulation = matmul(silu_mine, ada_weight) + ada_bias_row
    for bit, count in ((4, 2), (1, 1)):
        upper = (place & bit) != 0
        sent = jnp.where(upper, modulation[:count], modulation[count:])
        kept = jnp.where(upper, modulation[count:], modulation[:count])
        modulation = kept + permute(sent, lambda at: at ^ bit)
    modulation = modulation + permute(modulation, core_rule)
    shift_one, scale_one, gate_one, shift_two, scale_two, gate_two = jnp.split(
        modulation, 6, axis=-1
    )

    latent = latent_low[0].astype(jnp.float32)
    normed_one, inverse_one = normalize(latent)
    hidden_one = (normed_one * (1.0 + scale_one) + shift_one).astype(jnp.bfloat16)
    bias_full = jnp.concatenate(
        [full_qv_bias[:width], jnp.zeros((width,), jnp.float32), full_qv_bias[width:]]
    )
    projected = (matmul(hidden_one, full_qkv) + bias_full).astype(jnp.bfloat16)
    query = projected[:, :width]
    pair_own = projected[:, width:]
    pair_other = permute(pair_own, core_rule)
    heads = range(width // HEAD)
    halves = heads[: len(heads) // 2], heads[len(heads) // 2 :]
    attended_low, log_totals = attend(query, pair_own, pair_other, heads)
    log_rows = log_totals[:, : len(heads)].T[:, None, :]
    branch_one = matmul(attended_low, full_out) + full_out_bias
    middle = latent + gate_one * branch_one

    normed_two, inverse_two = normalize(middle)
    hidden_two = (normed_two * (1.0 + scale_two) + shift_two).astype(jnp.bfloat16)
    mask_row = slot_mask[0]
    d_out = cotangent_low[0].astype(jnp.float32) * mask_row
    d_branch_two = (gate_two * d_out).astype(jnp.bfloat16)
    branch_two, d_hidden_two, up_kept, up_sent, down_grad, up_bias_grad = mlp(
        hidden_two, d_branch_two, full_up, full_up_bias[None], full_down
    )
    up_scatter = Scatter((up_kept, up_sent))
    down_shard = lax.psum_scatter(down_grad, GROUP, scatter_dimension=0, tiled=True)
    branch_two = branch_two + full_down_bias
    block_out = (mask_row * (middle + gate_two * branch_two)).astype(jnp.bfloat16)
    d_gate_two = jnp.sum(d_out * branch_two, axis=0)
    down_bias_grad = jnp.sum(d_branch_two.astype(jnp.float32), axis=0)
    up_bias_grad = up_bias_grad[0]
    d_shift_two = jnp.sum(d_hidden_two, axis=0)
    d_scale_two = jnp.sum(d_hidden_two * normed_two, axis=0)
    d_middle = d_out + norm_back(d_hidden_two * (1.0 + scale_two), normed_two, inverse_two)
    d_gate_one = jnp.sum(d_middle * branch_one, axis=0)
    d_branch_one = (gate_one * d_middle).astype(jnp.bfloat16)

    d_attended, out_halves = product_back(attended_low, d_branch_one, full_out)
    d_attended = d_attended.astype(jnp.bfloat16)
    out_scatter = Scatter(out_halves)
    out_bias_grad = jnp.sum(d_branch_one.astype(jnp.float32), axis=0)
    d_attended, up_scatter.received = tie(d_attended, up_scatter.received)
    up_scatter.second()
    left = attend_back(query, pair_own, pair_other, d_attended, log_rows, halves[0])
    d_query, d_attended, out_scatter.received = tie(left[0], d_attended, out_scatter.received)
    out_scatter.second()
    right = attend_back(query, pair_own, pair_other, d_attended, log_rows, halves[1])
    d_other = permute(join_heads(left[2], right[2], width), core_rule)
    d_right, up_scatter.received, out_scatter.received = tie(
        right[1], up_scatter.received, out_scatter.received
    )
    up_scatter.add_third()
    out_scatter.add_third()
    d_query = join_heads(d_query, right[0], width)
    d_own = join_heads(left[1], d_right, width)
    d_own = (d_own + d_other.astype(jnp.float32)).astype(jnp.bfloat16)
    d_projected = jnp.concatenate([d_query, d_own[0], d_own[1]], axis=-1)

    d_projected, down_shard, up_scatter.sent, out_scatter.sent = tie(
        d_projected, down_shard, up_scatter.sent, out_scatter.sent
    )
    up_scatter.send_third()
    out_scatter.send_third()
    down_total = lax.psum(down_shard, "rep")
    d_hidden_one, qkv_halves = product_back(hidden_one, d_projected, full_qkv)
    qkv_scatter = Scatter(qkv_halves)
    d_hidden_one, d_projected, qkv_scatter.received = tie(
        d_hidden_one, d_projected, qkv_scatter.received
    )
    qkv_scatter.second()
    column_sums = jnp.sum(d_projected.astype(jnp.float32), axis=0)
    d_shift_one = jnp.sum(d_hidden_one, axis=0)
    d_scale_one = jnp.sum(d_hidden_one * normed_one, axis=0)
    latent_grad = d_middle + norm_back(d_hidden_one * (1.0 + scale_one), normed_one, inverse_one)
    bias_grads = (
        jnp.concatenate([column_sums[:width], column_sums[2 * width :]]),
        out_bias_grad,
        up_bias_grad,
        down_bias_grad,
    )
    sums = [d_shift_one, d_scale_one, d_gate_one, d_shift_two, d_scale_two, d_gate_two]
    ada_width = 6 * width
    small_sums = jnp.concatenate(sums + list(bias_grads))
    qkv_scatter.received, out_scatter.received, up_scatter.received = tie(
        qkv_scatter.received, out_scatter.received, up_scatter.received
    )
    up_shard = up_scatter.result().astype(jnp.bfloat16)
    qkv_scatter.third()
    qkv_shard = qkv_scatter.result()
    qkv_shard, latent_grad, block_out, small_sums = tie(
        qkv_shard, latent_grad.astype(jnp.bfloat16), block_out, small_sums
    )
    late_sum = ReplicaSum(
        jnp.concatenate([out_scatter.result(), qkv_shard], axis=1), replicas
    )
    latent_grad = swap_halves(latent_grad[None])
    block_out = swap_halves(block_out[None])
    sums_all = gather_group(small_sums)
    down_total, up_shard, sums_all, latent_grad, block_out, *late_sum.received = tie(
        down_total, up_shard, sums_all, latent_grad, block_out, *late_sum.received
    )
    up_total = lax.psum(up_shard, "rep")
    late_sum.second()

    d_group = sums_all[:, :ada_width].reshape(2, 2, 2, ada_width).sum(1).reshape(4, ada_width)
    bias_mine = []
    start = ada_width
    for grad in bias_grads:
        total = jnp.sum(sums_all[:, start : start + grad.shape[0]], axis=0)
        piece = grad.shape[0] // SHARDS
        bias_mine.append(lax.dynamic_slice_in_dim(total, place * piece, piece))
        start += grad.shape[0]
    d_silu = lax.dot_general(
        d_group,
        ada_weight.astype(jnp.float32),
        (((1,), (1,)), ((), ())),
        precision=exact_mode,
    )
    cond_mine = lax.dynamic_slice_in_dim(cond_group, place * rows, rows, 1)
    cond_part = jax.vjp(jax.nn.silu, cond_mine)[1](d_silu)[0]
    cond_all = gather_group(cond_part)
    cond_grad = lax.dynamic_index_in_dim(cond_all, fsdp_index, 1, keepdims=False)
    cond_grad = cond_grad.reshape(1, width)

    packed = jnp.concatenate(
        [d_group.reshape(-1), silu_mine.astype(jnp.float32).reshape(-1)] + bias_mine
    )
    packed_all = gather_replicas(packed, replicas)
    packed_all, *late_sum.received = tie(packed_all, *late_sum.received)
    late_total = late_sum.result()
    out_total, qkv_total = late_total[:, :width], late_total[:, width:]

    d_all = packed_all[:, : 4 * ada_width].reshape(-1, ada_width)
    silu_all = packed_all[:, 4 * ada_width : 4 * ada_width + 4 * rows].reshape(-1, rows)
    ada_total = lax.dot_general(
        silu_all, d_all, (((0,), (0,)), ((), ())), precision=exact_mode
    )
    ada_bias_total = jnp.sum(
        lax.dynamic_slice_in_dim(d_all, place * ada_bias.shape[0], ada_bias.shape[0], 1), axis=0
    )
    bias_totals = jnp.sum(packed_all[:, 4 * ada_width + 4 * rows :], axis=0)
    cuts = [0]
    for piece in bias_mine:
        cuts.append(cuts[-1] + piece.shape[0])
    qv_total, out_bias_total, up_bias_total, down_bias_total = (
        bias_totals[low:high] for low, high in zip(cuts[:-1], cuts[1:])
    )
    return (
        block_out,
        latent_grad.astype(jnp.float32),
        cond_grad,
        ada_total,
        ada_bias_total,
        qkv_total.astype(jnp.float32),
        qv_total,
        out_total.astype(jnp.float32),
        out_bias_total,
        up_total.astype(jnp.float32),
        up_bias_total,
        down_total.astype(jnp.float32),
        down_bias_total,
    )


def solution(mesh):
    tokens = P(("rep", "fsdp"), "sp", None)
    rows = P(("rep", "fsdp"), None)
    matrix = P(GROUP, None)
    vector = P(GROUP)
    weights = (matrix, vector) * 5
    return jax.shard_map(
        per_device,
        mesh=mesh,
        in_specs=(tokens, rows, P(("rep", "fsdp"))) + weights + (tokens,),
        out_specs=(tokens, tokens, rows) + weights,
        check_vma=False,
    )
```
